32 devices in a mesh: batch: 16 (over z, y, core), seq: 2 (over x).
Axes of the slice: x: 2, y: 2, z: 4, core: 2. Of those that a mesh axis runs over, the one named last changes fastest.
Arguments:
- tokens: bfloat16 [16, 1664, 1152], P('batch', 'seq'), may hold values from -6 to 6
- skip_parts: bfloat16 [2, 16, 1664, 1152], P('seq', 'batch'), may hold values from -4 to 4
- lengths: int32 [16, 4], P('batch'), may hold values from 0 to 1026, as said below
- cotangent: bfloat16 [16, 1664, 1152], P('batch', 'seq'), may hold values from -6 to 6
- skip_w: bfloat16 [2304, 1152], P('batch'), may hold values from -0.125 to 0.125
- qkv_w: bfloat16 [1152, 3456], P('batch'), may hold values from -0.1875 to 0.1875
- proj_w: bfloat16 [1152, 1152], P('batch'), may hold values from -0.75 to 0.75
- fc1_w: bfloat16 [1152, 4608], P('batch'), may hold values from -0.1875 to 0.1875
- fc2_w: bfloat16 [4608, 1152], P('batch'), may hold values from -0.125 to 0.125
- skip_bias: float32 [1152], replicated, may hold values from -2 to 2
- ln1_gain: float32 [1152], replicated, may hold values from 0.25 to 1.75
- ln1_bias: float32 [1152], replicated, may hold values from -2 to 2
- proj_bias: float32 [1152], replicated, may hold values from -2 to 2
- ln2_gain: float32 [1152], replicated, may hold values from 0.25 to 1.75
- ln2_bias: float32 [1152], replicated, may hold values from -2 to 2
- fc1_bias: float32 [4608], replicated, may hold values from -2 to 2
- fc2_bias: float32 [1152], replicated, may hold values from -2 to 2
Outputs:
- output: bfloat16 [16, 1664, 1152], P('batch', 'seq')
- d_tokens: float32 [16, 1664, 1152], P('batch', 'seq')
- d_skip: float32 [16, 1664, 1152], P('batch', 'seq')
- d_skip_w: float32 [2304, 1152], P('batch')
- d_qkv_w: float32 [1152, 3456], P('batch')
- d_proj_w: float32 [1152, 1152], P('batch')
- d_fc1_w: float32 [1152, 4608], P('batch')
- d_fc2_w: float32 [4608, 1152], P('batch')
- d_skip_bias: float32 [1152], replicated
- d_ln1_gain: float32 [1152], replicated
- d_ln1_bias: float32 [1152], replicated
- d_proj_bias: float32 [1152], replicated
- d_ln2_gain: float32 [1152], replicated
- d_ln2_bias: float32 [1152], replicated
- d_fc1_bias: float32 [4608], replicated
- d_fc2_bias: float32 [1152], replicated
The draws below stay inside these ranges and needn't reach their ends.
Inputs may be any that keep to these rules, and one draw needn't show every extreme that they name: `lengths`: each row holds in order an item of 258 tokens, an item of 1026 tokens, another of 258 tokens, and an item of 122 tokens in exactly half of the rows (rounded down) or an empty one (0) in the others; the rest of the row is padding.
All inputs are finite; a program needn't handle non-finite values.
Results may differ from the reference program's by a relative error of at most 0.03.
Values may be sent and summed in bfloat16 or wider, within the bound.
No kernel may reach another device: no remote copies, remote signals or barrier semaphores. Data moves between devices by JAX's collectives and lax.ppermute only.
A program may use at most 320 MiB of HBM per device.

```python
import math
from functools import partial
import jax
import jax.numpy as jnp
from jax import lax

D = 1152
HEADS = 16
HD = 72
FF = 4608
SHORT = 258
TINY = 122
ITEMS = 4
ROW_LEN = 1664
ROWS = 16
N_SEQ = 2


def draw_lengths(key, part):
    key = jax.random.fold_in(key, 11)
    row_order = jax.random.permutation(key, ROWS)
    has_tiny = (row_order < ROWS // 2).astype(jnp.int32)
    longest = jnp.full((ROWS,), ROW_LEN - 2 * SHORT - TINY, jnp.int32)
    short_len = jnp.full((ROWS,), SHORT, jnp.int32)
    return jnp.stack([short_len, longest, short_len, TINY * has_tiny], axis=1).astype(jnp.int32)


def raised(values, key, source, target, blocks, factor):
    owner, partner = [(jnp.arange(values.shape[dim]) // (values.shape[dim] // blocks)).reshape([-1 if axis == dim else 1 for axis in range(values.ndim)]) for dim in (source, target)]
    chosen = jax.random.permutation(key, blocks)[partner]
    strong = (owner == chosen) | (owner == (partner + blocks // 2) % blocks)
    return jnp.where(strong, factor * values, values)


def block_levels(stream_key, dims, split, least, largest):
    def one(position, shards_of):
        steps = jax.random.uniform(jax.random.fold_in(jax.random.fold_in(stream_key, 6), position), (shards_of,), jnp.float32, least / len(split), largest / len(split))
        return jnp.repeat(jnp.exp(steps), dims[position] // shards_of).reshape((-1,) + (1,) * (len(dims) - position - 1))

    level = one(*split[0])
    for cut in split[1:]:
        level = level * one(*cut)
    return level


def normal_values(stream_key, extent, scale, bound, shards=(), held_as=jnp.bfloat16):
    entries = jax.random.normal(stream_key, extent, jnp.float32) * scale
    if len(shards) > 0:
        entries = block_levels(stream_key, extent, shards, -0.22, 0.18) * entries
    return jnp.clip(entries, min=-bound, max=bound).astype(held_as)


def noise_with(own_key, shape, width, most, shards, heavy, kind=jnp.bfloat16):
    array = width * jax.random.normal(own_key, shape, jnp.float32)
    if shards:
        array = array * block_levels(own_key, shape, shards, -0.22, 0.18)
    return jnp.clip(raised(array, jax.random.fold_in(own_key, 3), *heavy), -most, most).astype(kind)


def setup_inputs(seed: int = 0) -> dict:
    arg_keys = jax.random.split(jax.random.key(seed), 18)
    tokens = normal_values(arg_keys[0], (ROWS, ROW_LEN, D), 1.0, 6.0, ((0, 16), (1, 2)))
    skip_parts = noise_with(arg_keys[1], (N_SEQ, ROWS, ROW_LEN, D), 0.5, 4.0, ((0, 2), (1, 16)), (0, 2, 2, 2.0))
    lengths = draw_lengths(jax.random.fold_in(arg_keys[17], 71), 0)
    cotangent = normal_values(arg_keys[3], (ROWS, ROW_LEN, D), 1.0, 6.0, ((0, 16), (1, 2)))
    skip_w = normal_values(arg_keys[4], (2 * D, D), (2 * D) ** -0.5, 0.125, ((0, 16),))
    qkv_w = normal_values(arg_keys[5], (D, 3 * D), D ** -0.5, 0.1875, ((0, 16),))
    proj_w = normal_values(arg_keys[6], (D, D), (D // 16) ** -0.5, 0.75, ((0, 16),))
    fc1_w = normal_values(arg_keys[7], (D, FF), D ** -0.5, 0.1875, ((0, 16),))
    fc2_w = normal_values(arg_keys[8], (FF, D), (FF // 2) ** -0.5, 0.125, ((0, 16),))
    skip_bias = normal_values(arg_keys[9], (D,), 0.3, 2.0, (), jnp.float32)
    ln1_gain = jnp.clip(1.0 + 0.15 * jax.random.normal(arg_keys[10], (D,), jnp.float32), 0.25, 1.75)
    ln1_bias = normal_values(arg_keys[11], (D,), 0.3, 2.0, (), jnp.float32)
    proj_bias = normal_values(arg_keys[12], (D,), 0.3, 2.0, (), jnp.float32)
    ln2_gain = jnp.clip(1.0 + 0.15 * jax.random.normal(arg_keys[13], (D,), jnp.float32), 0.25, 1.75)
    ln2_bias = normal_values(arg_keys[14], (D,), 0.3, 2.0, (), jnp.float32)
    fc1_bias = normal_values(arg_keys[15], (FF,), 0.3, 2.0, (), jnp.float32)
    fc2_bias = normal_values(arg_keys[16], (D,), 0.3, 2.0, (), jnp.float32)
    return dict(tokens=tokens, skip_parts=skip_parts, lengths=lengths, cotangent=cotangent, skip_w=skip_w, qkv_w=qkv_w, proj_w=proj_w, fc1_w=fc1_w, fc2_w=fc2_w, skip_bias=skip_bias, ln1_gain=ln1_gain, ln1_bias=ln1_bias, proj_bias=proj_bias, ln2_gain=ln2_gain, ln2_bias=ln2_bias, fc1_bias=fc1_bias, fc2_bias=fc2_bias)


EPS = 1e-05
HIGH = lax.Precision.HIGHEST

@jax.custom_vjp
def low(v):
    return lax.optimization_barrier(v.astype(jnp.bfloat16)).astype(jnp.float32)

@jax.custom_vjp
def low_back(v):
    return v

def low_keep(v):
    return (low(v), None)

def low_pass(kept, grad):
    return (grad,)

def back_keep(v):
    return (v, None)

def back_low(kept, grad):
    return (low(grad),)
low.defvjp(low_keep, low_pass)
low_back.defvjp(back_keep, back_low)

def layer_norm(hidden, gain, shift):
    centred = hidden - lax.optimization_barrier(jnp.mean(hidden, axis=-1, keepdims=True))
    spread = lax.optimization_barrier(jnp.mean(centred * centred, axis=-1, keepdims=True))
    return centred * lax.rsqrt(spread + EPS) * gain + shift

def segment_ids(offsets, positions):
    hits = (positions[None, :, None] >= offsets[:, None, :]).astype(jnp.int32)
    return lax.optimization_barrier(jnp.sum(hits, axis=-1)).astype(jnp.int32)

def attend_row(queries, keys_row, values_row, seg_row):
    block_len = math.gcd(ROW_LEN, 512)

    def query_block(inputs):
        q_part, seg_part = inputs
        scores = low_back(jnp.einsum('thd,khd->thk', q_part, keys_row, precision=HIGH) * HD ** (-0.5))
        same_item = seg_part[:, None, None] == seg_row[None, None, :]
        weights = low(jax.nn.softmax(jnp.where(same_item, scores, -1e+30), axis=-1))
        return jnp.einsum('thk,khd->thd', weights, values_row, precision=HIGH)
    blocks = lax.map(jax.checkpoint(query_block), (queries.reshape(ROW_LEN // block_len, block_len, HEADS, HD), seg_row.reshape(ROW_LEN // block_len, block_len)))
    return blocks.reshape(ROW_LEN, D)

def forward(tok_rows, skip_sum, w_skip, w_qkv, w_proj, w_up, w_down, skip_bias, ln1_gain, ln1_bias, proj_bias, ln2_gain, ln2_bias, up_bias, down_bias, seg_ids, live_mask):

    def one_row(inputs):
        tok_row, skip_row, seg_row, live_row = inputs
        joined = jnp.concatenate([tok_row, low(skip_row)], axis=-1)
        h_zero = low_back(jnp.dot(joined, w_skip, precision=HIGH)) + skip_bias
        act_one = low(layer_norm(h_zero, ln1_gain, ln1_bias))
        qkv_all = low(low_back(jnp.dot(act_one, w_qkv, precision=HIGH)))
        queries = qkv_all[:, :D].reshape(ROW_LEN, HEADS, HD)
        keys_row = qkv_all[:, D:2 * D].reshape(ROW_LEN, HEADS, HD)
        values_row = qkv_all[:, 2 * D:].reshape(ROW_LEN, HEADS, HD)
        attended = low(low_back(attend_row(queries, keys_row, values_row, seg_row)))
        h_one = h_zero + low_back(jnp.dot(attended, w_proj, precision=HIGH)) + proj_bias
        act_two = low(layer_norm(h_one, ln2_gain, ln2_bias))
        up_proj = low_back(jnp.dot(act_two, w_up, precision=HIGH)) + up_bias
        gelu_out = low(jax.nn.gelu(up_proj, approximate=False))
        h_two = h_one + low_back(jnp.dot(gelu_out, w_down, precision=HIGH)) + down_bias
        return h_two * live_row[:, None]
    return lax.map(jax.checkpoint(one_row), (tok_rows, skip_sum, seg_ids, live_mask))

def reference(tokens, skip_parts, lengths, cotangent, skip_w, qkv_w, proj_w, fc1_w, fc2_w, skip_bias, ln1_gain, ln1_bias, proj_bias, ln2_gain, ln2_bias, fc1_bias, fc2_bias):
    offsets = jnp.cumsum(lengths, axis=1).astype(jnp.int32)
    seg_ids = segment_ids(offsets, jnp.arange(ROW_LEN, dtype=jnp.int32))
    live_mask = (seg_ids < ITEMS).astype(jnp.float32)
    skip_sum = lax.optimization_barrier(jnp.sum(skip_parts.astype(jnp.float32), axis=0))
    block_fn = partial(forward, seg_ids=seg_ids, live_mask=live_mask)
    result, pull_back = jax.vjp(block_fn, tokens.astype(jnp.float32), skip_sum, skip_w.astype(jnp.float32), qkv_w.astype(jnp.float32), proj_w.astype(jnp.float32), fc1_w.astype(jnp.float32), fc2_w.astype(jnp.float32), skip_bias.astype(jnp.float32), ln1_gain.astype(jnp.float32), ln1_bias.astype(jnp.float32), proj_bias.astype(jnp.float32), ln2_gain.astype(jnp.float32), ln2_bias.astype(jnp.float32), fc1_bias.astype(jnp.float32), fc2_bias.astype(jnp.float32))
    gradients = pull_back(cotangent.astype(jnp.float32))
    return (result.astype(jnp.bfloat16), gradients[0], gradients[1], gradients[2], gradients[3], gradients[4], gradients[5], gradients[6], gradients[7], gradients[8], gradients[9], gradients[10], gradients[11], gradients[12], gradients[13], gradients[14])
```

```python
import math

import jax
import jax.numpy as jnp
from jax import lax
from jax.experimental import pallas as pl
from jax.experimental.pallas import tpu as pltpu
from jax.sharding import PartitionSpec as P

HEADS = 16
HD = 72
D = 1152
EPS = 1e-05

SCALE=HD**-0.5
C2=SCALE*math.log2(math.e)
REM=576
TILES={
 0:[(256,576,258,832,[(0,256,576,258,832),(1,0,464,0,452)]),
    (0,272,0,258,[(0,0,272,0,258)])],
 1:[(0,464,0,452,[(0,0,464,0,452),(1,0,576,2,576)]),
    (448,272,452,710,[(0,448,272,452,710)]),
    (704,128,710,832,[(0,704,128,710,832)])],
}
NT=(((1,),(1,)),((),()))
TN=(((0,),(0,)),((),()))
def dot(a,b,dims=(((1,),(0,)),((),()))):
    return lax.dot_general(a,b,dims,preferred_element_type=jnp.float32)

def split(n,step):
    out=[];i=0
    while i<n:
        out.append((i,min(step,n-i))); i+=step
    return out

def fwd_kernel(s_ref, qkv_ref, kvr_ref, o_ref, l_ref, *, qstep):
    h=pl.program_id(0)
    @pl.when(h==0)
    def _():
        o_ref[...]=jnp.zeros_like(o_ref); l_ref[...]=jnp.zeros_like(l_ref)
    t=jnp.minimum((72*h)//128, 7)
    lo=72*h-128*t
    base=pl.multiple_of(t*128,128)
    def win(ref,off,r0,n):
        return ref[r0:r0+n, pl.ds(pl.multiple_of(base+off,128),256)]
    def tile(q0,nq,qv0,qv1,keys):
        lane=lax.broadcasted_iota(jnp.int32,(1,256),1)
        hm=(lane>=lo)&(lane<lo+72)
        for (a,n) in split(nq,qstep):
            r0=q0+a
            q=win(qkv_ref,0,r0,n)
            qm=jnp.where(hm,q,jnp.zeros_like(q))
            ss=[]
            for (src,k0,kc,kv0,kv1) in keys:
                k=win(qkv_ref,D,k0,kc) if src==0 else win(kvr_ref,0,k0,kc)
                s=dot(qm,k,NT)
                if kv0>k0 or kv1<k0+kc:
                    kp=k0+lax.broadcasted_iota(jnp.int32,(1,kc),1)
                    s=jnp.where((kp>=kv0)&(kp<kv1),s,-1e30)
                ss.append(s)
            m=jnp.max(ss[0],axis=1,keepdims=True)
            for s in ss[1:]: m=jnp.maximum(m,jnp.max(s,axis=1,keepdims=True))
            mc=m*C2
            l=None; o=None
            for s,(src,k0,kc,kv0,kv1) in zip(ss,keys):
                p=jnp.exp2(s*C2-mc)
                lp=jnp.sum(p,axis=1,keepdims=True)
                v=win(qkv_ref,2*D,k0,kc) if src==0 else win(kvr_ref,D,k0,kc)
                op=dot(p.astype(jnp.bfloat16),v)
                l=lp if l is None else l+lp
                o=op if o is None else o+op
            o=o*(1.0/l)
            lse=mc+jnp.log2(l)
            sl=(slice(r0,r0+n),pl.ds(base,256))
            old=o_ref[sl]; ob=o.astype(jnp.bfloat16)
            hl=lax.broadcasted_iota(jnp.int32,(1,128),1)==h
            oldl=l_ref[r0:r0+n,:]
            if r0<qv0 or r0+n>qv1:
                row=r0+lax.broadcasted_iota(jnp.int32,(n,1),0)
                rv=(row>=qv0)&(row<qv1)
                o_ref[sl]=jnp.where(hm&rv,ob,old)
                l_ref[r0:r0+n,:]=jnp.where(hl&rv,lse,oldl)
            else:
                o_ref[sl]=jnp.where(hm,ob,old)
                l_ref[r0:r0+n,:]=jnp.where(hl,lse,oldl)
    for sidx in (0,1):
        @pl.when(s_ref[0]==sidx)
        def _():
            for tl in TILES[sidx]: tile(*tl)

def full(shape,n=1):
    return pl.BlockSpec(shape,lambda h,s:(0,)*len(shape),pipeline_mode=pl.Buffered(1))
def attn_fwd(sidx,qkv,kvr,qstep=192):
    return pl.pallas_call(
        lambda *r: fwd_kernel(*r,qstep=qstep),
        out_shape=(jax.ShapeDtypeStruct((832,D),jnp.bfloat16),jax.ShapeDtypeStruct((832,128),jnp.float32)),
        grid_spec=pltpu.PrefetchScalarGridSpec(num_scalar_prefetch=1,grid=(HEADS,),
            in_specs=[full((832,3*D)),full((REM,2*D))],
            out_specs=(full((832,D)),full((832,128)))),
        compiler_params=pltpu.CompilerParams(vmem_limit_bytes=60*2**20),
        name="attn_fwd",
    )(sidx,qkv,kvr)

def bwd_kernel(s_ref,qkv_ref,kvr_ref,do_ref,lt_ref,dt_ref,dqkv_ref,dkvr_ref,*,kstep,expl):
    h=pl.program_id(0)
    @pl.when(h==0)
    def _():
        dqkv_ref[...]=jnp.zeros_like(dqkv_ref); dkvr_ref[...]=jnp.zeros_like(dkvr_ref)
    t=jnp.minimum((72*h)//128, 7)
    lo=72*h-128*t
    base=pl.multiple_of(t*128,128)
    def ws(off,r0,n):
        return (slice(r0,r0+n), pl.ds(pl.multiple_of(base+off,128),256))
    def tile(q0,nq,qv0,qv1,keys):
        lane=lax.broadcasted_iota(jnp.int32,(1,256),1)
        hm=(lane>=lo)&(lane<lo+72)
        q=qkv_ref[ws(0,q0,nq)]; qm=jnp.where(hm,q,jnp.zeros_like(q))
        do=do_ref[ws(0,q0,nq)]; dom=jnp.where(hm,do,jnp.zeros_like(do))
        lrow=lt_ref[pl.ds(h,1),:][:,q0:q0+nq]; drow=dt_ref[pl.ds(h,1),:][:,q0:q0+nq]
        if qv0>q0 or qv1<q0+nq:
            qp=q0+lax.broadcasted_iota(jnp.int32,(1,nq),1)
            lrow=jnp.where((qp>=qv0)&(qp<qv1),lrow,1e30)
        dqt=None
        for (src,k00,kcc,kv0,kv1) in keys:
            for (a,kc) in split(kcc,kstep):
                k0=k00+a
                k=qkv_ref[ws(D,k0,kc)] if src==0 else kvr_ref[ws(0,k0,kc)]
                v=qkv_ref[ws(2*D,k0,kc)] if src==0 else kvr_ref[ws(D,k0,kc)]
                st=dot(k,qm,NT)
                p=jnp.exp2(st*C2-lrow)
                if kv0>k0 or kv1<k0+kc:
                    kp=k0+lax.broadcasted_iota(jnp.int32,(kc,1),0)
                    p=jnp.where((kp>=kv0)&(kp<kv1),p,0.0)
                dp=dot(v,dom,NT)
                ds=(p*(dp-drow)).astype(jnp.bfloat16)
                dv=dot(p.astype(jnp.bfloat16),dom)
                dk=dot(ds,qm)*SCALE
                if src==0:
                    dqkv_ref[ws(D,k0,kc)]+=dk.astype(jnp.bfloat16)
                    dqkv_ref[ws(2*D,k0,kc)]+=dv.astype(jnp.bfloat16)
                else:
                    dkvr_ref[ws(0,k0,kc)]+=dk.astype(jnp.bfloat16)
                    dkvr_ref[ws(D,k0,kc)]+=dv.astype(jnp.bfloat16)
                if expl: d=dot(k.T,ds)
                else: d=dot(k,ds,TN)
                dqt=d if dqt is None else dqt+d
        dq=(dqt*SCALE).T
        sl=ws(0,q0,nq)
        dqkv_ref[sl]=dqkv_ref[sl]+jnp.where(hm,dq,0.0).astype(jnp.bfloat16)
    for sidx in (0,1):
        @pl.when(s_ref[0]==sidx)
        def _():
            for tl in TILES[sidx]: tile(*tl)

def attn_bwd(sidx,qkv,kvr,do,lt,dt,kstep=1024,expl=True):
    return pl.pallas_call(
        lambda *r: bwd_kernel(*r,kstep=kstep,expl=expl),
        out_shape=(jax.ShapeDtypeStruct((832,3*D),jnp.bfloat16),jax.ShapeDtypeStruct((REM,2*D),jnp.bfloat16)),
        grid_spec=pltpu.PrefetchScalarGridSpec(num_scalar_prefetch=1,grid=(HEADS,),
            in_specs=[full((832,3*D)),full((REM,2*D)),full((832,D)),full((16,832)),full((16,832))],
            out_specs=(full((832,3*D)),full((REM,2*D)))),
        compiler_params=pltpu.CompilerParams(vmem_limit_bytes=60*2**20),
        name="attn_bwd",
    )(sidx,qkv,kvr,do,lt,dt)


def layer_norm(hidden, gain, shift):
    centred = hidden - jnp.mean(hidden, axis=-1, keepdims=True)
    spread = jnp.mean(centred * centred, axis=-1, keepdims=True)
    return centred * lax.rsqrt(spread + EPS) * gain + shift


def exact_gelu(value):
    return jax.nn.gelu(value, approximate=False)


def segment_ids(offsets, positions):
    hits = (positions[None, :, None] >= offsets[:, None, :]).astype(jnp.int32)
    return jnp.sum(hits, axis=-1)


def fwd_dot(left, right):
    return jnp.dot(left, right, preferred_element_type=jnp.float32)


def contract_rows(left, right):
    return lax.dot_general(
        left, right, (((0,), (0,)), ((), ())), preferred_element_type=jnp.float32
    )


def back_dot(grad_rows, weight):
    return lax.dot_general(
        grad_rows, weight, (((1,), (1,)), ((), ())), preferred_element_type=jnp.float32
    )


class PairAttention:
    def __init__(self, qkv_all):
        self.side = lax.axis_index("seq")
        self.index = self.side.astype(jnp.int32).reshape(1)
        self.qkv = qkv_all
        self.away = jnp.where(self.side == 0, 256, 0)
        sent = lax.dynamic_slice(qkv_all, (self.away, D), (REM, 2 * D))
        self.kv_far = lax.ppermute(sent, "seq", [(0, 1), (1, 0)])

    def forward(self):
        self.out, self.lse = attn_fwd(self.index, self.qkv, self.kv_far, 288)
        return self.out

    def backward(self, d_att):
        pick = (
            lax.broadcasted_iota(jnp.int32, (D, HEADS), 0) // HD
            == lax.broadcasted_iota(jnp.int32, (D, HEADS), 1)
        ).astype(jnp.float32)
        prod = d_att.astype(jnp.float32) * self.out.astype(jnp.float32)
        row_dot = lax.dot_general(
            pick, prod, (((0,), (1,)), ((), ())), precision=lax.Precision.HIGHEST
        )
        lse = self.lse[:, :HEADS].T
        d_qkv, d_far = attn_bwd(self.index, self.qkv, self.kv_far, d_att, lse, row_dot)
        back = lax.ppermute(d_far, "seq", [(0, 1), (1, 0)])
        own = lax.dynamic_slice(d_qkv, (self.away, D), (REM, 2 * D))
        total = (own.astype(jnp.float32) + back.astype(jnp.float32)).astype(jnp.bfloat16)
        return lax.dynamic_update_slice(d_qkv, total, (self.away, D))


class RowAttention:
    def __init__(self, qkv_all, offsets, row_count, local_len):
        self.row_count, self.local_len = row_count, local_len
        self.row_len = local_len * lax.axis_size("seq")
        self.offsets = offsets
        first_pos = lax.axis_index("seq") * local_len
        self.query_seg = segment_ids(offsets, first_pos + jnp.arange(local_len, dtype=jnp.int32))
        self.scale = HD ** (-0.5)
        self.queries = qkv_all[:, :D].reshape(row_count, local_len, HEADS, HD)
        keyvals = qkv_all[:, D:].reshape(row_count, local_len, 2 * D)
        self.kv = lax.all_gather(keyvals, "seq", axis=1, tiled=True)

    def block(self, first, size):
        kv = lax.dynamic_slice_in_dim(self.kv, first, size, 1)
        shape = (self.row_count, size, HEADS, HD)
        key_seg = segment_ids(self.offsets, first + jnp.arange(size, dtype=jnp.int32))
        same = self.query_seg[:, :, None, None] == key_seg[:, None, None, :]
        return kv[:, :, :D].reshape(shape), kv[:, :, D:].reshape(shape), same

    def scores(self, keys):
        return (
            jnp.einsum("rthd,rkhd->rthk", self.queries, keys, preferred_element_type=jnp.float32)
            * self.scale
        )

    def forward(self):
        keys, values, same = self.block(0, self.row_len)
        scores = jnp.where(same, self.scores(keys), -1e30)
        top = jnp.max(scores, axis=-1)
        expo = jnp.where(same, jnp.exp(scores - top[..., None]), 0.0)
        norm = jnp.sum(expo, axis=-1)
        weighted = jnp.einsum(
            "rthk,rkhd->rthd",
            expo.astype(jnp.bfloat16),
            values,
            preferred_element_type=jnp.float32,
        )
        self.attended = weighted / norm[..., None]
        self.log_total = top + jnp.log(norm)
        return self.attended.reshape(-1, D).astype(jnp.bfloat16)

    def backward(self, d_att):
        rows, length = self.row_count, self.local_len
        d_att = d_att.reshape(rows, length, HEADS, HD)
        row_dot = jnp.sum(d_att.astype(jnp.float32) * self.attended, axis=-1)
        size = math.gcd(self.row_len, 512)

        def step(index, totals):
            d_query, d_kv = totals
            keys, values, same = self.block(index * size, size)
            weights = jnp.where(same, jnp.exp(self.scores(keys) - self.log_total[..., None]), 0.0)
            d_weights = jnp.einsum(
                "rthd,rkhd->rthk", d_att, values, preferred_element_type=jnp.float32
            )
            d_scores = (weights * (d_weights - row_dot[..., None])).astype(jnp.bfloat16)
            d_query = d_query + self.scale * jnp.einsum(
                "rthk,rkhd->rthd", d_scores, keys, preferred_element_type=jnp.float32
            )
            d_key = self.scale * jnp.einsum(
                "rthk,rthd->rkhd", d_scores, self.queries, preferred_element_type=jnp.float32
            )
            d_value = jnp.einsum(
                "rthk,rthd->rkhd",
                weights.astype(jnp.bfloat16),
                d_att,
                preferred_element_type=jnp.float32,
            )
            both = jnp.concatenate(
                [d_key.reshape(rows, size, D), d_value.reshape(rows, size, D)], axis=2
            )
            return d_query, lax.dynamic_update_slice_in_dim(d_kv, both, index * size, 1)

        start = (
            jnp.zeros((rows, length, HEADS, HD), jnp.float32),
            jnp.zeros((rows, self.row_len, 2 * D), jnp.float32),
        )
        d_query, d_kv = lax.fori_loop(0, self.row_len // size, step, start)
        d_kv = lax.psum_scatter(
            d_kv.astype(jnp.bfloat16), "seq", scatter_dimension=1, tiled=True
        ).astype(jnp.float32)
        return jnp.concatenate(
            [d_query.reshape(rows * length, D), d_kv.reshape(rows * length, 2 * D)], axis=1
        ).astype(jnp.bfloat16)


def per_device(
    tokens,
    skip_parts,
    lengths,
    cotangent,
    skip_w,
    qkv_w,
    proj_w,
    fc1_w,
    fc2_w,
    skip_bias,
    ln1_gain,
    ln1_bias,
    proj_bias,
    ln2_gain,
    ln2_bias,
    fc1_bias,
    fc2_bias,
):
    row_count, local_len, features = tokens.shape
    tok_count = row_count * local_len
    offsets = jnp.cumsum(lengths, axis=1)
    first_pos = lax.axis_index("seq") * local_len
    query_seg = segment_ids(offsets, first_pos + jnp.arange(local_len, dtype=jnp.int32))
    live_mask = (query_seg < lengths.shape[1]).astype(jnp.float32).reshape(tok_count, 1)
    skip_rows = lax.psum_scatter(skip_parts[0], "seq", scatter_dimension=1, tiled=True)
    w_skip, w_qkv, w_proj, w_up, w_down = (
        lax.all_gather(w, "batch", axis=0, tiled=True)
        for w in (skip_w, qkv_w, proj_w, fc1_w, fc2_w)
    )
    tok_flat = tokens.reshape(tok_count, features)
    skip_flat = skip_rows.reshape(tok_count, features)
    h_zero = (
        fwd_dot(tok_flat, w_skip[:features]) + fwd_dot(skip_flat, w_skip[features:]) + skip_bias
    )
    normed_one, ln1_back = jax.vjp(layer_norm, h_zero, ln1_gain, ln1_bias)
    act_one = normed_one.astype(jnp.bfloat16)
    qkv_all = fwd_dot(act_one, w_qkv).astype(jnp.bfloat16)
    if lax.axis_size("seq") == 2 and row_count == 1 and local_len == 832:
        attention = PairAttention(qkv_all)
    else:
        attention = RowAttention(qkv_all, offsets, row_count, local_len)
    att_low = attention.forward()
    h_one = h_zero + fwd_dot(att_low, w_proj) + proj_bias
    normed_two, ln2_back = jax.vjp(layer_norm, h_one, ln2_gain, ln2_bias)
    act_two = normed_two.astype(jnp.bfloat16)
    up_proj = fwd_dot(act_two, w_up) + fc1_bias
    gelu_out, gelu_back = jax.vjp(exact_gelu, up_proj)
    gelu_low = gelu_out.astype(jnp.bfloat16)
    h_two = h_one + fwd_dot(gelu_low, w_down) + fc2_bias
    output = (h_two * live_mask).astype(jnp.bfloat16).reshape(row_count, local_len, features)
    grad_two = cotangent.reshape(tok_count, features).astype(jnp.float32) * live_mask
    grad_low = grad_two.astype(jnp.bfloat16)
    d_w_down = contract_rows(gelu_low, grad_low)
    d_gelu = back_dot(grad_low, w_down)
    d_up = gelu_back(d_gelu)[0]
    up_low = d_up.astype(jnp.bfloat16)
    d_w_up = contract_rows(act_two, up_low)
    d_act_two = back_dot(up_low, w_up)
    d_h_one, d_ln2_gain, d_ln2_bias = ln2_back(d_act_two)
    d_h_one = d_h_one + grad_two
    proj_low = d_h_one.astype(jnp.bfloat16)
    d_w_proj = contract_rows(att_low, proj_low)
    d_att = back_dot(proj_low, w_proj).astype(jnp.bfloat16)
    d_qkv = attention.backward(d_att)
    d_w_qkv = contract_rows(act_one, d_qkv)
    d_act_one = back_dot(d_qkv, w_qkv)
    d_h_zero, d_ln1_gain, d_ln1_bias = ln1_back(d_act_one)
    d_h_zero = d_h_zero + d_h_one
    zero_low = d_h_zero.astype(jnp.bfloat16)
    d_w_skip = jnp.concatenate(
        [contract_rows(tok_flat, zero_low), contract_rows(skip_flat, zero_low)], axis=0
    )
    d_tokens = back_dot(zero_low, w_skip[:features]).reshape(row_count, local_len, features)
    d_skip = back_dot(zero_low, w_skip[features:]).reshape(row_count, local_len, features)
    vector_sums = lax.psum(
        (
            jnp.sum(d_h_zero, axis=0),
            d_ln1_gain,
            d_ln1_bias,
            jnp.sum(d_h_one, axis=0),
            d_ln2_gain,
            d_ln2_bias,
            jnp.sum(d_up, axis=0),
            jnp.sum(grad_two, axis=0),
        ),
        ("batch", "seq"),
    )
    weight_grads = tuple(
        lax.psum(
            lax.psum_scatter(
                grad.astype(jnp.bfloat16), "batch", scatter_dimension=0, tiled=True
            ),
            "seq",
        ).astype(jnp.float32)
        for grad in (d_w_skip, d_w_qkv, d_w_proj, d_w_up, d_w_down)
    )
    return (output, d_tokens, d_skip, *weight_grads, *vector_sums)


def solution(mesh):
    in_specs = (
        P("batch", "seq", None),
        P("seq", "batch", None, None),
        P("batch", None),
        P("batch", "seq", None),
        *(P("batch", None),) * 5,
        *(P(),) * 8,
    )
    out_specs = (*(P("batch", "seq", None),) * 3, *(P("batch", None),) * 5, *(P(),) * 8)
    return jax.shard_map(
        per_device, mesh=mesh, in_specs=in_specs, out_specs=out_specs, check_vma=False
    )
```

```python
import math

import jax
import jax.numpy as jnp
from jax import lax
from jax.experimental import pallas as pl
from jax.experimental.pallas import tpu as pltpu
from jax.sharding import PartitionSpec as P

HEADS = 16
HD = 72
D = 1152
ROWS = 16
EPS = 1e-05

SCALE=HD**-0.5
C2=SCALE*math.log2(math.e)
REM=576
TILES={
 0:[(256,576,258,832,[(0,256,576,258,832),(1,0,464,0,452)]),
    (0,272,0,258,[(0,0,272,0,258)])],
 1:[(0,464,0,452,[(0,0,464,0,452),(1,0,576,2,576)]),
    (448,272,452,710,[(0,448,272,452,710)]),
    (704,128,710,832,[(0,704,128,710,832)])],
}
NT=(((1,),(1,)),((),()))
TN=(((0,),(0,)),((),()))
def dot(a,b,dims=(((1,),(0,)),((),()))):
    return lax.dot_general(a,b,dims,preferred_element_type=jnp.float32)

def split(n,step):
    out=[];i=0
    while i<n:
        out.append((i,min(step,n-i))); i+=step
    return out

def fwd_kernel(s_ref, qkv_ref, kvr_ref, o_ref, l_ref, *, qstep):
    h=pl.program_id(0)
    @pl.when(h==0)
    def _():
        o_ref[...]=jnp.zeros_like(o_ref); l_ref[...]=jnp.zeros_like(l_ref)
    t=jnp.minimum((72*h)//128, 7)
    lo=72*h-128*t
    base=pl.multiple_of(t*128,128)
    def win(ref,off,r0,n):
        return ref[r0:r0+n, pl.ds(pl.multiple_of(base+off,128),256)]
    def tile(q0,nq,qv0,qv1,keys):
        lane=lax.broadcasted_iota(jnp.int32,(1,256),1)
        hm=(lane>=lo)&(lane<lo+72)
        for (a,n) in split(nq,qstep):
            r0=q0+a
            q=win(qkv_ref,0,r0,n)
            qm=jnp.where(hm,q,jnp.zeros_like(q))
            ss=[]
            for (src,k0,kc,kv0,kv1) in keys:
                k=win(qkv_ref,D,k0,kc) if src==0 else win(kvr_ref,0,k0,kc)
                s=dot(qm,k,NT)
                if kv0>k0 or kv1<k0+kc:
                    kp=k0+lax.broadcasted_iota(jnp.int32,(1,kc),1)
                    s=jnp.where((kp>=kv0)&(kp<kv1),s,-1e30)
                ss.append(s)
            m=jnp.max(ss[0],axis=1,keepdims=True)
            for s in ss[1:]: m=jnp.maximum(m,jnp.max(s,axis=1,keepdims=True))
            mc=m*C2
            l=None; o=None
            for s,(src,k0,kc,kv0,kv1) in zip(ss,keys):
                p=jnp.exp2(s*C2-mc)
                lp=jnp.sum(p,axis=1,keepdims=True)
                v=win(qkv_ref,2*D,k0,kc) if src==0 else win(kvr_ref,D,k0,kc)
                op=dot(p.astype(jnp.bfloat16),v)
                l=lp if l is None else l+lp
                o=op if o is None else o+op
            o=o*(1.0/l)
            lse=mc+jnp.log2(l)
            sl=(slice(r0,r0+n),pl.ds(base,256))
            old=o_ref[sl]; ob=o.astype(jnp.bfloat16)
            hl=lax.broadcasted_iota(jnp.int32,(1,128),1)==h
            oldl=l_ref[r0:r0+n,:]
            if r0<qv0 or r0+n>qv1:
                row=r0+lax.broadcasted_iota(jnp.int32,(n,1),0)
                rv=(row>=qv0)&(row<qv1)
                o_ref[sl]=jnp.where(hm&rv,ob,old)
                l_ref[r0:r0+n,:]=jnp.where(hl&rv,lse,oldl)
            else:
                o_ref[sl]=jnp.where(hm,ob,old)
                l_ref[r0:r0+n,:]=jnp.where(hl,lse,oldl)
    for sidx in (0,1):
        @pl.when(s_ref[0]==sidx)
        def _():
            for tl in TILES[sidx]: tile(*tl)

def full(shape,n=1):
    return pl.BlockSpec(shape,lambda h,s:(0,)*len(shape),pipeline_mode=pl.Buffered(1))
def attn_fwd(sidx,qkv,kvr,qstep=192):
    return pl.pallas_call(
        lambda *r: fwd_kernel(*r,qstep=qstep),
        out_shape=(jax.ShapeDtypeStruct((832,D),jnp.bfloat16),jax.ShapeDtypeStruct((832,128),jnp.float32)),
        grid_spec=pltpu.PrefetchScalarGridSpec(num_scalar_prefetch=1,grid=(HEADS,),
            in_specs=[full((832,3*D)),full((REM,2*D))],
            out_specs=(full((832,D)),full((832,128)))),
        compiler_params=pltpu.CompilerParams(vmem_limit_bytes=60*2**20),
        name="attn_fwd",
    )(sidx,qkv,kvr)

def bwd_kernel(s_ref,qkv_ref,kvr_ref,do_ref,lt_ref,dt_ref,dqkv_ref,dkvr_ref,*,kstep,expl):
    h=pl.program_id(0)
    @pl.when(h==0)
    def _():
        dqkv_ref[...]=jnp.zeros_like(dqkv_ref); dkvr_ref[...]=jnp.zeros_like(dkvr_ref)
    t=jnp.minimum((72*h)//128, 7)
    lo=72*h-128*t
    base=pl.multiple_of(t*128,128)
    def ws(off,r0,n):
        return (slice(r0,r0+n), pl.ds(pl.multiple_of(base+off,128),256))
    def tile(q0,nq,qv0,qv1,keys):
        lane=lax.broadcasted_iota(jnp.int32,(1,256),1)
        hm=(lane>=lo)&(lane<lo+72)
        q=qkv_ref[ws(0,q0,nq)]; qm=jnp.where(hm,q,jnp.zeros_like(q))
        do=do_ref[ws(0,q0,nq)]; dom=jnp.where(hm,do,jnp.zeros_like(do))
        lrow=lt_ref[pl.ds(h,1),:][:,q0:q0+nq]; drow=dt_ref[pl.ds(h,1),:][:,q0:q0+nq]
        if qv0>q0 or qv1<q0+nq:
            qp=q0+lax.broadcasted_iota(jnp.int32,(1,nq),1)
            lrow=jnp.where((qp>=qv0)&(qp<qv1),lrow,1e30)
        dqt=None
        for (src,k00,kcc,kv0,kv1) in keys:
            for (a,kc) in split(kcc,kstep):
                k0=k00+a
                k=qkv_ref[ws(D,k0,kc)] if src==0 else kvr_ref[ws(0,k0,kc)]
                v=qkv_ref[ws(2*D,k0,kc)] if src==0 else kvr_ref[ws(D,k0,kc)]
                st=dot(k,qm,NT)
                p=jnp.exp2(st*C2-lrow)
                if kv0>k0 or kv1<k0+kc:
                    kp=k0+lax.broadcasted_iota(jnp.int32,(kc,1),0)
                    p=jnp.where((kp>=kv0)&(kp<kv1),p,0.0)
                dp=dot(v,dom,NT)
                ds=(p*(dp-drow)).astype(jnp.bfloat16)
                dv=dot(p.astype(jnp.bfloat16),dom)
                dk=dot(ds,qm)*SCALE
                if src==0:
                    dqkv_ref[ws(D,k0,kc)]+=dk.astype(jnp.bfloat16)
                    dqkv_ref[ws(2*D,k0,kc)]+=dv.astype(jnp.bfloat16)
                else:
                    dkvr_ref[ws(0,k0,kc)]+=dk.astype(jnp.bfloat16)
                    dkvr_ref[ws(D,k0,kc)]+=dv.astype(jnp.bfloat16)
                if expl: d=dot(k.T,ds)
                else: d=dot(k,ds,TN)
                dqt=d if dqt is None else dqt+d
        dq=(dqt*SCALE).T
        sl=ws(0,q0,nq)
        dqkv_ref[sl]=dqkv_ref[sl]+jnp.where(hm,dq,0.0).astype(jnp.bfloat16)
    for sidx in (0,1):
        @pl.when(s_ref[0]==sidx)
        def _():
            for tl in TILES[sidx]: tile(*tl)

def attn_bwd(sidx,qkv,kvr,do,lt,dt,kstep=1024,expl=True):
    return pl.pallas_call(
        lambda *r: bwd_kernel(*r,kstep=kstep,expl=expl),
        out_shape=(jax.ShapeDtypeStruct((832,3*D),jnp.bfloat16),jax.ShapeDtypeStruct((REM,2*D),jnp.bfloat16)),
        grid_spec=pltpu.PrefetchScalarGridSpec(num_scalar_prefetch=1,grid=(HEADS,),
            in_specs=[full((832,3*D)),full((REM,2*D)),full((832,D)),full((16,832)),full((16,832))],
            out_specs=(full((832,3*D)),full((REM,2*D)))),
        compiler_params=pltpu.CompilerParams(vmem_limit_bytes=60*2**20),
        name="attn_bwd",
    )(sidx,qkv,kvr,do,lt,dt)


ERF_A = (
    -2.72614225801306e-10, 2.77068142495902e-08, -2.10102402082508e-06, -5.69250639462346e-05,
    -7.34990630326855e-04, -2.95459980854025e-03, -1.60960333262415e-02,
)
ERF_B = (
    -1.45660718464996e-05, -2.13374055278905e-04, -1.68282697438203e-03, -7.37332916720468e-03,
    -1.42647390514189e-02,
)


def erf(v):
    v = jnp.clip(v, -4.0, 4.0)
    square = v * v
    top, bottom = ERF_A[0], ERF_B[0]
    for term in ERF_A[1:]:
        top = top * square + term
    for term in ERF_B[1:]:
        bottom = bottom * square + term
    return v * top / bottom


def mlp_up(act, weight, bias, tile=768):
    rows, width = act.shape[0], weight.shape[1]

    def kernel(a_ref, w_ref, b_ref, g_ref, d_ref):
        u = dot(a_ref[...], w_ref[...]) + b_ref[...]
        phi = 0.5 + 0.5 * erf(u * math.sqrt(0.5))
        g_ref[...] = (u * phi).astype(jnp.bfloat16)
        density = jnp.exp(u * u * -0.5) * (1.0 / math.sqrt(2.0 * math.pi))
        d_ref[...] = (phi + u * density).astype(jnp.bfloat16)

    out = jax.ShapeDtypeStruct((rows, width), jnp.bfloat16)
    return pl.pallas_call(
        kernel,
        grid=(width // tile,),
        out_shape=(out, out),
        in_specs=[
            pl.BlockSpec((rows, D), lambda t: (0, 0), pipeline_mode=pl.Buffered(1)),
            pl.BlockSpec((D, tile), lambda t: (0, t)),
            pl.BlockSpec((1, tile), lambda t: (0, t)),
        ],
        out_specs=(pl.BlockSpec((rows, tile), lambda t: (0, t)),) * 2,
        compiler_params=pltpu.CompilerParams(vmem_limit_bytes=60 * 2**20),
        cost_estimate=pl.CostEstimate(
            flops=2 * rows * D * width, bytes_accessed=2 * D * width, transcendentals=rows * width
        ),
        name="mlp_up",
    )(act, weight, bias.reshape(1, width))


def ordered_transpose(at, value, held):
    held[...] = value.astype(jnp.float32).T.reshape(held.shape)
    blocks = []
    for crel in (0, 1):
        for yrel in (0, 1):
            for zrel in range(4):
                zz = lax.rem(at[0] + zrel, 4)
                yy = at[1] + yrel - 2 * at[1] * yrel
                cc = at[2] + crel - 2 * at[2] * crel
                blocks.append(held[zz * 4 + yy * 2 + cc])
    return jnp.concatenate(blocks, 0).astype(jnp.bfloat16)


def mlp_back(at, act, grad, gelu, slope, w_up, w_down):
    rows = act.shape[0]
    half = rows // 2

    def kernel(at, a_ref, e_ref, g_ref, s_ref, wu_ref, wd_ref, *refs):
        dn_mine, dn_other, up_mine, up_other, h_ref, c_ref, b_ref, a_t, g_t, du_ref, held = refs
        t = pl.program_id(0)
        y, c, x = at[1], at[2], at[3]

        @pl.when(t == 0)
        def _():
            a_t[...] = ordered_transpose(at, a_ref[...], held)
            h_ref[...] = jnp.zeros_like(h_ref)
            c_ref[...] = jnp.zeros_like(c_ref)

        bias = None
        for i in (0, 1):
            part = slice(i * half, (i + 1) * half)
            du = dot(e_ref[part], wd_ref[...], NT) * s_ref[part].astype(jnp.float32)
            total = jnp.sum(du, axis=0, keepdims=True)
            bias = total if bias is None else bias + total
            du = du.astype(jnp.bfloat16)
            du_ref[part] = du
            h_ref[part] += dot(g_ref[part], wd_ref[...])
            c_ref[part] += dot(du, wu_ref[...], NT)
        b_ref[...] = bias
        g_t[...] = g_ref[...].T
        for yy in (0, 1):
            both = dot(g_t[yy * 576 : yy * 576 + 576], e_ref[...])
            low, high = both[:288], both[288:]
            yrel = yy + y - 2 * yy * y
            for ref, value in (
                (dn_mine, jnp.where(c == 0, low, high)),
                (dn_other, jnp.where(c == 0, high, low)),
            ):
                value = value.astype(jnp.bfloat16)
                ref[x, 0, yrel] = value[:144]
                ref[1 - x, 0, yrel] = value[144:]
        for i, ref in ((0, up_mine), (1, up_other)):
            both = dot(a_t[i * 576 : i * 576 + 576], du_ref[...])
            for j in range(8):
                ref[j // 4, j % 4] = both[j * 72 : j * 72 + 72].astype(jnp.bfloat16)

    def part(t, at):
        return lax.rem(at[0] + t, 4)

    once = pl.Buffered(1)
    down = jax.ShapeDtypeStruct((2, 4, 2, 144, D), jnp.bfloat16)
    up = jax.ShapeDtypeStruct((2, 4, 72, 4 * D), jnp.bfloat16)
    whole = jax.ShapeDtypeStruct((rows, D), jnp.float32)
    down_spec = pl.BlockSpec((2, 1, 2, 144, D), lambda t, at: (0, t, 0, 0, 0))
    up_spec = pl.BlockSpec((2, 4, 72, D), lambda t, at: (0, 0, 0, part(t, at)))
    whole_spec = pl.BlockSpec((rows, D), lambda t, at: (0, 0), pipeline_mode=once)
    by_column = pl.BlockSpec((rows, D), lambda t, at: (0, part(t, at)))
    return pl.pallas_call(
        kernel,
        out_shape=(down, down, up, up, whole, whole, jax.ShapeDtypeStruct((1, 4 * D), jnp.float32)),
        grid_spec=pltpu.PrefetchScalarGridSpec(
            num_scalar_prefetch=1,
            grid=(4,),
            in_specs=[
                whole_spec,
                whole_spec,
                by_column,
                by_column,
                pl.BlockSpec((D, D), lambda t, at: (0, part(t, at))),
                pl.BlockSpec((D, D), lambda t, at: (part(t, at), 0)),
            ],
            out_specs=(
                down_spec,
                down_spec,
                up_spec,
                up_spec,
                whole_spec,
                whole_spec,
                pl.BlockSpec((1, D), lambda t, at: (0, part(t, at))),
            ),
            scratch_shapes=[
                pltpu.VMEM((D, rows), jnp.bfloat16),
                pltpu.VMEM((D, rows), jnp.bfloat16),
                pltpu.VMEM((rows, D), jnp.bfloat16),
                pltpu.VMEM((16, 72, rows), jnp.float32),
            ],
        ),
        compiler_params=pltpu.CompilerParams(vmem_limit_bytes=62 * 2**20),
        cost_estimate=pl.CostEstimate(
            flops=10 * rows * D * 4 * D, bytes_accessed=64 * 2**20, transcendentals=0
        ),
        name="mlp_back",
    )(at, act, grad, gelu, slope, w_up, w_down)


def qkv_back(at, act, act_far, grad, grad_far, weight):
    rows, far = act.shape[0], act_far.shape[0]

    def kernel(at, a_ref, f_ref, g_ref, h_ref, w_ref, mine, other, c_ref, a_t, f_t, held, held_far):
        t = pl.program_id(0)

        @pl.when(t == 0)
        def _():
            a_t[...] = ordered_transpose(at, a_ref[...], held)
            f_t[...] = ordered_transpose(at, f_ref[...], held_far)
            c_ref[...] = jnp.zeros_like(c_ref)

        c_ref[...] += dot(g_ref[...], w_ref[...], NT)
        away = jnp.where(t > 0, h_ref[...], jnp.zeros_like(h_ref))
        for i, ref in ((0, mine), (1, other)):
            part = slice(i * 576, (i + 1) * 576)
            both = dot(a_t[part], g_ref[...]) + dot(f_t[part], away)
            for j in range(8):
                ref[j // 4, j % 4] = both[j * 72 : j * 72 + 72].astype(jnp.bfloat16)

    once = pl.Buffered(1)
    split = jax.ShapeDtypeStruct((2, 4, 72, 3 * D), jnp.bfloat16)
    split_spec = pl.BlockSpec((2, 4, 72, D), lambda t, at: (0, 0, 0, t))
    return pl.pallas_call(
        kernel,
        out_shape=(split, split, jax.ShapeDtypeStruct((rows, D), jnp.float32)),
        grid_spec=pltpu.PrefetchScalarGridSpec(
            num_scalar_prefetch=1,
            grid=(3,),
            in_specs=[
                pl.BlockSpec((rows, D), lambda t, at: (0, 0), pipeline_mode=once),
                pl.BlockSpec((far, D), lambda t, at: (0, 0), pipeline_mode=once),
                pl.BlockSpec((rows, D), lambda t, at: (0, t)),
                pl.BlockSpec((far, D), lambda t, at: (0, jnp.maximum(t - 1, 0))),
                pl.BlockSpec((D, D), lambda t, at: (0, t)),
            ],
            out_specs=(
                split_spec,
                split_spec,
                pl.BlockSpec((rows, D), lambda t, at: (0, 0), pipeline_mode=once),
            ),
            scratch_shapes=[
                pltpu.VMEM((D, rows), jnp.bfloat16),
                pltpu.VMEM((D, far), jnp.bfloat16),
                pltpu.VMEM((16, 72, rows), jnp.float32),
                pltpu.VMEM((16, 72, far), jnp.float32),
            ],
        ),
        compiler_params=pltpu.CompilerParams(vmem_limit_bytes=60 * 2**20),
        cost_estimate=pl.CostEstimate(
            flops=16 * rows * D * D, bytes_accessed=40 * 2**20, transcendentals=0
        ),
        name="qkv_back",
    )(at, act, act_far, grad, grad_far, weight)


def skip_back(at, tok, skip, grad):
    rows = tok.shape[0]

    def kernel(at, t_ref, s_ref, g_ref, mine, other, in_t):
        i = pl.program_id(0)

        @pl.when(i == 0)
        def _():
            in_t[0:D] = t_ref[...].T
            in_t[D:] = s_ref[...].T

        first = pl.multiple_of(lax.rem(at[0] + i, 4) * 576, 16)
        both = dot(in_t[pl.ds(first, 576)], g_ref[...])
        for yy in (0, 1):
            low, high = both[yy * 288 : yy * 288 + 144], both[yy * 288 + 144 : yy * 288 + 288]
            yrel = yy + at[1] - 2 * yy * at[1]
            for ref, value in (
                (mine, jnp.where(at[2] == 0, low, high)),
                (other, jnp.where(at[2] == 0, high, low)),
            ):
                value = value.astype(jnp.bfloat16)
                ref[at[3], 0, yrel] = value[:72]
                ref[1 - at[3], 0, yrel] = value[72:]

    split = jax.ShapeDtypeStruct((2, 4, 2, 72, D), jnp.bfloat16)
    split_spec = pl.BlockSpec((2, 1, 2, 72, D), lambda t, at: (0, t, 0, 0, 0))
    whole_spec = pl.BlockSpec((rows, D), lambda t, at: (0, 0), pipeline_mode=pl.Buffered(1))
    return pl.pallas_call(
        kernel,
        out_shape=(split, split),
        grid_spec=pltpu.PrefetchScalarGridSpec(
            num_scalar_prefetch=1,
            grid=(4,),
            in_specs=[whole_spec] * 3,
            out_specs=(split_spec, split_spec),
            scratch_shapes=[pltpu.VMEM((2 * D, rows), jnp.bfloat16)],
        ),
        compiler_params=pltpu.CompilerParams(vmem_limit_bytes=40 * 2**20),
        cost_estimate=pl.CostEstimate(
            flops=4 * rows * D * D, bytes_accessed=12 * 2**20, transcendentals=0
        ),
        name="skip_back",
    )(at, tok, skip, grad)


def layer_norm(hidden, gain, shift):
    centred = hidden - jnp.mean(hidden, axis=-1, keepdims=True)
    spread = jnp.mean(centred * centred, axis=-1, keepdims=True)
    return centred * lax.rsqrt(spread + EPS) * gain + shift


def exact_gelu(value):
    return jax.nn.gelu(value, approximate=False)


def segment_ids(offsets, positions):
    hits = (positions[None, :, None] >= offsets[:, None, :]).astype(jnp.int32)
    return jnp.sum(hits, axis=-1)


def fwd_dot(left, right):
    return jnp.dot(left, right, preferred_element_type=jnp.float32)


def contract_rows(left, right):
    return lax.dot_general(
        left, right, (((0,), (0,)), ((), ())), preferred_element_type=jnp.float32
    )


def back_dot(grad_rows, weight):
    return lax.dot_general(
        grad_rows, weight, (((1,), (1,)), ((), ())), preferred_element_type=jnp.float32
    )


class RowAttention:
    def __init__(self, qkv_all, offsets, row_count, local_len):
        self.row_count, self.local_len = row_count, local_len
        self.row_len = local_len * lax.axis_size("seq")
        self.offsets = offsets
        first_pos = lax.axis_index("seq") * local_len
        self.query_seg = segment_ids(offsets, first_pos + jnp.arange(local_len, dtype=jnp.int32))
        self.scale = HD ** (-0.5)
        self.queries = qkv_all[:, :D].reshape(row_count, local_len, HEADS, HD)
        keyvals = qkv_all[:, D:].reshape(row_count, local_len, 2 * D)
        self.kv = lax.all_gather(keyvals, "seq", axis=1, tiled=True)

    def block(self, first, size):
        kv = lax.dynamic_slice_in_dim(self.kv, first, size, 1)
        shape = (self.row_count, size, HEADS, HD)
        key_seg = segment_ids(self.offsets, first + jnp.arange(size, dtype=jnp.int32))
        same = self.query_seg[:, :, None, None] == key_seg[:, None, None, :]
        return kv[:, :, :D].reshape(shape), kv[:, :, D:].reshape(shape), same

    def scores(self, keys):
        return (
            jnp.einsum("rthd,rkhd->rthk", self.queries, keys, preferred_element_type=jnp.float32)
            * self.scale
        )

    def forward(self):
        keys, values, same = self.block(0, self.row_len)
        scores = jnp.where(same, self.scores(keys), -1e30)
        top = jnp.max(scores, axis=-1)
        expo = jnp.where(same, jnp.exp(scores - top[..., None]), 0.0)
        norm = jnp.sum(expo, axis=-1)
        weighted = jnp.einsum(
            "rthk,rkhd->rthd",
            expo.astype(jnp.bfloat16),
            values,
            preferred_element_type=jnp.float32,
        )
        self.attended = weighted / norm[..., None]
        self.log_total = top + jnp.log(norm)
        return self.attended.reshape(-1, D).astype(jnp.bfloat16)

    def backward(self, d_att):
        rows, length = self.row_count, self.local_len
        d_att = d_att.reshape(rows, length, HEADS, HD)
        row_dot = jnp.sum(d_att.astype(jnp.float32) * self.attended, axis=-1)
        size = math.gcd(self.row_len, 512)

        def step(index, totals):
            d_query, d_kv = totals
            keys, values, same = self.block(index * size, size)
            weights = jnp.where(same, jnp.exp(self.scores(keys) - self.log_total[..., None]), 0.0)
            d_weights = jnp.einsum(
                "rthd,rkhd->rthk", d_att, values, preferred_element_type=jnp.float32
            )
            d_scores = (weights * (d_weights - row_dot[..., None])).astype(jnp.bfloat16)
            d_query = d_query + self.scale * jnp.einsum(
                "rthk,rkhd->rthd", d_scores, keys, preferred_element_type=jnp.float32
            )
            d_key = self.scale * jnp.einsum(
                "rthk,rthd->rkhd", d_scores, self.queries, preferred_element_type=jnp.float32
            )
            d_value = jnp.einsum(
                "rthk,rthd->rkhd",
                weights.astype(jnp.bfloat16),
                d_att,
                preferred_element_type=jnp.float32,
            )
            both = jnp.concatenate(
                [d_key.reshape(rows, size, D), d_value.reshape(rows, size, D)], axis=2
            )
            return d_query, lax.dynamic_update_slice_in_dim(d_kv, both, index * size, 1)

        start = (
            jnp.zeros((rows, length, HEADS, HD), jnp.float32),
            jnp.zeros((rows, self.row_len, 2 * D), jnp.float32),
        )
        d_query, d_kv = lax.fori_loop(0, self.row_len // size, step, start)
        d_kv = lax.psum_scatter(
            d_kv.astype(jnp.bfloat16), "seq", scatter_dimension=1, tiled=True
        ).astype(jnp.float32)
        return jnp.concatenate(
            [d_query.reshape(rows * length, D), d_kv.reshape(rows * length, 2 * D)], axis=1
        ).astype(jnp.bfloat16)


def per_device(
    tokens,
    skip_parts,
    lengths,
    cotangent,
    skip_w,
    qkv_w,
    proj_w,
    fc1_w,
    fc2_w,
    skip_bias,
    ln1_gain,
    ln1_bias,
    proj_bias,
    ln2_gain,
    ln2_bias,
    fc1_bias,
    fc2_bias,
):
    row_count, local_len, features = tokens.shape
    tok_count = row_count * local_len
    offsets = jnp.cumsum(lengths, axis=1)
    first_pos = lax.axis_index("seq") * local_len
    query_seg = segment_ids(offsets, first_pos + jnp.arange(local_len, dtype=jnp.int32))
    live_mask = (query_seg < lengths.shape[1]).astype(jnp.float32).reshape(tok_count, 1)
    skip_rows = lax.psum_scatter(skip_parts[0], "seq", scatter_dimension=1, tiled=True)
    w_skip, w_qkv, w_proj, w_up, w_down = (
        lax.all_gather(w, "batch", axis=0, tiled=True)
        for w in (skip_w, qkv_w, proj_w, fc1_w, fc2_w)
    )
    tok_flat = tokens.reshape(tok_count, features)
    skip_flat = skip_rows.reshape(tok_count, features)
    h_zero = (
        fwd_dot(tok_flat, w_skip[:features]) + fwd_dot(skip_flat, w_skip[features:]) + skip_bias
    )
    normed_one, ln1_back = jax.vjp(layer_norm, h_zero, ln1_gain, ln1_bias)
    act_one = normed_one.astype(jnp.bfloat16)
    qkv_all = fwd_dot(act_one, w_qkv).astype(jnp.bfloat16)
    attention = RowAttention(qkv_all, offsets, row_count, local_len)
    att_low = attention.forward()
    h_one = h_zero + fwd_dot(att_low, w_proj) + proj_bias
    normed_two, ln2_back = jax.vjp(layer_norm, h_one, ln2_gain, ln2_bias)
    act_two = normed_two.astype(jnp.bfloat16)
    up_proj = fwd_dot(act_two, w_up) + fc1_bias
    gelu_out, gelu_back = jax.vjp(exact_gelu, up_proj)
    gelu_low = gelu_out.astype(jnp.bfloat16)
    h_two = h_one + fwd_dot(gelu_low, w_down) + fc2_bias
    output = (h_two * live_mask).astype(jnp.bfloat16).reshape(row_count, local_len, features)
    grad_two = cotangent.reshape(tok_count, features).astype(jnp.float32) * live_mask
    grad_low = grad_two.astype(jnp.bfloat16)
    d_w_down = contract_rows(gelu_low, grad_low)
    d_gelu = back_dot(grad_low, w_down)
    d_up = gelu_back(d_gelu)[0]
    up_low = d_up.astype(jnp.bfloat16)
    d_w_up = contract_rows(act_two, up_low)
    d_act_two = back_dot(up_low, w_up)
    d_h_one, d_ln2_gain, d_ln2_bias = ln2_back(d_act_two)
    d_h_one = d_h_one + grad_two
    proj_low = d_h_one.astype(jnp.bfloat16)
    d_w_proj = contract_rows(att_low, proj_low)
    d_att = back_dot(proj_low, w_proj).astype(jnp.bfloat16)
    d_qkv = attention.backward(d_att)
    d_w_qkv = contract_rows(act_one, d_qkv)
    d_act_one = back_dot(d_qkv, w_qkv)
    d_h_zero, d_ln1_gain, d_ln1_bias = ln1_back(d_act_one)
    d_h_zero = d_h_zero + d_h_one
    zero_low = d_h_zero.astype(jnp.bfloat16)
    d_w_skip = jnp.concatenate(
        [contract_rows(tok_flat, zero_low), contract_rows(skip_flat, zero_low)], axis=0
    )
    d_tokens = back_dot(zero_low, w_skip[:features]).reshape(row_count, local_len, features)
    d_skip = back_dot(zero_low, w_skip[features:]).reshape(row_count, local_len, features)
    vector_sums = lax.psum(
        (
            jnp.sum(d_h_zero, axis=0),
            d_ln1_gain,
            d_ln1_bias,
            jnp.sum(d_h_one, axis=0),
            d_ln2_gain,
            d_ln2_bias,
            jnp.sum(d_up, axis=0),
            jnp.sum(grad_two, axis=0),
        ),
        ("batch", "seq"),
    )
    weight_grads = tuple(
        lax.psum(
            lax.psum_scatter(
                grad.astype(jnp.bfloat16), "batch", scatter_dimension=0, tiled=True
            ),
            "seq",
        ).astype(jnp.float32)
        for grad in (d_w_skip, d_w_qkv, d_w_proj, d_w_up, d_w_down)
    )
    return (output, d_tokens, d_skip, *weight_grads, *vector_sums)


YSW = [(b, b ^ 2) for b in range(16)]
CSW = [(b, b ^ 1) for b in range(16)]
ZUP = [(b, (b + 4) % 16) for b in range(16)]


def swap_y(v):
    return lax.ppermute(v, "batch", YSW)


def swap_core(v):
    return lax.ppermute(v, "batch", CSW)


def next_z(v):
    return lax.ppermute(v, "batch", ZUP)


def swap_seq(v):
    return lax.ppermute(v, "seq", [(0, 1), (1, 0)])


def place():
    b = lax.axis_index("batch").astype(jnp.int32)
    return b // 4, (b // 2) % 2, b % 2


def f32(v):
    return v.astype(jnp.float32)


def b16(v):
    return v.astype(jnp.bfloat16)


def core_pair(shard):
    core = place()[2]
    half = shard.shape[1] // 2
    low, high = shard[:, :half], shard[:, half:]
    keep = jnp.where(core == 0, low, high)
    got = swap_core(jnp.where(core == 0, high, low))
    return jnp.where(
        core == 0, jnp.concatenate([keep, got], 0), jnp.concatenate([got, keep], 0)
    )


def tied(*values):
    return lax.optimization_barrier(values)


def with_core(own):
    return own + [swap_core(v) for v in own]


def assemble(pieces, halves):
    rows, cols = pieces[0].shape
    shape = (8 * rows, 2 * cols) if halves else (16 * rows, cols)

    def kernel(at, *refs):
        ins, out, held, came, left = refs[:16], refs[16], refs[17], refs[18], refs[19]
        z, y, c = at[0], at[1], at[2]
        loads = [
            pltpu.make_async_copy(ins[j], held.at[j], came.at[j]) for j in range(16)
        ]
        for load in loads:
            load.start()
        stores = []
        for j in range(16):
            core = c if j < 8 else 1 - c
            yy = y if j % 8 < 4 else 1 - y
            zz = lax.rem(z - j % 4 + 4, 4)
            if halves:
                first = pl.multiple_of((zz * 2 + yy) * rows, 16)
                target = out.at[
                    pl.ds(first, rows), pl.ds(pl.multiple_of(core * cols, 128), cols)
                ]
            else:
                first = pl.multiple_of((zz * 4 + yy * 2 + core) * rows, 16)
                target = out.at[pl.ds(first, rows), :]
            loads[j].wait()
            stores.append(pltpu.make_async_copy(held.at[j], target, left.at[j]))
            stores[-1].start()
        for store in stores:
            store.wait()

    return pl.pallas_call(
        kernel,
        out_shape=jax.ShapeDtypeStruct(shape, pieces[0].dtype),
        in_specs=[pl.BlockSpec(memory_space=pltpu.SMEM)]
        + [pl.BlockSpec(memory_space=pl.ANY)] * 16,
        out_specs=pl.BlockSpec(memory_space=pl.ANY),
        scratch_shapes=[
            pltpu.VMEM((16, rows, cols), pieces[0].dtype),
            pltpu.SemaphoreType.DMA((16,)),
            pltpu.SemaphoreType.DMA((16,)),
        ],
        compiler_params=pltpu.CompilerParams(vmem_limit_bytes=16 * 2**20),
        cost_estimate=pl.CostEstimate(
            flops=0, bytes_accessed=64 * rows * cols, transcendentals=0
        ),
        name="assemble",
    )(jnp.stack(place()), *pieces)


def take(v, axis, index):
    return lax.dynamic_index_in_dim(v, index, axis, keepdims=False)


def added(left, right):
    return b16(f32(left) + f32(right))


def by_side(side, own, other):
    own, other = f32(own), f32(other)
    return jnp.where(
        side == 0, jnp.concatenate([own, other], 0), jnp.concatenate([other, own], 0)
    )


def vector_step(value, bit, axis="batch"):
    if axis == "seq":
        return value + swap_seq(value)
    return value + lax.ppermute(value, "batch", [(b, b ^ bit) for b in range(16)])


def sc_scatter(grad):
    part = lax.psum_scatter(grad, "batch", scatter_dimension=0, tiled=True)
    return f32(part) + f32(swap_seq(part))


def per_device_pair(
    tokens,
    skip_parts,
    lengths,
    cotangent,
    skip_w,
    qkv_w,
    proj_w,
    fc1_w,
    fc2_w,
    skip_bias,
    ln1_gain,
    ln1_bias,
    proj_bias,
    ln2_gain,
    ln2_bias,
    fc1_bias,
    fc2_bias,
):
    count = tokens.shape[1]
    side = lax.axis_index("seq").astype(jnp.int32)
    index = side.reshape(1)
    at = jnp.stack([*place(), side])
    shared = jnp.where(side == 0, 256, 0)
    live = (
        (side * count + lax.broadcasted_iota(jnp.int32, (count, 1), 0)) < jnp.sum(lengths)
    ).astype(jnp.float32)

    parts = skip_parts.reshape(2, count, D)
    skip_far = swap_seq(take(parts, 0, 1 - side))
    tok_flat = tokens.reshape(count, D)

    q0 = core_pair(jnp.concatenate([qkv_w, proj_w], 1))
    s0 = skip_w
    s1, t0 = next_z(s0), swap_y(s0)
    s1, t0 = tied(s1, t0)
    s2, t1 = next_z(s1), swap_y(s1)
    s2, t1, s1, q0 = tied(s2, t1, s1, q0)
    s3, t2, q1 = next_z(s2), swap_y(s2), next_z(q0)
    s3, t2, s2, q0 = tied(s3, t2, s2, q0)
    t3, r0 = swap_y(s3), swap_y(q0)
    w_skip = assemble(with_core([s0, s1, s2, s3, t0, t1, t2, t3]), False)
    r0, q1, w_skip, skip_far = tied(r0, q1, w_skip, skip_far)
    q2, r1 = next_z(q1), swap_y(q1)
    skip_flat = b16(f32(take(parts, 0, side)) + f32(skip_far))
    h_zero = fwd_dot(tok_flat, w_skip[:D]) + fwd_dot(skip_flat, w_skip[D:]) + skip_bias
    normed_one, ln1_back = jax.vjp(layer_norm, h_zero, ln1_gain, ln1_bias)
    act_one = b16(normed_one)
    act_send = lax.dynamic_slice(act_one, (shared, 0), (REM, D))
    q2, r1, act_one, act_send = tied(q2, r1, act_one, act_send)
    act_far = swap_seq(act_send)
    u0 = core_pair(fc1_w)
    q3, r2 = next_z(q2), swap_y(q2)
    q3, r2, u0, q2 = tied(q3, r2, u0, q2)
    r3, u1 = swap_y(q3), next_z(u0)
    r3, u1, q3 = tied(r3, u1, q3)
    u2, v0 = next_z(u1), swap_y(u0)
    w_qp = assemble(with_core([q0, q1, q2, q3, r0, r1, r2, r3]), True)
    w_qkv, w_proj = w_qp[:, : 3 * D], w_qp[:, 3 * D :]
    qkv = b16(fwd_dot(act_one, w_qkv))
    kv_far = b16(fwd_dot(act_far, w_qkv[:, D:]))
    u2, v0, qkv, kv_far, fc2_w = tied(u2, v0, qkv, kv_far, fc2_w)
    w_down = lax.all_gather(fc2_w, "batch", axis=0, tiled=True)
    u3, v1, v2 = next_z(u2), swap_y(u1), swap_y(u2)
    att, lse = attn_fwd(index, qkv, kv_far, 288)
    u3, v1, v2, att = tied(u3, v1, v2, att)
    v3 = swap_y(u3)
    h_one = h_zero + fwd_dot(att, w_proj) + proj_bias
    normed_two, ln2_back = jax.vjp(layer_norm, h_one, ln2_gain, ln2_bias)
    act_two = b16(normed_two)
    w_up = assemble(with_core([u0, u1, u2, u3, v0, v1, v2, v3]), True)
    gelu_low, slope = mlp_up(act_two, w_up, fc1_bias)

    grad_two = f32(cotangent.reshape(count, D)) * live
    grad_low = b16(grad_two)
    dn, dn_got, up, up_got, h_add, d_act_two, d_up_bias = mlp_back(
        at, act_two, grad_low, gelu_low, slope, w_up, w_down
    )
    dn_got, up_got, d_act_two = tied(dn_got, up_got, d_act_two)
    dn_got, up_got = swap_core(dn_got), swap_core(up_got)
    output = b16((h_one + h_add + fc2_bias) * live).reshape(1, count, D)
    d_h_one, d_ln2_gain, d_ln2_bias = ln2_back(d_act_two)
    d_h_one = d_h_one + grad_two
    proj_low = b16(d_h_one)
    d_att = b16(back_dot(proj_low, w_proj))
    d_proj = b16(contract_rows(att, proj_low))
    dn_got, up_got, d_att, d_proj = tied(dn_got, up_got, d_att, d_proj)
    out_proj = sc_scatter(d_proj)
    dn_send, up_send = added(dn[1], dn_got[1]), added(up[1], up_got[1])
    dn_got_x, up_got_y = swap_seq(dn_send), swap_y(up_send)
    dn, up = added(dn[0], dn_got[0]), added(up[0], up_got[0])
    pick = (
        lax.broadcasted_iota(jnp.int32, (D, HEADS), 0) // HD
        == lax.broadcasted_iota(jnp.int32, (D, HEADS), 1)
    ).astype(jnp.float32)
    row_dot = lax.dot_general(
        pick, f32(d_att) * f32(att), (((0,), (1,)), ((), ())), precision=lax.Precision.HIGHEST
    )
    d_qkv, d_far = attn_bwd(index, qkv, kv_far, d_att, lse[:, :HEADS].T, row_dot)
    dn, up, dn_got, up_got, d_qkv, d_far = tied(dn, up, dn_got_x, up_got_y, d_qkv, d_far)
    dn_next, up_next = added(dn[3], dn_got[3]), added(up[3], up_got[3])
    dn_next, up_next = next_z(dn_next), next_z(up_next)
    far = b16(back_dot(d_far, w_qkv[:, D:]))
    dn_next, up_next, far, d_far, d_qkv = tied(dn_next, up_next, far, d_far, d_qkv)
    far = swap_seq(far)
    dn_next, up_next = (
        next_z(b16(f32(dn[2]) + f32(dn_got[2]) + f32(dn_next))),
        next_z(b16(f32(up[2]) + f32(up_got[2]) + f32(up_next))),
    )
    q, q_got, d_act_one = qkv_back(at, act_one, act_far, d_qkv, d_far, w_qkv)
    dn_next, up_next, far, d_act_one, q_got = tied(dn_next, up_next, far, d_act_one, q_got)
    q_got = swap_core(q_got)
    dn_next, up_next = (
        next_z(b16(f32(dn[1]) + f32(dn_got[1]) + f32(dn_next))),
        next_z(b16(f32(up[1]) + f32(up_got[1]) + f32(up_next))),
    )
    here = lax.dynamic_slice(d_act_one, (shared, 0), (REM, D))
    d_act_one = lax.dynamic_update_slice(d_act_one, here + f32(far), (shared, 0))
    d_h_zero, d_ln1_gain, d_ln1_bias = ln1_back(d_act_one)
    d_h_zero = d_h_zero + d_h_one
    zero_low = b16(d_h_zero)
    q_got, zero_low = tied(q_got, zero_low)
    q_send = added(q[1], q_got[1])
    q_got_y = swap_y(q_send)
    q = added(q[0], q_got[0])
    k, k_got = skip_back(at, tok_flat, skip_flat, zero_low)
    sums = jnp.concatenate(
        [
            jnp.sum(d_h_zero, axis=0),
            d_ln1_gain,
            d_ln1_bias,
            jnp.sum(d_h_one, axis=0),
            d_ln2_gain,
            d_ln2_bias,
            d_up_bias[0],
            jnp.sum(grad_two, axis=0),
        ]
    ).reshape(-1, 128)
    dn_next, up_next, k, k_got, zero_low = tied(dn_next, up_next, k, k_got, zero_low)
    d_tokens = back_dot(zero_low, w_skip[:D]).reshape(1, count, D)
    dn_sum = b16(f32(dn[0]) + f32(dn_got[0]) + f32(dn_next))
    up_sum = b16(f32(up[0]) + f32(up_got[0]) + f32(up_next))
    dn_next, up_next, k_got = swap_y(dn_sum[1]), swap_seq(up_sum), swap_core(k_got)
    sums = vector_step(sums, 1)
    out_up = f32(up_sum) + f32(up_next)
    q, q_got, k, k_got, dn_next, dn_sum, sums, zero_low, d_tokens = tied(
        q, q_got_y, k, k_got, dn_next, dn_sum, sums, zero_low, d_tokens
    )
    d_skip = back_dot(zero_low, w_skip[D:]).reshape(1, count, D)
    q_next = next_z(added(q[3], q_got[3]))
    k_got_x = swap_seq(added(k[1], k_got[1]))
    k = added(k[0], k_got[0])
    dn_sum = added(dn_sum[0], dn_next)
    dn_next = swap_seq(dn_sum)
    sums = vector_step(sums, 2)
    q, q_next, q_got, dn_next, sums, d_skip = tied(q, q_next, q_got, dn_next, sums, d_skip)
    out_down = by_side(side, dn_sum, dn_next)
    q_next = next_z(b16(f32(q[2]) + f32(q_got[2]) + f32(q_next)))
    sums = vector_step(sums, 4)
    q, q_next, q_got, k, k_got, sums = tied(q, q_next, q_got, k, k_got_x, sums)
    q_next = next_z(b16(f32(q[1]) + f32(q_got[1]) + f32(q_next)))
    k_next = next_z(added(k[3], k_got[3]))
    sums = vector_step(sums, 8)
    q, q_next, q_got, k_next, k, k_got, sums = tied(q, q_next, q_got, k_next, k, k_got, sums)
    q_sum = b16(f32(q[0]) + f32(q_got[0]) + f32(q_next))
    q_next = swap_seq(q_sum)
    out_qkv = f32(q_sum) + f32(q_next)
    sums = vector_step(sums, 0, "seq").reshape(-1)
    k_next = next_z(b16(f32(k[2]) + f32(k_got[2]) + f32(k_next)))
    k_next = next_z(b16(f32(k[1]) + f32(k_got[1]) + f32(k_next)))
    k_sum = b16(f32(k[0]) + f32(k_got[0]) + f32(k_next))
    k_sum = added(k_sum[0], swap_y(k_sum[1]))
    out_skip = by_side(side, k_sum, swap_seq(k_sum))
    starts = [0, D, 2 * D, 3 * D, 4 * D, 5 * D, 6 * D, 10 * D, 11 * D]
    sums = [sums[a:b] for a, b in zip(starts, starts[1:])]
    grads = (out_skip, out_qkv, out_proj, out_up, out_down)
    return (output, d_tokens, d_skip, *grads, *sums)


def solution(mesh):
    in_specs = (
        P("batch", "seq", None),
        P("seq", "batch", None, None),
        P("batch", None),
        P("batch", "seq", None),
        *(P("batch", None),) * 5,
        *(P(),) * 8,
    )
    out_specs = (*(P("batch", "seq", None),) * 3, *(P("batch", None),) * 5, *(P(),) * 8)
    pair = mesh.shape["batch"] == ROWS and mesh.shape["seq"] == 2
    return jax.shard_map(
        per_device_pair if pair else per_device,
        mesh=mesh,
        in_specs=in_specs,
        out_specs=out_specs,
        check_vma=False,

    )
```

```python
import math

import jax
import jax.numpy as jnp
from jax import lax
from jax.experimental import pallas as pl
from jax.experimental.pallas import tpu as pltpu
from jax.sharding import PartitionSpec as P

HEADS = 16
HD = 72
D = 1152
ROWS = 16
EPS = 1e-05

SCALE=HD**-0.5
C2=SCALE*math.log2(math.e)
REM=576
TILES={
 0:[(256,576,258,832,[(0,256,576,258,832),(1,0,464,0,452)]),
    (0,272,0,258,[(0,0,272,0,258)])],
 1:[(0,464,0,452,[(0,0,464,0,452),(1,0,576,2,576)]),
    (448,272,452,710,[(0,448,272,452,710)]),
    (704,128,710,832,[(0,704,128,710,832)])],
}
NT=(((1,),(1,)),((),()))
TN=(((0,),(0,)),((),()))
def dot(a,b,dims=(((1,),(0,)),((),()))):
    return lax.dot_general(a,b,dims,preferred_element_type=jnp.float32)

def split(n,step):
    out=[];i=0
    while i<n:
        out.append((i,min(step,n-i))); i+=step
    return out

def fwd_kernel(s_ref, qkv_ref, kvr_ref, *refs, qstep, first):
    o_ref, l_ref = refs[-2:]
    h = pl.program_id(0) + first

    @pl.when(h == first)
    def _():
        for ref, old in zip((o_ref, l_ref), refs[:-2] or (None, None)):
            ref[...] = jnp.zeros_like(ref) if old is None else old[...]

    t=jnp.minimum((72*h)//128, 7)
    lo=72*h-128*t
    base=pl.multiple_of(t*128,128)
    def win(ref,off,r0,n):
        return ref[r0:r0+n, pl.ds(pl.multiple_of(base+off,128),256)]
    def tile(q0,nq,qv0,qv1,keys):
        lane=lax.broadcasted_iota(jnp.int32,(1,256),1)
        hm=(lane>=lo)&(lane<lo+72)
        for (a,n) in split(nq,qstep):
            r0=q0+a
            q=win(qkv_ref,0,r0,n)
            qm=jnp.where(hm,q,jnp.zeros_like(q))
            ss=[]
            for (src,k0,kc,kv0,kv1) in keys:
                k=win(qkv_ref,D,k0,kc) if src==0 else win(kvr_ref,0,k0,kc)
                s=dot(qm,k,NT)
                if kv0>k0 or kv1<k0+kc:
                    kp=k0+lax.broadcasted_iota(jnp.int32,(1,kc),1)
                    s=jnp.where((kp>=kv0)&(kp<kv1),s,-1e30)
                ss.append(s)
            m=jnp.max(ss[0],axis=1,keepdims=True)
            for s in ss[1:]: m=jnp.maximum(m,jnp.max(s,axis=1,keepdims=True))
            mc=m*C2
            l=None; o=None
            for s,(src,k0,kc,kv0,kv1) in zip(ss,keys):
                p=jnp.exp2(s*C2-mc)
                lp=jnp.sum(p,axis=1,keepdims=True)
                v=win(qkv_ref,2*D,k0,kc) if src==0 else win(kvr_ref,D,k0,kc)
                op=dot(p.astype(jnp.bfloat16),v)
                l=lp if l is None else l+lp
                o=op if o is None else o+op
            o=o*(1.0/l)
            lse=mc+jnp.log2(l)
            sl=(slice(r0,r0+n),pl.ds(base,256))
            old=o_ref[sl]; ob=o.astype(jnp.bfloat16)
            hl=lax.broadcasted_iota(jnp.int32,(1,128),1)==h
            oldl=l_ref[r0:r0+n,:]
            if r0<qv0 or r0+n>qv1:
                row=r0+lax.broadcasted_iota(jnp.int32,(n,1),0)
                rv=(row>=qv0)&(row<qv1)
                o_ref[sl]=jnp.where(hm&rv,ob,old)
                l_ref[r0:r0+n,:]=jnp.where(hl&rv,lse,oldl)
            else:
                o_ref[sl]=jnp.where(hm,ob,old)
                l_ref[r0:r0+n,:]=jnp.where(hl,lse,oldl)
    for sidx in (0,1):
        @pl.when(s_ref[0]==sidx)
        def _():
            for tl in TILES[sidx]: tile(*tl)

def full(shape,n=1):
    return pl.BlockSpec(shape,lambda h,s:(0,)*len(shape),pipeline_mode=pl.Buffered(1))
def attn_fwd(sidx, qkv, kvr, first, count, prev=(), qstep=288):
    return pl.pallas_call(
        lambda *r: fwd_kernel(*r, qstep=qstep, first=first),
        out_shape=(
            jax.ShapeDtypeStruct((832, D), jnp.bfloat16),
            jax.ShapeDtypeStruct((832, 128), jnp.float32),
        ),
        grid_spec=pltpu.PrefetchScalarGridSpec(
            num_scalar_prefetch=1,
            grid=(count,),
            in_specs=[full((832, 3 * D)), full((REM, 2 * D))] + [full(v.shape) for v in prev],
            out_specs=(full((832, D)), full((832, 128))),
        ),
        compiler_params=pltpu.CompilerParams(vmem_limit_bytes=60 * 2**20),
        cost_estimate=pl.CostEstimate(
            flops=count * 1200 * 10**6, bytes_accessed=12 * 2**20, transcendentals=0
        ),
        name="attn_fwd",
    )(sidx, qkv, kvr, *prev)


def bwd_kernel(s_ref, qkv_ref, kvr_ref, do_ref, lt_ref, dt_ref, *refs, kstep, expl, first):
    dqkv_ref, dkvr_ref = refs[-2:]
    h = pl.program_id(0) + first

    @pl.when(h == first)
    def _():
        for ref, old in zip((dqkv_ref, dkvr_ref), refs[:-2] or (None, None)):
            ref[...] = jnp.zeros_like(ref) if old is None else old[...]

    t=jnp.minimum((72*h)//128, 7)
    lo=72*h-128*t
    base=pl.multiple_of(t*128,128)
    def ws(off,r0,n):
        return (slice(r0,r0+n), pl.ds(pl.multiple_of(base+off,128),256))
    def tile(q0,nq,qv0,qv1,keys):
        lane=lax.broadcasted_iota(jnp.int32,(1,256),1)
        hm=(lane>=lo)&(lane<lo+72)
        q=qkv_ref[ws(0,q0,nq)]; qm=jnp.where(hm,q,jnp.zeros_like(q))
        do=do_ref[ws(0,q0,nq)]; dom=jnp.where(hm,do,jnp.zeros_like(do))
        lrow=lt_ref[pl.ds(h,1),:][:,q0:q0+nq]; drow=dt_ref[pl.ds(h,1),:][:,q0:q0+nq]
        if qv0>q0 or qv1<q0+nq:
            qp=q0+lax.broadcasted_iota(jnp.int32,(1,nq),1)
            lrow=jnp.where((qp>=qv0)&(qp<qv1),lrow,1e30)
        dqt=None
        for (src,k00,kcc,kv0,kv1) in keys:
            for (a,kc) in split(kcc,kstep):
                k0=k00+a
                k=qkv_ref[ws(D,k0,kc)] if src==0 else kvr_ref[ws(0,k0,kc)]
                v=qkv_ref[ws(2*D,k0,kc)] if src==0 else kvr_ref[ws(D,k0,kc)]
                st=dot(k,qm,NT)
                p=jnp.exp2(st*C2-lrow)
                if kv0>k0 or kv1<k0+kc:
                    kp=k0+lax.broadcasted_iota(jnp.int32,(kc,1),0)
                    p=jnp.where((kp>=kv0)&(kp<kv1),p,0.0)
                dp=dot(v,dom,NT)
                ds=(p*(dp-drow)).astype(jnp.bfloat16)
                dv=dot(p.astype(jnp.bfloat16),dom)
                dk=dot(ds,qm)*SCALE
                if src==0:
                    dqkv_ref[ws(D,k0,kc)]+=dk.astype(jnp.bfloat16)
                    dqkv_ref[ws(2*D,k0,kc)]+=dv.astype(jnp.bfloat16)
                else:
                    dkvr_ref[ws(0,k0,kc)]+=dk.astype(jnp.bfloat16)
                    dkvr_ref[ws(D,k0,kc)]+=dv.astype(jnp.bfloat16)
                if expl: d=dot(k.T,ds)
                else: d=dot(k,ds,TN)
                dqt=d if dqt is None else dqt+d
        dq=(dqt*SCALE).T
        sl=ws(0,q0,nq)
        dqkv_ref[sl]=dqkv_ref[sl]+jnp.where(hm,dq,0.0).astype(jnp.bfloat16)
    for sidx in (0,1):
        @pl.when(s_ref[0]==sidx)
        def _():
            for tl in TILES[sidx]: tile(*tl)

def attn_bwd(sidx, qkv, kvr, do, lt, dt, first, count, prev=(), kstep=1024, expl=True):
    return pl.pallas_call(
        lambda *r: bwd_kernel(*r, kstep=kstep, expl=expl, first=first),
        out_shape=(
            jax.ShapeDtypeStruct((832, 3 * D), jnp.bfloat16),
            jax.ShapeDtypeStruct((REM, 2 * D), jnp.bfloat16),
        ),
        grid_spec=pltpu.PrefetchScalarGridSpec(
            num_scalar_prefetch=1,
            grid=(count,),
            in_specs=[
                full((832, 3 * D)),
                full((REM, 2 * D)),
                full((832, D)),
                full((16, 832)),
                full((16, 832)),
            ]
            + [full(v.shape) for v in prev],
            out_specs=(full((832, 3 * D)), full((REM, 2 * D))),
        ),
        compiler_params=pltpu.CompilerParams(vmem_limit_bytes=60 * 2**20),
        cost_estimate=pl.CostEstimate(
            flops=count * 2500 * 10**6, bytes_accessed=20 * 2**20, transcendentals=0
        ),
        name="attn_bwd",
    )(sidx, qkv, kvr, do, lt, dt, *prev)


ERFC = (0.5 * 1.061405429, -0.5 * 1.453152027, 0.5 * 1.421413741, -0.5 * 0.284496736, 0.5 * 0.254829592)


def normal_cdf(u):
    expo = jnp.exp2(u * u * (-0.5 * math.log2(math.e)))
    below = 1.0 + (0.3275911 * math.sqrt(0.5)) * jnp.abs(u)
    step = pltpu.reciprocal(below, approx=True)
    step = step * (2.0 - below * step)
    tail = ERFC[0]
    for term in ERFC[1:]:
        tail = tail * step + term
    tail = tail * step * expo
    return jnp.where(u < 0.0, tail, 1.0 - tail), expo


def mlp_up(at, act, weight, bias, grad, tile=D, chunks=4):
    rows, width = act.shape[0], weight.shape[1]
    steps = width // tile
    size = rows // chunks

    def kernel(at, a_ref, w_ref, b_ref, e_ref, g_ref, d_ref, mine, other, held):
        t = pl.program_id(0)

        def forward():
            for i in range(chunks):
                part = slice(i * size, (i + 1) * size)
                u = dot(a_ref[part], w_ref[...]) + b_ref[...]
                phi, expo = normal_cdf(u)
                g = (u * phi).astype(jnp.bfloat16)
                g_ref[part] = g
                d_ref[part] = (phi + u * expo * (1.0 / math.sqrt(2.0 * math.pi))).astype(jnp.bfloat16)

        def keep():
            held[...] = g_ref[...].T

        def back():
            for yy in (0, 1):
                both = dot(held[yy * 576 : yy * 576 + 576], e_ref[...])
                low, high = both[:288], both[288:]
                yrel = yy + at[1] - 2 * yy * at[1]
                for ref, value in (
                    (mine, jnp.where(at[2] == 0, low, high)),
                    (other, jnp.where(at[2] == 0, high, low)),
                ):
                    value = value.astype(jnp.bfloat16)
                    ref[at[3], yrel, 0] = value[:144]
                    ref[1 - at[3], yrel, 0] = value[144:]

        @pl.when(t == 0)
        def _():
            forward()
            keep()

        @pl.when((t > 0) & (t < steps))
        def _():
            back()
            forward()
            keep()

        @pl.when(t == steps)
        def _():
            back()

    out = jax.ShapeDtypeStruct((rows, width), jnp.bfloat16)
    split = jax.ShapeDtypeStruct((2, 2, 4, 144, D), jnp.bfloat16)

    def now(t):
        return jnp.minimum(t, steps - 1)

    whole = pl.BlockSpec((rows, D), lambda t, at: (0, 0), pipeline_mode=pl.Buffered(1))
    by_column = pl.BlockSpec((rows, tile), lambda t, at: (0, now(t)))
    split_spec = pl.BlockSpec((2, 2, 1, 144, D), lambda t, at: (0, 0, jnp.maximum(t - 1, 0), 0, 0))
    return pl.pallas_call(
        kernel,
        out_shape=(out, out, split, split),
        grid_spec=pltpu.PrefetchScalarGridSpec(
            num_scalar_prefetch=1,
            grid=(steps + 1,),
            in_specs=[
                whole,
                pl.BlockSpec((D, tile), lambda t, at: (0, now(t))),
                pl.BlockSpec((1, tile), lambda t, at: (0, now(t))),
                whole,
            ],
            out_specs=(by_column, by_column, split_spec, split_spec),
            scratch_shapes=[pltpu.VMEM((tile, rows), jnp.bfloat16)],
        ),
        compiler_params=pltpu.CompilerParams(vmem_limit_bytes=60 * 2**20),
        cost_estimate=pl.CostEstimate(
            flops=4 * rows * D * width,
            bytes_accessed=5 * D * width,
            transcendentals=rows * width,
        ),
        name="mlp_up",
    )(at, act, weight, bias.reshape(1, width), grad)


def ordered_transpose(at, value, held, ring=True):
    held[...] = value.astype(jnp.float32).T.reshape(held.shape)
    blocks = []
    for crel in (0, 1):
        for yrel in (0, 1):
            for zrel in range(4):
                zz = lax.rem(at[0] + zrel, 4) if ring else zrel
                yy = at[1] + yrel - 2 * at[1] * yrel
                cc = at[2] + crel - 2 * at[2] * crel
                blocks.append(held[zz * 4 + yy * 2 + cc])
    return jnp.concatenate(blocks, 0).astype(jnp.bfloat16)


def mlp_back(at, act, grad, gelu, slope, w_up, w_down, halves=1, tile=768):
    rows, width = gelu.shape
    half = rows // halves

    def kernel(at, a_ref, e_ref, g_ref, s_ref, wu_ref, wd_ref, *refs):
        mine, other, h_ref, c_ref, b_ref, a_t, du_ref, held = refs

        @pl.when(pl.program_id(0) == 0)
        def _():
            a_t[...] = ordered_transpose(at, a_ref[...], held, ring=False)
            h_ref[...] = jnp.zeros_like(h_ref)
            c_ref[...] = jnp.zeros_like(c_ref)

        bias = None
        for i in range(halves):
            part = slice(i * half, (i + 1) * half)
            du = dot(e_ref[part], wd_ref[...], NT) * s_ref[part].astype(jnp.float32)
            total = jnp.sum(du, axis=0, keepdims=True)
            bias = total if bias is None else bias + total
            du = du.astype(jnp.bfloat16)
            du_ref[part] = du
            h_ref[part] += dot(g_ref[part], wd_ref[...])
            c_ref[part] += dot(du, wu_ref[...], NT)
        b_ref[...] = bias
        for i, ref in ((0, mine), (1, other)):
            both = dot(a_t[i * 576 : i * 576 + 576], du_ref[...])
            for j in range(8):
                ref[j // 4, j % 4] = both[j * 72 : j * 72 + 72].astype(jnp.bfloat16)

    once = pl.Buffered(1)
    whole = jax.ShapeDtypeStruct((rows, D), jnp.float32)
    split = jax.ShapeDtypeStruct((2, 4, 72, width), jnp.bfloat16)
    split_spec = pl.BlockSpec((2, 4, 72, tile), lambda t, at: (0, 0, 0, t))
    whole_spec = pl.BlockSpec((rows, D), lambda t, at: (0, 0), pipeline_mode=once)
    by_column = pl.BlockSpec((rows, tile), lambda t, at: (0, t))
    weight_column = pl.BlockSpec((D, tile), lambda t, at: (0, t))
    return pl.pallas_call(
        kernel,
        out_shape=(
            split,
            split,
            whole,
            whole,
            jax.ShapeDtypeStruct((1, width), jnp.float32),
        ),
        grid_spec=pltpu.PrefetchScalarGridSpec(
            num_scalar_prefetch=1,
            grid=(width // tile,),
            in_specs=[
                whole_spec,
                whole_spec,
                by_column,
                by_column,
                weight_column,
                pl.BlockSpec((tile, D), lambda t, at: (t, 0)),
            ],
            out_specs=(
                split_spec,
                split_spec,
                whole_spec,
                whole_spec,
                pl.BlockSpec((1, tile), lambda t, at: (0, t)),
            ),
            scratch_shapes=[
                pltpu.VMEM((D, rows), jnp.bfloat16),
                pltpu.VMEM((rows, tile), jnp.bfloat16),
                pltpu.VMEM((16, 72, rows), jnp.float32),
            ],
        ),
        compiler_params=pltpu.CompilerParams(vmem_limit_bytes=62 * 2**20),
        cost_estimate=pl.CostEstimate(
            flops=8 * rows * D * width, bytes_accessed=50 * 2**20, transcendentals=0
        ),
        name="mlp_back",
    )(at, act, grad, gelu, slope, w_up, w_down)


def qkv_grad(at, act, act_far, grad, grad_far):
    rows, far = act.shape[0], act_far.shape[0]

    def kernel(at, a_ref, f_ref, g_ref, h_ref, mine, other, a_t, f_t, held, held_far):
        t = pl.program_id(0)

        @pl.when(t == 0)
        def _():
            a_t[...] = ordered_transpose(at, a_ref[...], held)
            f_t[...] = ordered_transpose(at, f_ref[...], held_far)

        away = jnp.where(t > 0, h_ref[...], jnp.zeros_like(h_ref))
        for i, ref in ((0, mine), (1, other)):
            part = slice(i * 576, (i + 1) * 576)
            both = dot(a_t[part], g_ref[...]) + dot(f_t[part], away)
            for j in range(8):
                ref[j // 4, j % 4] = both[j * 72 : j * 72 + 72].astype(jnp.bfloat16)

    once = pl.Buffered(1)
    split = jax.ShapeDtypeStruct((2, 4, 72, 3 * D), jnp.bfloat16)
    split_spec = pl.BlockSpec((2, 4, 72, D), lambda t, at: (0, 0, 0, t))
    return pl.pallas_call(
        kernel,
        out_shape=(split, split),
        grid_spec=pltpu.PrefetchScalarGridSpec(
            num_scalar_prefetch=1,
            grid=(3,),
            in_specs=[
                pl.BlockSpec((rows, D), lambda t, at: (0, 0), pipeline_mode=once),
                pl.BlockSpec((far, D), lambda t, at: (0, 0), pipeline_mode=once),
                pl.BlockSpec((rows, D), lambda t, at: (0, t)),
                pl.BlockSpec((far, D), lambda t, at: (0, jnp.maximum(t - 1, 0))),
            ],
            out_specs=(split_spec, split_spec),
            scratch_shapes=[
                pltpu.VMEM((D, rows), jnp.bfloat16),
                pltpu.VMEM((D, far), jnp.bfloat16),
                pltpu.VMEM((16, 72, rows), jnp.float32),
                pltpu.VMEM((16, 72, far), jnp.float32),
            ],
        ),
        compiler_params=pltpu.CompilerParams(vmem_limit_bytes=60 * 2**20),
        cost_estimate=pl.CostEstimate(
            flops=10 * rows * D * D, bytes_accessed=40 * 2**20, transcendentals=0
        ),
        name="qkv_grad",
    )(at, act, act_far, grad, grad_far)


def skip_back(at, tok, skip, grad):
    rows = tok.shape[0]

    def kernel(at, t_ref, s_ref, g_ref, mine, other, in_t):
        i = pl.program_id(0)

        @pl.when(i == 0)
        def _():
            in_t[0:D] = t_ref[...].T
            in_t[D:] = s_ref[...].T

        first = pl.multiple_of(lax.rem(at[0] + i, 4) * 576, 16)
        both = dot(in_t[pl.ds(first, 576)], g_ref[...])
        for yy in (0, 1):
            low, high = both[yy * 288 : yy * 288 + 144], both[yy * 288 + 144 : yy * 288 + 288]
            yrel = yy + at[1] - 2 * yy * at[1]
            mine[yrel, 0] = jnp.where(at[2] == 0, low, high).astype(jnp.bfloat16)
            other[yrel, 0] = jnp.where(at[2] == 0, high, low).astype(jnp.bfloat16)

    split = jax.ShapeDtypeStruct((2, 4, 144, D), jnp.bfloat16)
    split_spec = pl.BlockSpec((2, 1, 144, D), lambda t, at: (0, t, 0, 0))
    whole_spec = pl.BlockSpec((rows, D), lambda t, at: (0, 0), pipeline_mode=pl.Buffered(1))
    return pl.pallas_call(
        kernel,
        out_shape=(split, split),
        grid_spec=pltpu.PrefetchScalarGridSpec(
            num_scalar_prefetch=1,
            grid=(4,),
            in_specs=[whole_spec] * 3,
            out_specs=(split_spec, split_spec),
            scratch_shapes=[pltpu.VMEM((2 * D, rows), jnp.bfloat16)],
        ),
        compiler_params=pltpu.CompilerParams(vmem_limit_bytes=40 * 2**20),
        cost_estimate=pl.CostEstimate(
            flops=4 * rows * D * D, bytes_accessed=12 * 2**20, transcendentals=0
        ),
        name="skip_back",
    )(at, tok, skip, grad)


def layer_norm(hidden, gain, shift):
    centred = hidden - jnp.mean(hidden, axis=-1, keepdims=True)
    spread = jnp.mean(centred * centred, axis=-1, keepdims=True)
    return centred * lax.rsqrt(spread + EPS) * gain + shift


def exact_gelu(value):
    return jax.nn.gelu(value, approximate=False)


def segment_ids(offsets, positions):
    hits = (positions[None, :, None] >= offsets[:, None, :]).astype(jnp.int32)
    return jnp.sum(hits, axis=-1)


def fwd_dot(left, right):
    return jnp.dot(left, right, preferred_element_type=jnp.float32)


def contract_rows(left, right):
    return lax.dot_general(
        left, right, (((0,), (0,)), ((), ())), preferred_element_type=jnp.float32
    )


def back_dot(grad_rows, weight):
    return lax.dot_general(
        grad_rows, weight, (((1,), (1,)), ((), ())), preferred_element_type=jnp.float32
    )


class RowAttention:
    def __init__(self, qkv_all, offsets, row_count, local_len):
        self.row_count, self.local_len = row_count, local_len
        self.row_len = local_len * lax.axis_size("seq")
        self.offsets = offsets
        first_pos = lax.axis_index("seq") * local_len
        self.query_seg = segment_ids(offsets, first_pos + jnp.arange(local_len, dtype=jnp.int32))
        self.scale = HD ** (-0.5)
        self.queries = qkv_all[:, :D].reshape(row_count, local_len, HEADS, HD)
        keyvals = qkv_all[:, D:].reshape(row_count, local_len, 2 * D)
        self.kv = lax.all_gather(keyvals, "seq", axis=1, tiled=True)

    def block(self, first, size):
        kv = lax.dynamic_slice_in_dim(self.kv, first, size, 1)
        shape = (self.row_count, size, HEADS, HD)
        key_seg = segment_ids(self.offsets, first + jnp.arange(size, dtype=jnp.int32))
        same = self.query_seg[:, :, None, None] == key_seg[:, None, None, :]
        return kv[:, :, :D].reshape(shape), kv[:, :, D:].reshape(shape), same

    def scores(self, keys):
        return (
            jnp.einsum("rthd,rkhd->rthk", self.queries, keys, preferred_element_type=jnp.float32)
            * self.scale
        )

    def forward(self):
        keys, values, same = self.block(0, self.row_len)
        scores = jnp.where(same, self.scores(keys), -1e30)
        top = jnp.max(scores, axis=-1)
        expo = jnp.where(same, jnp.exp(scores - top[..., None]), 0.0)
        norm = jnp.sum(expo, axis=-1)
        weighted = jnp.einsum(
            "rthk,rkhd->rthd",
            expo.astype(jnp.bfloat16),
            values,
            preferred_element_type=jnp.float32,
        )
        self.attended = weighted / norm[..., None]
        self.log_total = top + jnp.log(norm)
        return self.attended.reshape(-1, D).astype(jnp.bfloat16)

    def backward(self, d_att):
        rows, length = self.row_count, self.local_len
        d_att = d_att.reshape(rows, length, HEADS, HD)
        row_dot = jnp.sum(d_att.astype(jnp.float32) * self.attended, axis=-1)
        size = math.gcd(self.row_len, 512)

        def step(index, totals):
            d_query, d_kv = totals
            keys, values, same = self.block(index * size, size)
            weights = jnp.where(same, jnp.exp(self.scores(keys) - self.log_total[..., None]), 0.0)
            d_weights = jnp.einsum(
                "rthd,rkhd->rthk", d_att, values, preferred_element_type=jnp.float32
            )
            d_scores = (weights * (d_weights - row_dot[..., None])).astype(jnp.bfloat16)
            d_query = d_query + self.scale * jnp.einsum(
                "rthk,rkhd->rthd", d_scores, keys, preferred_element_type=jnp.float32
            )
            d_key = self.scale * jnp.einsum(
                "rthk,rthd->rkhd", d_scores, self.queries, preferred_element_type=jnp.float32
            )
            d_value = jnp.einsum(
                "rthk,rthd->rkhd",
                weights.astype(jnp.bfloat16),
                d_att,
                preferred_element_type=jnp.float32,
            )
            both = jnp.concatenate(
                [d_key.reshape(rows, size, D), d_value.reshape(rows, size, D)], axis=2
            )
            return d_query, lax.dynamic_update_slice_in_dim(d_kv, both, index * size, 1)

        start = (
            jnp.zeros((rows, length, HEADS, HD), jnp.float32),
            jnp.zeros((rows, self.row_len, 2 * D), jnp.float32),
        )
        d_query, d_kv = lax.fori_loop(0, self.row_len // size, step, start)
        d_kv = lax.psum_scatter(
            d_kv.astype(jnp.bfloat16), "seq", scatter_dimension=1, tiled=True
        ).astype(jnp.float32)
        return jnp.concatenate(
            [d_query.reshape(rows * length, D), d_kv.reshape(rows * length, 2 * D)], axis=1
        ).astype(jnp.bfloat16)


def per_device(
    tokens,
    skip_parts,
    lengths,
    cotangent,
    skip_w,
    qkv_w,
    proj_w,
    fc1_w,
    fc2_w,
    skip_bias,
    ln1_gain,
    ln1_bias,
    proj_bias,
    ln2_gain,
    ln2_bias,
    fc1_bias,
    fc2_bias,
):
    row_count, local_len, features = tokens.shape
    tok_count = row_count * local_len
    offsets = jnp.cumsum(lengths, axis=1)
    first_pos = lax.axis_index("seq") * local_len
    query_seg = segment_ids(offsets, first_pos + jnp.arange(local_len, dtype=jnp.int32))
    live_mask = (query_seg < lengths.shape[1]).astype(jnp.float32).reshape(tok_count, 1)
    skip_rows = lax.psum_scatter(skip_parts[0], "seq", scatter_dimension=1, tiled=True)
    w_skip, w_qkv, w_proj, w_up, w_down = (
        lax.all_gather(w, "batch", axis=0, tiled=True)
        for w in (skip_w, qkv_w, proj_w, fc1_w, fc2_w)
    )
    tok_flat = tokens.reshape(tok_count, features)
    skip_flat = skip_rows.reshape(tok_count, features)
    h_zero = (
        fwd_dot(tok_flat, w_skip[:features]) + fwd_dot(skip_flat, w_skip[features:]) + skip_bias
    )
    normed_one, ln1_back = jax.vjp(layer_norm, h_zero, ln1_gain, ln1_bias)
    act_one = normed_one.astype(jnp.bfloat16)
    qkv_all = fwd_dot(act_one, w_qkv).astype(jnp.bfloat16)
    attention = RowAttention(qkv_all, offsets, row_count, local_len)
    att_low = attention.forward()
    h_one = h_zero + fwd_dot(att_low, w_proj) + proj_bias
    normed_two, ln2_back = jax.vjp(layer_norm, h_one, ln2_gain, ln2_bias)
    act_two = normed_two.astype(jnp.bfloat16)
    up_proj = fwd_dot(act_two, w_up) + fc1_bias
    gelu_out, gelu_back = jax.vjp(exact_gelu, up_proj)
    gelu_low = gelu_out.astype(jnp.bfloat16)
    h_two = h_one + fwd_dot(gelu_low, w_down) + fc2_bias
    output = (h_two * live_mask).astype(jnp.bfloat16).reshape(row_count, local_len, features)
    grad_two = cotangent.reshape(tok_count, features).astype(jnp.float32) * live_mask
    grad_low = grad_two.astype(jnp.bfloat16)
    d_w_down = contract_rows(gelu_low, grad_low)
    d_gelu = back_dot(grad_low, w_down)
    d_up = gelu_back(d_gelu)[0]
    up_low = d_up.astype(jnp.bfloat16)
    d_w_up = contract_rows(act_two, up_low)
    d_act_two = back_dot(up_low, w_up)
    d_h_one, d_ln2_gain, d_ln2_bias = ln2_back(d_act_two)
    d_h_one = d_h_one + grad_two
    proj_low = d_h_one.astype(jnp.bfloat16)
    d_w_proj = contract_rows(att_low, proj_low)
    d_att = back_dot(proj_low, w_proj).astype(jnp.bfloat16)
    d_qkv = attention.backward(d_att)
    d_w_qkv = contract_rows(act_one, d_qkv)
    d_act_one = back_dot(d_qkv, w_qkv)
    d_h_zero, d_ln1_gain, d_ln1_bias = ln1_back(d_act_one)
    d_h_zero = d_h_zero + d_h_one
    zero_low = d_h_zero.astype(jnp.bfloat16)
    d_w_skip = jnp.concatenate(
        [contract_rows(tok_flat, zero_low), contract_rows(skip_flat, zero_low)], axis=0
    )
    d_tokens = back_dot(zero_low, w_skip[:features]).reshape(row_count, local_len, features)
    d_skip = back_dot(zero_low, w_skip[features:]).reshape(row_count, local_len, features)
    vector_sums = lax.psum(
        (
            jnp.sum(d_h_zero, axis=0),
            d_ln1_gain,
            d_ln1_bias,
            jnp.sum(d_h_one, axis=0),
            d_ln2_gain,
            d_ln2_bias,
            jnp.sum(d_up, axis=0),
            jnp.sum(grad_two, axis=0),
        ),
        ("batch", "seq"),
    )
    weight_grads = tuple(
        lax.psum(
            lax.psum_scatter(
                grad.astype(jnp.bfloat16), "batch", scatter_dimension=0, tiled=True
            ),
            "seq",
        ).astype(jnp.float32)
        for grad in (d_w_skip, d_w_qkv, d_w_proj, d_w_up, d_w_down)
    )
    return (output, d_tokens, d_skip, *weight_grads, *vector_sums)


YSW = [(b, b ^ 2) for b in range(16)]
CSW = [(b, b ^ 1) for b in range(16)]
ZUP = [(b, (b + 4) % 16) for b in range(16)]


def swap_y(v):
    return lax.ppermute(v, "batch", YSW)


def swap_core(v):
    return lax.ppermute(v, "batch", CSW)


def next_z(v):
    return lax.ppermute(v, "batch", ZUP)


def swap_seq(v):
    return lax.ppermute(v, "seq", [(0, 1), (1, 0)])


def place():
    b = lax.axis_index("batch").astype(jnp.int32)
    return b // 4, (b // 2) % 2, b % 2


def f32(v):
    return v.astype(jnp.float32)


def b16(v):
    return v.astype(jnp.bfloat16)


def core_pair(shard):
    core = place()[2]
    half = shard.shape[1] // 2
    low, high = shard[:, :half], shard[:, half:]
    keep = jnp.where(core == 0, low, high)
    got = swap_core(jnp.where(core == 0, high, low))
    return jnp.where(
        core == 0, jnp.concatenate([keep, got], 0), jnp.concatenate([got, keep], 0)
    )


def tied(*values):
    return lax.optimization_barrier(values)


def with_core(own):
    return own + [swap_core(v) for v in own]


def assemble(pieces, kind):
    rows, cols = pieces[0].shape
    split, halves, paired = kind == "split", kind.endswith("halves"), kind == "halves"
    if split:
        shapes = [(8 * rows, 3 * D), (8 * rows, D)]
    elif halves:
        shapes = [(8 * rows, 2 * cols)]
    else:
        shapes = [(16 * rows, cols)]

    def kernel(at, *refs):
        ins, outs, (held, came, left) = refs[:16], refs[16:-3], refs[-3:]
        z, y, c, x = at[0], at[1], at[2], at[3]
        loads = [pltpu.make_async_copy(ins[j], held.at[j], came.at[j]) for j in range(16)]
        for load in loads:
            load.start()
        waits = []
        for j in range(16):
            core = c if j < 8 else 1 - c
            yy = y if j % 8 < 4 else 1 - y
            away = j % 4
            if paired and j % 8 in (4, 5):
                away = away + x - 2 * away * x
            zz = lax.rem(z - away + 4, 4)
            loads[j].wait()
            if not split:
                if halves:
                    first = pl.multiple_of((zz * 2 + yy) * rows, 16)
                    at_cols = pl.ds(pl.multiple_of(core * cols, 128), cols)
                    target = outs[0].at[pl.ds(first, rows), at_cols]
                else:
                    first = pl.multiple_of((zz * 4 + yy * 2 + core) * rows, 16)
                    target = outs[0].at[pl.ds(first, rows), :]
                store = pltpu.make_async_copy(held.at[j], target, left.at[j])
                store.start()
                waits.append((None, store))
                continue
            at_rows = pl.ds(pl.multiple_of((zz * 2 + yy) * rows, 16), rows)
            at_cols = pl.ds(pl.multiple_of(core * (2 * D), 128), D)
            store = pltpu.make_async_copy(
                held.at[j, :, pl.ds(0, D)], outs[0].at[at_rows, at_cols], left.at[j]
            )
            store.start()
            waits.append((None, store))
            for which, target in ((0, outs[0].at[at_rows, pl.ds(D, D)]), (1, outs[1].at[at_rows, :])):
                store = pltpu.make_async_copy(held.at[j, :, pl.ds(D, D)], target, left.at[16 + j])
                pl.when(core == which)(store.start)
                waits.append((core == which, store))
        for needed, store in waits:
            if needed is None:
                store.wait()
            else:
                pl.when(needed)(store.wait)

    out = pl.pallas_call(
        kernel,
        out_shape=[jax.ShapeDtypeStruct(v, pieces[0].dtype) for v in shapes],
        in_specs=[pl.BlockSpec(memory_space=pltpu.SMEM)]
        + [pl.BlockSpec(memory_space=pl.ANY)] * 16,
        out_specs=[pl.BlockSpec(memory_space=pl.ANY)] * len(shapes),
        scratch_shapes=[
            pltpu.VMEM((16, rows, cols), pieces[0].dtype),
            pltpu.SemaphoreType.DMA((16,)),
            pltpu.SemaphoreType.DMA((32,)),
        ],
        compiler_params=pltpu.CompilerParams(vmem_limit_bytes=16 * 2**20),
        cost_estimate=pl.CostEstimate(
            flops=0, bytes_accessed=64 * rows * cols, transcendentals=0
        ),
        name="assemble",
    )(jnp.stack([*place(), lax.axis_index("seq").astype(jnp.int32)]), *pieces)
    return out if split else out[0]


def take(v, axis, index):
    return lax.dynamic_index_in_dim(v, index, axis, keepdims=False)


def added(left, right):
    return b16(f32(left) + f32(right))


def by_side(side, own, other):
    own, other = f32(own), f32(other)
    return jnp.where(
        side == 0, jnp.concatenate([own, other], 0), jnp.concatenate([other, own], 0)
    )


def vector_step(value, bit, axis="batch"):
    if axis == "seq":
        return value + swap_seq(value)
    return value + lax.ppermute(value, "batch", [(b, b ^ bit) for b in range(16)])


def z_scatter(blocks):
    groups = [[q + 4 * z for z in range(4)] for q in range(4)]
    return lax.psum_scatter(
        blocks, "batch", scatter_dimension=0, tiled=True, axis_index_groups=groups
    )


def sc_sum(grad):
    return lax.psum_scatter(grad, "batch", scatter_dimension=0, tiled=True)


def per_device_pair(
    tokens,
    skip_parts,
    lengths,
    cotangent,
    skip_w,
    qkv_w,
    proj_w,
    fc1_w,
    fc2_w,
    skip_bias,
    ln1_gain,
    ln1_bias,
    proj_bias,
    ln2_gain,
    ln2_bias,
    fc1_bias,
    fc2_bias,
):
    count = tokens.shape[1]
    side = lax.axis_index("seq").astype(jnp.int32)
    index = side.reshape(1)
    at = jnp.stack([*place(), side])
    shared = jnp.where(side == 0, 256, 0)
    live = (
        (side * count + lax.broadcasted_iota(jnp.int32, (count, 1), 0)) < jnp.sum(lengths)
    ).astype(jnp.float32)

    parts = skip_parts.reshape(2, count, D)
    skip_far = swap_seq(take(parts, 0, 1 - side))
    tok_flat = tokens.reshape(count, D)

    q0 = core_pair(jnp.concatenate([qkv_w, proj_w], 1))
    s0 = skip_w
    s1, t0, s0c = next_z(s0), swap_y(s0), swap_core(s0)
    s1, t0 = tied(s1, t0)
    s2, t1 = next_z(s1), swap_y(s1)
    s2, t1, s1, q0, t0, s0c = tied(s2, t1, s1, q0, t0, s0c)
    s3, t2, q1 = next_z(s2), swap_y(s2), next_z(q0)
    s1c, t0c = swap_core(s1), swap_core(t0)
    s3, t2, s2, q0, t1, s1c, t0c = tied(s3, t2, s2, q0, t1, s1c, t0c)
    t3, r0 = swap_y(s3), swap_y(q0)
    s2c, s3c, t1c, t2c = swap_core(s2), swap_core(s3), swap_core(t1), swap_core(t2)
    s2c, s3c, t1c, t2c, t3, skip_far = tied(s2c, s3c, t1c, t2c, t3, skip_far)
    w_skip = assemble(
        [s0, s1, s2, s3, t0, t1, t2, t3, s0c, s1c, s2c, s3c, t0c, t1c, t2c, swap_core(t3)], "rows"
    )
    r0, q1, w_skip, q0 = tied(r0, q1, w_skip, q0)
    q2, r1 = next_z(q1), swap_y(q1)
    skip_flat = b16(f32(take(parts, 0, side)) + f32(skip_far))
    h_zero = fwd_dot(tok_flat, w_skip[:D]) + fwd_dot(skip_flat, w_skip[D:]) + skip_bias
    normed_one, ln1_back = jax.vjp(layer_norm, h_zero, ln1_gain, ln1_bias)
    act_one = b16(normed_one)
    act_send = lax.dynamic_slice(act_one, (shared, 0), (REM, D))
    u0 = core_pair(fc1_w)
    q2, r1, act_one, act_send, u0, q1 = tied(q2, r1, act_one, act_send, u0, q1)
    act_far = swap_seq(act_send)
    q3, r2 = next_z(q2), swap_y(q2)
    q0c, q1c, r0c = swap_core(q0), swap_core(q1), swap_core(r0)
    q3, r2, u0, q2, q0c, q1c, r0c, r1 = tied(q3, r2, u0, q2, q0c, q1c, r0c, r1)
    r3, u1 = swap_y(q3), next_z(u0)
    q2c, q3c, r1c, r2c = swap_core(q2), swap_core(q3), swap_core(r1), swap_core(r2)
    r3, u1, q3, q2c, q3c, r1c, r2c = tied(r3, u1, q3, q2c, q3c, r1c, r2c)
    u2, v0 = next_z(u1), swap_y(u0)
    w_qkv, w_proj = assemble(
        [q0, q1, q2, q3, r0, r1, r2, r3, q0c, q1c, q2c, q3c, r0c, r1c, r2c, swap_core(r3)], "split"
    )
    u2, v0, w_qkv, w_proj, u1, u0, act_far = tied(u2, v0, w_qkv, w_proj, u1, u0, act_far)
    u3, v1 = next_z(u2), swap_y(u1)
    u0c, u1c, v0c = swap_core(u0), swap_core(u1), swap_core(v0)
    qkv = b16(fwd_dot(act_one, w_qkv))
    kv_far = b16(fwd_dot(act_far, w_qkv[:, D:]))
    u3, v1, u2, u0c, u1c, v0c, qkv, kv_far, fc2_w = tied(
        u3, v1, u2, u0c, u1c, v0c, qkv, kv_far, fc2_w
    )
    w_down = lax.all_gather(fc2_w, "batch", axis=0, tiled=True)
    v2, v3 = swap_y(u2), swap_y(u3)
    u2c, u3c, v1c = swap_core(u2), swap_core(u3), swap_core(v1)
    att, lse = attn_fwd(index, qkv, kv_far, 0, HEADS)
    v2, v3, u2c, u3c, v1c, att = tied(v2, v3, u2c, u3c, v1c, att)
    v2c, v3c = swap_core(v2), swap_core(v3)
    h_one = h_zero + fwd_dot(att, w_proj) + proj_bias
    normed_two, ln2_back = jax.vjp(layer_norm, h_one, ln2_gain, ln2_bias)
    act_two = b16(normed_two)
    w_up = assemble(
        [u0, u1, u2, u3, v0, v1, v2, v3, u0c, u1c, u2c, u3c, v0c, v1c, v2c, v3c], "ringhalves"
    )

    grad_two = f32(cotangent.reshape(count, D)) * live
    grad_low = b16(grad_two)
    gelu_low, slope, dn, dn_got = mlp_up(at, act_two, w_up, fc1_bias, grad_low)
    dn_got, gelu_low, slope, w_down = tied(dn_got, gelu_low, slope, w_down)
    dn_got = swap_core(dn_got)
    up, up_got, h_add, d_act_two, d_up_bias = mlp_back(
        at, act_two, grad_low, gelu_low, slope, w_up, w_down
    )
    dn, dn_got, up_got, d_act_two = tied(dn, dn_got, up_got, d_act_two)
    up_got = swap_core(up_got)
    dn_far = swap_seq(added(dn[1], dn_got[1]))
    dn = added(dn[0], dn_got[0])
    output = b16((h_one + h_add + fc2_bias) * live).reshape(1, count, D)
    d_h_one, d_ln2_gain, d_ln2_bias = ln2_back(d_act_two)
    d_h_one = d_h_one + grad_two
    proj_low = b16(d_h_one)
    d_proj = b16(contract_rows(att, proj_low))
    d_att = b16(back_dot(proj_low, w_proj))
    d_att, d_proj, up_got, output, dn = tied(d_att, d_proj, up_got, output, dn)
    proj_part = sc_sum(d_proj)
    up_far = swap_y(added(up[1], up_got[1]))
    up = added(up[0], up_got[0])
    pick = (
        lax.broadcasted_iota(jnp.int32, (D, HEADS), 0) // HD
        == lax.broadcasted_iota(jnp.int32, (D, HEADS), 1)
    ).astype(jnp.float32)
    row_dot = lax.dot_general(
        pick, f32(d_att) * f32(att), (((0,), (1,)), ((), ())), precision=lax.Precision.HIGHEST
    )
    lse = lse[:, :HEADS].T
    d_qkv, d_far = attn_bwd(index, qkv, kv_far, d_att, lse, row_dot, 0, HEADS)
    far = b16(back_dot(d_far, w_qkv[:, D:]))
    far, d_qkv, d_far, dn, dn_far, up, up_far, proj_part = tied(
        far, d_qkv, d_far, dn, dn_far, up, up_far, proj_part
    )
    up = added(up, up_far)
    dn_send = [added(dn[1, 0:2], dn_far[1, 0:2]), added(dn[1, 2:4], dn_far[1, 2:4])]
    dn = added(dn[0], dn_far[0])
    far, d_qkv, d_far, dn, dn_send, up = tied(far, d_qkv, d_far, dn, dn_send, up)
    up_part = z_scatter(up.reshape(4 * 72, 4 * D))
    low_far = swap_seq(far[: REM // 2])
    dn_low = swap_y(dn_send[0])
    q, q_got = qkv_grad(at, act_one, act_far, d_qkv, d_far)
    d_qkv, q, q_got, low_far, dn_low, far = tied(d_qkv, q, q_got, low_far, dn_low, far)
    q_got = swap_core(q_got)
    high_far = swap_seq(far[REM // 2 :])
    dn_high = swap_y(dn_send[1])
    d_act_one = back_dot(d_qkv, w_qkv)
    q_got, d_act_one, high_far, dn_high = tied(q_got, d_act_one, high_far, dn_high)
    far = f32(jnp.concatenate([low_far, high_far], 0))
    here = lax.dynamic_slice(d_act_one, (shared, 0), (REM, D))
    d_act_one = lax.dynamic_update_slice(d_act_one, here + far, (shared, 0))
    q_send = [added(q[1, i], q_got[1, i]) for i in range(4)]
    q_y = {i: swap_y(q_send[i]) for i in (3, 2)}
    q = added(q[0], q_got[0])
    dn_part = z_scatter(added(dn, jnp.concatenate([dn_low, dn_high], 0)).reshape(4 * 144, D))
    d_h_zero, d_ln1_gain, d_ln1_bias = ln1_back(d_act_one)
    d_h_zero = d_h_zero + d_h_one
    zero_low = b16(d_h_zero)
    k, k_got = skip_back(at, tok_flat, skip_flat, zero_low)

    def onward(mine, got, so_far):
        return next_z(b16(f32(mine) + f32(got) + f32(so_far)))

    sums = jnp.concatenate(
        [
            jnp.sum(d_h_zero, axis=0),
            d_ln1_gain,
            d_ln1_bias,
            jnp.sum(d_h_one, axis=0),
            d_ln2_gain,
            d_ln2_bias,
            d_up_bias[0],
            jnp.sum(grad_two, axis=0),
        ]
    ).reshape(-1, 128)
    q_y[3], q_y[2], q, q_send, k, k_got, zero_low, sums = tied(
        q_y[3], q_y[2], q, q_send, k, k_got, zero_low, sums
    )
    k_got = swap_core(k_got)
    q_next = next_z(added(q[3], q_y[3]))
    q_y[1], q_y[0] = swap_y(q_send[1]), swap_y(q_send[0])
    d_tokens = back_dot(zero_low, w_skip[:D]).reshape(1, count, D)
    sums = vector_step(sums, 1)
    q_next, q_y, k, k_got, sums, zero_low, d_tokens = tied(
        q_next, q_y, k, k_got, sums, zero_low, d_tokens
    )
    q_next = onward(q[2], q_y[2], q_next)
    k_send = [added(k[1, i], k_got[1, i]) for i in range(4)]
    k_y = {i: swap_y(k_send[i]) for i in (3, 2)}
    k = added(k[0], k_got[0])
    sums = vector_step(sums, 0, "seq")
    d_skip = back_dot(zero_low, w_skip[D:]).reshape(1, count, D)
    q_next, k_y, k, k_send, sums, d_skip = tied(q_next, k_y, k, k_send, sums, d_skip)
    q_next = onward(q[1], q_y[1], q_next)
    k_next = next_z(added(k[3], k_y[3]))
    k_y[1], k_y[0] = swap_y(k_send[1]), swap_y(k_send[0])
    q_next, k_next, k_y, up_part, proj_part = tied(q_next, k_next, k_y, up_part, proj_part)
    up_far = swap_seq(up_part)
    proj_far = swap_seq(proj_part)
    q_sum = b16(f32(q[0]) + f32(q_y[0]) + f32(q_next))
    q_got = swap_seq(q_sum)
    k_next = onward(k[2], k_y[2], k_next)
    sums = vector_step(sums, 2)
    q_got, k_next, k_y, sums, dn_part, proj_far, up_far = tied(
        q_got, k_next, k_y, sums, dn_part, proj_far, up_far
    )
    dn_got = swap_seq(dn_part)
    out_up = f32(up_part) + f32(up_far)
    out_proj = f32(proj_part) + f32(proj_far)
    out_qkv = f32(q_sum) + f32(q_got)
    k_next = onward(k[1], k_y[1], k_next)
    k_next, k_y, sums, dn_got = tied(k_next, k_y, sums, dn_got)
    out_down = by_side(side, dn_part, dn_got)
    k_sum = b16(f32(k[0]) + f32(k_y[0]) + f32(k_next))
    out_skip = f32(k_sum) + f32(swap_seq(k_sum))
    sums = vector_step(vector_step(sums, 4), 8).reshape(-1)
    starts = [0, D, 2 * D, 3 * D, 4 * D, 5 * D, 6 * D, 10 * D, 11 * D]
    sums = [sums[a:b] for a, b in zip(starts, starts[1:])]
    grads = (out_skip, out_qkv, out_proj, out_up, out_down)
    return (output, d_tokens, d_skip, *grads, *sums)


def solution(mesh):
    in_specs = (
        P("batch", "seq", None),
        P("seq", "batch", None, None),
        P("batch", None),
        P("batch", "seq", None),
        *(P("batch", None),) * 5,
        *(P(),) * 8,
    )
    out_specs = (*(P("batch", "seq", None),) * 3, *(P("batch", None),) * 5, *(P(),) * 8)
    pair = mesh.shape["batch"] == ROWS and mesh.shape["seq"] == 2
    return jax.shard_map(
        per_device_pair if pair else per_device,
        mesh=mesh,
        in_specs=in_specs,
        out_specs=out_specs,
        check_vma=False,

    )
```

```python
import math

import jax
import jax.numpy as jnp
from jax import lax
from jax.experimental import pallas as pl
from jax.experimental.pallas import tpu as pltpu
from jax.sharding import PartitionSpec as P

HEADS = 16
HD = 72
D = 1152
ROWS = 16
EPS = 1e-05

SCALE = HD**-0.5
C2 = SCALE * math.log2(math.e)
REM = 576
TILES = {
    0: [
        (256, 576, 258, 832, [(False, 256, 576, 258, 832), (True, 0, 464, 0, 452)]),
        (0, 272, 0, 258, [(False, 0, 272, 0, 258)]),
    ],
    1: [
        (0, 464, 0, 452, [(False, 0, 464, 0, 452), (True, 0, 576, 2, 576)]),
        (448, 272, 452, 710, [(False, 448, 272, 452, 710)]),
        (704, 128, 710, 832, [(False, 704, 128, 710, 832)]),
    ],
}
NT = (((1,), (1,)), ((), ()))


def dot(a, b, dims=(((1,), (0,)), ((), ()))):
    return lax.dot_general(a, b, dims, preferred_element_type=jnp.float32)


def split(n, step):
    return [(i, min(step, n - i)) for i in range(0, n, step)]


def full(shape):
    return pl.BlockSpec(shape, lambda h, s: (0,) * len(shape), pipeline_mode=pl.Buffered(1))


def pair_window(pair):
    tile = (2 * HD * pair) // 128
    first = 2 * HD * pair - 128 * tile
    lane = lax.broadcasted_iota(jnp.int32, (1, 256), 1)
    left = (lane >= first) & (lane < first + HD)
    right = (lane >= first + HD) & (lane < first + 2 * HD)
    base = pl.multiple_of(tile * 128, 128)

    def at(offset, row, count):
        return slice(row, row + count), pl.ds(pl.multiple_of(base + offset, 128), 256)

    return at, left, right


def stacked(value, left, right):
    zero = jnp.zeros_like(value)
    return jnp.concatenate([jnp.where(left, value, zero), jnp.where(right, value, zero)], 0)


def fwd_kernel(s_ref, qkv_ref, kvr_ref, o_ref, l_ref, *, qstep):
    pair = pl.program_id(0)

    @pl.when(pair == 0)
    def _():
        o_ref[...] = jnp.zeros_like(o_ref)
        l_ref[...] = jnp.zeros_like(l_ref)

    at, left, right = pair_window(pair)

    def chunk(r0, n, qv0, qv1, keys):
        q2 = stacked(qkv_ref[at(0, r0, n)], left, right)
        scores = []
        for far, k0, kc, kv0, kv1 in keys:
            k = kvr_ref[at(0, k0, kc)] if far else qkv_ref[at(D, k0, kc)]
            s = dot(q2, k, NT)
            if kv0 > k0 or kv1 < k0 + kc:
                kp = k0 + lax.broadcasted_iota(jnp.int32, (1, kc), 1)
                s = jnp.where((kp >= kv0) & (kp < kv1), s, -1e30)
            scores.append(s)
        top = jnp.max(scores[0], axis=1, keepdims=True)
        for s in scores[1:]:
            top = jnp.maximum(top, jnp.max(s, axis=1, keepdims=True))
        top = top * C2
        total, out = 0.0, 0.0
        for s, (far, k0, kc, _, _) in zip(scores, keys):
            p = jnp.exp2(s * C2 - top)
            total = total + jnp.sum(p, axis=1, keepdims=True)
            v = kvr_ref[at(D, k0, kc)] if far else qkv_ref[at(2 * D, k0, kc)]
            out = out + dot(p.astype(jnp.bfloat16), v)
        out = out * (1.0 / total)
        lse = top + jnp.log2(total)
        out = jnp.where(left, out[:n], out[n:]).astype(jnp.bfloat16)
        head = lax.broadcasted_iota(jnp.int32, (1, 128), 1) - 2 * pair
        lse = jnp.where(head == 0, lse[:n], lse[n:])
        keep, keep_l = left | right, (head == 0) | (head == 1)
        if r0 < qv0 or r0 + n > qv1:
            row = r0 + lax.broadcasted_iota(jnp.int32, (n, 1), 0)
            valid = (row >= qv0) & (row < qv1)
            keep, keep_l = keep & valid, keep_l & valid
        o_ref[at(0, r0, n)] = jnp.where(keep, out, o_ref[at(0, r0, n)])
        l_ref[r0 : r0 + n, :] = jnp.where(keep_l, lse, l_ref[r0 : r0 + n, :])

    for side in (0, 1):

        @pl.when(s_ref[0] == side)
        def _():
            for q0, nq, qv0, qv1, keys in TILES[side]:
                for a, n in split(nq, qstep):
                    chunk(q0 + a, n, qv0, qv1, keys)


def attn_fwd(sidx, qkv, kvr, qstep=288):
    return pl.pallas_call(
        lambda *r: fwd_kernel(*r, qstep=qstep),
        out_shape=(
            jax.ShapeDtypeStruct((832, D), jnp.bfloat16),
            jax.ShapeDtypeStruct((832, 128), jnp.float32),
        ),
        grid_spec=pltpu.PrefetchScalarGridSpec(
            num_scalar_prefetch=1,
            grid=(HEADS // 2,),
            in_specs=[full((832, 3 * D)), full((REM, 2 * D))],
            out_specs=(full((832, D)), full((832, 128))),
        ),
        compiler_params=pltpu.CompilerParams(vmem_limit_bytes=60 * 2**20),
        cost_estimate=pl.CostEstimate(
            flops=20 * 10**9, bytes_accessed=12 * 2**20, transcendentals=0
        ),
        name="attn_fwd",
    )(sidx, qkv, kvr)


def bwd_kernel(s_ref, qkv_ref, kvr_ref, do_ref, lt_ref, dt_ref, dqkv_ref, dkvr_ref, *, kstep):
    pair = pl.program_id(0)

    @pl.when(pair == 0)
    def _():
        dqkv_ref[...] = jnp.zeros_like(dqkv_ref)
        dkvr_ref[...] = jnp.zeros_like(dkvr_ref)

    at, left, right = pair_window(pair)

    def tile(q0, nq, qv0, qv1, keys):
        q2 = stacked(qkv_ref[at(0, q0, nq)], left, right)
        do2 = stacked(do_ref[at(0, q0, nq)], left, right)

        def both(ref, mask):
            rows = []
            for h in (0, 1):
                row = ref[pl.ds(2 * pair + h, 1), :][:, q0 : q0 + nq]
                if mask and (qv0 > q0 or qv1 < q0 + nq):
                    qp = q0 + lax.broadcasted_iota(jnp.int32, (1, nq), 1)
                    row = jnp.where((qp >= qv0) & (qp < qv1), row, 1e30)
                rows.append(row)
            return jnp.concatenate(rows, 1)

        lse, row_dot = both(lt_ref, True), both(dt_ref, False)
        dqt = 0.0
        for far, first, count, kv0, kv1 in keys:
            for a, kc in split(count, kstep):
                k0 = first + a
                k = kvr_ref[at(0, k0, kc)] if far else qkv_ref[at(D, k0, kc)]
                v = kvr_ref[at(D, k0, kc)] if far else qkv_ref[at(2 * D, k0, kc)]
                p = jnp.exp2(dot(k, q2, NT) * C2 - lse)
                if kv0 > k0 or kv1 < k0 + kc:
                    kp = k0 + lax.broadcasted_iota(jnp.int32, (kc, 1), 0)
                    p = jnp.where((kp >= kv0) & (kp < kv1), p, 0.0)
                ds = (p * (dot(v, do2, NT) - row_dot)).astype(jnp.bfloat16)
                dv = dot(p.astype(jnp.bfloat16), do2).astype(jnp.bfloat16)
                dk = (dot(ds, q2) * SCALE).astype(jnp.bfloat16)
                if far:
                    dkvr_ref[at(0, k0, kc)] += dk
                    dkvr_ref[at(D, k0, kc)] += dv
                else:
                    dqkv_ref[at(D, k0, kc)] += dk
                    dqkv_ref[at(2 * D, k0, kc)] += dv
                dqt = dqt + dot(k.T, ds)
        dq = (dqt * SCALE).T
        dq = jnp.where(left, dq[:nq], jnp.where(right, dq[nq:], 0.0)).astype(jnp.bfloat16)
        dqkv_ref[at(0, q0, nq)] += dq

    for side in (0, 1):

        @pl.when(s_ref[0] == side)
        def _():
            for parts in TILES[side]:
                tile(*parts)


def attn_bwd(sidx, qkv, kvr, do, lt, dt, kstep=1024):
    return pl.pallas_call(
        lambda *r: bwd_kernel(*r, kstep=kstep),
        out_shape=(
            jax.ShapeDtypeStruct((832, 3 * D), jnp.bfloat16),
            jax.ShapeDtypeStruct((REM, 2 * D), jnp.bfloat16),
        ),
        grid_spec=pltpu.PrefetchScalarGridSpec(
            num_scalar_prefetch=1,
            grid=(HEADS // 2,),
            in_specs=[
                full((832, 3 * D)),
                full((REM, 2 * D)),
                full((832, D)),
                full((16, 832)),
                full((16, 832)),
            ],
            out_specs=(full((832, 3 * D)), full((REM, 2 * D))),
        ),
        compiler_params=pltpu.CompilerParams(vmem_limit_bytes=60 * 2**20),
        cost_estimate=pl.CostEstimate(
            flops=40 * 10**9, bytes_accessed=20 * 2**20, transcendentals=0
        ),
        name="attn_bwd",
    )(sidx, qkv, kvr, do, lt, dt)


ERFC = (0.5 * 1.061405429, -0.5 * 1.453152027, 0.5 * 1.421413741, -0.5 * 0.284496736, 0.5 * 0.254829592)


def normal_cdf(u):
    expo = jnp.exp2(u * u * (-0.5 * math.log2(math.e)))
    below = 1.0 + (0.3275911 * math.sqrt(0.5)) * jnp.abs(u)
    step = pltpu.reciprocal(below, approx=True)
    step = step * (2.0 - below * step)
    tail = ERFC[0]
    for term in ERFC[1:]:
        tail = tail * step + term
    tail = tail * step * expo
    return jnp.where(u < 0.0, tail, 1.0 - tail), expo


def mlp_up(at, act, weight, bias, grad, tile=D, chunks=4):
    rows, width = act.shape[0], weight.shape[1]
    steps = width // tile
    size = rows // chunks

    def kernel(at, a_ref, w_ref, b_ref, e_ref, g_ref, d_ref, mine, other, held):
        t = pl.program_id(0)

        def forward():
            for i in range(chunks):
                part = slice(i * size, (i + 1) * size)
                u = dot(a_ref[part], w_ref[...]) + b_ref[...]
                phi, expo = normal_cdf(u)
                g = (u * phi).astype(jnp.bfloat16)
                g_ref[part] = g
                d_ref[part] = (phi + u * expo * (1.0 / math.sqrt(2.0 * math.pi))).astype(jnp.bfloat16)

        def keep():
            held[...] = g_ref[...].T

        def back():
            for yy in (0, 1):
                both = dot(held[yy * 576 : yy * 576 + 576], e_ref[...])
                low, high = both[:288], both[288:]
                yrel = yy + at[1] - 2 * yy * at[1]
                for ref, value in (
                    (mine, jnp.where(at[2] == 0, low, high)),
                    (other, jnp.where(at[2] == 0, high, low)),
                ):
                    value = value.astype(jnp.bfloat16)
                    ref[at[3], yrel, 0] = value[:144]
                    ref[1 - at[3], yrel, 0] = value[144:]

        @pl.when(t == 0)
        def _():
            forward()
            keep()

        @pl.when((t > 0) & (t < steps))
        def _():
            back()
            forward()
            keep()

        @pl.when(t == steps)
        def _():
            back()

    out = jax.ShapeDtypeStruct((rows, width), jnp.bfloat16)
    split = jax.ShapeDtypeStruct((2, 2, 4, 144, D), jnp.bfloat16)

    def now(t):
        return jnp.minimum(t, steps - 1)

    whole = pl.BlockSpec((rows, D), lambda t, at: (0, 0), pipeline_mode=pl.Buffered(1))
    by_column = pl.BlockSpec((rows, tile), lambda t, at: (0, now(t)))
    split_spec = pl.BlockSpec((2, 2, 1, 144, D), lambda t, at: (0, 0, jnp.maximum(t - 1, 0), 0, 0))
    return pl.pallas_call(
        kernel,
        out_shape=(out, out, split, split),
        grid_spec=pltpu.PrefetchScalarGridSpec(
            num_scalar_prefetch=1,
            grid=(steps + 1,),
            in_specs=[
                whole,
                pl.BlockSpec((D, tile), lambda t, at: (0, now(t))),
                pl.BlockSpec((1, tile), lambda t, at: (0, now(t))),
                whole,
            ],
            out_specs=(by_column, by_column, split_spec, split_spec),
            scratch_shapes=[pltpu.VMEM((tile, rows), jnp.bfloat16)],
        ),
        compiler_params=pltpu.CompilerParams(vmem_limit_bytes=60 * 2**20),
        cost_estimate=pl.CostEstimate(
            flops=4 * rows * D * width,
            bytes_accessed=5 * D * width,
            transcendentals=rows * width,
        ),
        name="mlp_up",
    )(at, act, weight, bias.reshape(1, width), grad)


def ordered_transpose(at, value, held, ring=True):
    held[...] = value.astype(jnp.float32).T.reshape(held.shape)
    blocks = []
    for crel in (0, 1):
        for yrel in (0, 1):
            for zrel in range(4):
                zz = lax.rem(at[0] + zrel, 4) if ring else zrel
                yy = at[1] + yrel - 2 * at[1] * yrel
                cc = at[2] + crel - 2 * at[2] * crel
                blocks.append(held[zz * 4 + yy * 2 + cc])
    return jnp.concatenate(blocks, 0).astype(jnp.bfloat16)


def mlp_back(at, act, grad, gelu, slope, w_up, w_down, halves=1, tile=768):
    rows, width = gelu.shape
    half = rows // halves

    def kernel(at, a_ref, e_ref, g_ref, s_ref, wu_ref, wd_ref, *refs):
        mine, other, h_ref, c_ref, b_ref, a_t, du_ref, held = refs

        @pl.when(pl.program_id(0) == 0)
        def _():
            a_t[...] = ordered_transpose(at, a_ref[...], held, ring=False)
            h_ref[...] = jnp.zeros_like(h_ref)
            c_ref[...] = jnp.zeros_like(c_ref)

        bias = None
        for i in range(halves):
            part = slice(i * half, (i + 1) * half)
            du = dot(e_ref[part], wd_ref[...], NT) * s_ref[part].astype(jnp.float32)
            total = jnp.sum(du, axis=0, keepdims=True)
            bias = total if bias is None else bias + total
            du = du.astype(jnp.bfloat16)
            du_ref[part] = du
            h_ref[part] += dot(g_ref[part], wd_ref[...])
            c_ref[part] += dot(du, wu_ref[...], NT)
        b_ref[...] = bias
        for i, ref in ((0, mine), (1, other)):
            both = dot(a_t[i * 576 : i * 576 + 576], du_ref[...])
            for j in range(8):
                ref[j // 4, j % 4] = both[j * 72 : j * 72 + 72].astype(jnp.bfloat16)

    once = pl.Buffered(1)
    whole = jax.ShapeDtypeStruct((rows, D), jnp.float32)
    split = jax.ShapeDtypeStruct((2, 4, 72, width), jnp.bfloat16)
    split_spec = pl.BlockSpec((2, 4, 72, tile), lambda t, at: (0, 0, 0, t))
    whole_spec = pl.BlockSpec((rows, D), lambda t, at: (0, 0), pipeline_mode=once)
    by_column = pl.BlockSpec((rows, tile), lambda t, at: (0, t))
    weight_column = pl.BlockSpec((D, tile), lambda t, at: (0, t))
    return pl.pallas_call(
        kernel,
        out_shape=(
            split,
            split,
            whole,
            whole,
            jax.ShapeDtypeStruct((1, width), jnp.float32),
        ),
        grid_spec=pltpu.PrefetchScalarGridSpec(
            num_scalar_prefetch=1,
            grid=(width // tile,),
            in_specs=[
                whole_spec,
                whole_spec,
                by_column,
                by_column,
                weight_column,
                pl.BlockSpec((tile, D), lambda t, at: (t, 0)),
            ],
            out_specs=(
                split_spec,
                split_spec,
                whole_spec,
                whole_spec,
                pl.BlockSpec((1, tile), lambda t, at: (0, t)),
            ),
            scratch_shapes=[
                pltpu.VMEM((D, rows), jnp.bfloat16),
                pltpu.VMEM((rows, tile), jnp.bfloat16),
                pltpu.VMEM((16, 72, rows), jnp.float32),
            ],
        ),
        compiler_params=pltpu.CompilerParams(vmem_limit_bytes=62 * 2**20),
        cost_estimate=pl.CostEstimate(
            flops=8 * rows * D * width, bytes_accessed=50 * 2**20, transcendentals=0
        ),
        name="mlp_back",
    )(at, act, grad, gelu, slope, w_up, w_down)


def qkv_grad(at, act, act_far, grad, grad_far):
    rows, far = act.shape[0], act_far.shape[0]

    def kernel(at, a_ref, f_ref, g_ref, h_ref, mine, other, a_t, f_t, held, held_far):
        t = pl.program_id(0)

        @pl.when(t == 0)
        def _():
            a_t[...] = ordered_transpose(at, a_ref[...], held)
            f_t[...] = ordered_transpose(at, f_ref[...], held_far)

        away = jnp.where(t > 0, h_ref[...], jnp.zeros_like(h_ref))
        for i, ref in ((0, mine), (1, other)):
            part = slice(i * 576, (i + 1) * 576)
            both = dot(a_t[part], g_ref[...]) + dot(f_t[part], away)
            for j in range(8):
                ref[j // 4, j % 4] = both[j * 72 : j * 72 + 72].astype(jnp.bfloat16)

    once = pl.Buffered(1)
    split = jax.ShapeDtypeStruct((2, 4, 72, 3 * D), jnp.bfloat16)
    split_spec = pl.BlockSpec((2, 4, 72, D), lambda t, at: (0, 0, 0, t))
    return pl.pallas_call(
        kernel,
        out_shape=(split, split),
        grid_spec=pltpu.PrefetchScalarGridSpec(
            num_scalar_prefetch=1,
            grid=(3,),
            in_specs=[
                pl.BlockSpec((rows, D), lambda t, at: (0, 0), pipeline_mode=once),
                pl.BlockSpec((far, D), lambda t, at: (0, 0), pipeline_mode=once),
                pl.BlockSpec((rows, D), lambda t, at: (0, t)),
                pl.BlockSpec((far, D), lambda t, at: (0, jnp.maximum(t - 1, 0))),
            ],
            out_specs=(split_spec, split_spec),
            scratch_shapes=[
                pltpu.VMEM((D, rows), jnp.bfloat16),
                pltpu.VMEM((D, far), jnp.bfloat16),
                pltpu.VMEM((16, 72, rows), jnp.float32),
                pltpu.VMEM((16, 72, far), jnp.float32),
            ],
        ),
        compiler_params=pltpu.CompilerParams(vmem_limit_bytes=60 * 2**20),
        cost_estimate=pl.CostEstimate(
            flops=10 * rows * D * D, bytes_accessed=40 * 2**20, transcendentals=0
        ),
        name="qkv_grad",
    )(at, act, act_far, grad, grad_far)


def skip_back(at, tok, skip, grad):
    rows = tok.shape[0]

    def kernel(at, t_ref, s_ref, g_ref, mine, other, in_t):
        i = pl.program_id(0)

        @pl.when(i == 0)
        def _():
            in_t[0:D] = t_ref[...].T
            in_t[D:] = s_ref[...].T

        first = pl.multiple_of(lax.rem(at[0] + i, 4) * 576, 16)
        both = dot(in_t[pl.ds(first, 576)], g_ref[...])
        for yy in (0, 1):
            low, high = both[yy * 288 : yy * 288 + 144], both[yy * 288 + 144 : yy * 288 + 288]
            yrel = yy + at[1] - 2 * yy * at[1]
            mine[yrel, 0] = jnp.where(at[2] == 0, low, high).astype(jnp.bfloat16)
            other[yrel, 0] = jnp.where(at[2] == 0, high, low).astype(jnp.bfloat16)

    split = jax.ShapeDtypeStruct((2, 4, 144, D), jnp.bfloat16)
    split_spec = pl.BlockSpec((2, 1, 144, D), lambda t, at: (0, t, 0, 0))
    whole_spec = pl.BlockSpec((rows, D), lambda t, at: (0, 0), pipeline_mode=pl.Buffered(1))
    return pl.pallas_call(
        kernel,
        out_shape=(split, split),
        grid_spec=pltpu.PrefetchScalarGridSpec(
            num_scalar_prefetch=1,
            grid=(4,),
            in_specs=[whole_spec] * 3,
            out_specs=(split_spec, split_spec),
            scratch_shapes=[pltpu.VMEM((2 * D, rows), jnp.bfloat16)],
        ),
        compiler_params=pltpu.CompilerParams(vmem_limit_bytes=40 * 2**20),
        cost_estimate=pl.CostEstimate(
            flops=4 * rows * D * D, bytes_accessed=12 * 2**20, transcendentals=0
        ),
        name="skip_back",
    )(at, tok, skip, grad)


def layer_norm(hidden, gain, shift):
    centred = hidden - jnp.mean(hidden, axis=-1, keepdims=True)
    spread = jnp.mean(centred * centred, axis=-1, keepdims=True)
    return centred * lax.rsqrt(spread + EPS) * gain + shift


def exact_gelu(value):
    return jax.nn.gelu(value, approximate=False)


def segment_ids(offsets, positions):
    hits = (positions[None, :, None] >= offsets[:, None, :]).astype(jnp.int32)
    return jnp.sum(hits, axis=-1)


def fwd_dot(left, right):
    return jnp.dot(left, right, preferred_element_type=jnp.float32)


def contract_rows(left, right):
    return lax.dot_general(
        left, right, (((0,), (0,)), ((), ())), preferred_element_type=jnp.float32
    )


def back_dot(grad_rows, weight):
    return lax.dot_general(
        grad_rows, weight, (((1,), (1,)), ((), ())), preferred_element_type=jnp.float32
    )


class RowAttention:
    def __init__(self, qkv_all, offsets, row_count, local_len):
        self.row_count, self.local_len = row_count, local_len
        self.row_len = local_len * lax.axis_size("seq")
        self.offsets = offsets
        first_pos = lax.axis_index("seq") * local_len
        self.query_seg = segment_ids(offsets, first_pos + jnp.arange(local_len, dtype=jnp.int32))
        self.scale = HD ** (-0.5)
        self.queries = qkv_all[:, :D].reshape(row_count, local_len, HEADS, HD)
        keyvals = qkv_all[:, D:].reshape(row_count, local_len, 2 * D)
        self.kv = lax.all_gather(keyvals, "seq", axis=1, tiled=True)

    def block(self, first, size):
        kv = lax.dynamic_slice_in_dim(self.kv, first, size, 1)
        shape = (self.row_count, size, HEADS, HD)
        key_seg = segment_ids(self.offsets, first + jnp.arange(size, dtype=jnp.int32))
        same = self.query_seg[:, :, None, None] == key_seg[:, None, None, :]
        return kv[:, :, :D].reshape(shape), kv[:, :, D:].reshape(shape), same

    def scores(self, keys):
        return (
            jnp.einsum("rthd,rkhd->rthk", self.queries, keys, preferred_element_type=jnp.float32)
            * self.scale
        )

    def forward(self):
        keys, values, same = self.block(0, self.row_len)
        scores = jnp.where(same, self.scores(keys), -1e30)
        top = jnp.max(scores, axis=-1)
        expo = jnp.where(same, jnp.exp(scores - top[..., None]), 0.0)
        norm = jnp.sum(expo, axis=-1)
        weighted = jnp.einsum(
            "rthk,rkhd->rthd",
            expo.astype(jnp.bfloat16),
            values,
            preferred_element_type=jnp.float32,
        )
        self.attended = weighted / norm[..., None]
        self.log_total = top + jnp.log(norm)
        return self.attended.reshape(-1, D).astype(jnp.bfloat16)

    def backward(self, d_att):
        rows, length = self.row_count, self.local_len
        d_att = d_att.reshape(rows, length, HEADS, HD)
        row_dot = jnp.sum(d_att.astype(jnp.float32) * self.attended, axis=-1)
        size = math.gcd(self.row_len, 512)

        def step(index, totals):
            d_query, d_kv = totals
            keys, values, same = self.block(index * size, size)
            weights = jnp.where(same, jnp.exp(self.scores(keys) - self.log_total[..., None]), 0.0)
            d_weights = jnp.einsum(
                "rthd,rkhd->rthk", d_att, values, preferred_element_type=jnp.float32
            )
            d_scores = (weights * (d_weights - row_dot[..., None])).astype(jnp.bfloat16)
            d_query = d_query + self.scale * jnp.einsum(
                "rthk,rkhd->rthd", d_scores, keys, preferred_element_type=jnp.float32
            )
            d_key = self.scale * jnp.einsum(
                "rthk,rthd->rkhd", d_scores, self.queries, preferred_element_type=jnp.float32
            )
            d_value = jnp.einsum(
                "rthk,rthd->rkhd",
                weights.astype(jnp.bfloat16),
                d_att,
                preferred_element_type=jnp.float32,
            )
            both = jnp.concatenate(
                [d_key.reshape(rows, size, D), d_value.reshape(rows, size, D)], axis=2
            )
            return d_query, lax.dynamic_update_slice_in_dim(d_kv, both, index * size, 1)

        start = (
            jnp.zeros((rows, length, HEADS, HD), jnp.float32),
            jnp.zeros((rows, self.row_len, 2 * D), jnp.float32),
        )
        d_query, d_kv = lax.fori_loop(0, self.row_len // size, step, start)
        d_kv = lax.psum_scatter(
            d_kv.astype(jnp.bfloat16), "seq", scatter_dimension=1, tiled=True
        ).astype(jnp.float32)
        return jnp.concatenate(
            [d_query.reshape(rows * length, D), d_kv.reshape(rows * length, 2 * D)], axis=1
        ).astype(jnp.bfloat16)


def per_device(
    tokens,
    skip_parts,
    lengths,
    cotangent,
    skip_w,
    qkv_w,
    proj_w,
    fc1_w,
    fc2_w,
    skip_bias,
    ln1_gain,
    ln1_bias,
    proj_bias,
    ln2_gain,
    ln2_bias,
    fc1_bias,
    fc2_bias,
):
    row_count, local_len, features = tokens.shape
    tok_count = row_count * local_len
    offsets = jnp.cumsum(lengths, axis=1)
    first_pos = lax.axis_index("seq") * local_len
    query_seg = segment_ids(offsets, first_pos + jnp.arange(local_len, dtype=jnp.int32))
    live_mask = (query_seg < lengths.shape[1]).astype(jnp.float32).reshape(tok_count, 1)
    skip_rows = lax.psum_scatter(skip_parts[0], "seq", scatter_dimension=1, tiled=True)
    w_skip, w_qkv, w_proj, w_up, w_down = (
        lax.all_gather(w, "batch", axis=0, tiled=True)
        for w in (skip_w, qkv_w, proj_w, fc1_w, fc2_w)
    )
    tok_flat = tokens.reshape(tok_count, features)
    skip_flat = skip_rows.reshape(tok_count, features)
    h_zero = (
        fwd_dot(tok_flat, w_skip[:features]) + fwd_dot(skip_flat, w_skip[features:]) + skip_bias
    )
    normed_one, ln1_back = jax.vjp(layer_norm, h_zero, ln1_gain, ln1_bias)
    act_one = normed_one.astype(jnp.bfloat16)
    qkv_all = fwd_dot(act_one, w_qkv).astype(jnp.bfloat16)
    attention = RowAttention(qkv_all, offsets, row_count, local_len)
    att_low = attention.forward()
    h_one = h_zero + fwd_dot(att_low, w_proj) + proj_bias
    normed_two, ln2_back = jax.vjp(layer_norm, h_one, ln2_gain, ln2_bias)
    act_two = normed_two.astype(jnp.bfloat16)
    up_proj = fwd_dot(act_two, w_up) + fc1_bias
    gelu_out, gelu_back = jax.vjp(exact_gelu, up_proj)
    gelu_low = gelu_out.astype(jnp.bfloat16)
    h_two = h_one + fwd_dot(gelu_low, w_down) + fc2_bias
    output = (h_two * live_mask).astype(jnp.bfloat16).reshape(row_count, local_len, features)
    grad_two = cotangent.reshape(tok_count, features).astype(jnp.float32) * live_mask
    grad_low = grad_two.astype(jnp.bfloat16)
    d_w_down = contract_rows(gelu_low, grad_low)
    d_gelu = back_dot(grad_low, w_down)
    d_up = gelu_back(d_gelu)[0]
    up_low = d_up.astype(jnp.bfloat16)
    d_w_up = contract_rows(act_two, up_low)
    d_act_two = back_dot(up_low, w_up)
    d_h_one, d_ln2_gain, d_ln2_bias = ln2_back(d_act_two)
    d_h_one = d_h_one + grad_two
    proj_low = d_h_one.astype(jnp.bfloat16)
    d_w_proj = contract_rows(att_low, proj_low)
    d_att = back_dot(proj_low, w_proj).astype(jnp.bfloat16)
    d_qkv = attention.backward(d_att)
    d_w_qkv = contract_rows(act_one, d_qkv)
    d_act_one = back_dot(d_qkv, w_qkv)
    d_h_zero, d_ln1_gain, d_ln1_bias = ln1_back(d_act_one)
    d_h_zero = d_h_zero + d_h_one
    zero_low = d_h_zero.astype(jnp.bfloat16)
    d_w_skip = jnp.concatenate(
        [contract_rows(tok_flat, zero_low), contract_rows(skip_flat, zero_low)], axis=0
    )
    d_tokens = back_dot(zero_low, w_skip[:features]).reshape(row_count, local_len, features)
    d_skip = back_dot(zero_low, w_skip[features:]).reshape(row_count, local_len, features)
    vector_sums = lax.psum(
        (
            jnp.sum(d_h_zero, axis=0),
            d_ln1_gain,
            d_ln1_bias,
            jnp.sum(d_h_one, axis=0),
            d_ln2_gain,
            d_ln2_bias,
            jnp.sum(d_up, axis=0),
            jnp.sum(grad_two, axis=0),
        ),
        ("batch", "seq"),
    )
    weight_grads = tuple(
        lax.psum(
            lax.psum_scatter(
                grad.astype(jnp.bfloat16), "batch", scatter_dimension=0, tiled=True
            ),
            "seq",
        ).astype(jnp.float32)
        for grad in (d_w_skip, d_w_qkv, d_w_proj, d_w_up, d_w_down)
    )
    return (output, d_tokens, d_skip, *weight_grads, *vector_sums)


YSW = [(b, b ^ 2) for b in range(16)]
CSW = [(b, b ^ 1) for b in range(16)]
ZUP = [(b, (b + 4) % 16) for b in range(16)]


def swap_y(v):
    return lax.ppermute(v, "batch", YSW)


def swap_core(v):
    return lax.ppermute(v, "batch", CSW)


def next_z(v):
    return lax.ppermute(v, "batch", ZUP)


def swap_seq(v):
    return lax.ppermute(v, "seq", [(0, 1), (1, 0)])


def place():
    b = lax.axis_index("batch").astype(jnp.int32)
    return b // 4, (b // 2) % 2, b % 2


def f32(v):
    return v.astype(jnp.float32)


def b16(v):
    return v.astype(jnp.bfloat16)


def core_pair(shard):
    core = place()[2]
    half = shard.shape[1] // 2
    low, high = shard[:, :half], shard[:, half:]
    keep = jnp.where(core == 0, low, high)
    got = swap_core(jnp.where(core == 0, high, low))
    return jnp.where(
        core == 0, jnp.concatenate([keep, got], 0), jnp.concatenate([got, keep], 0)
    )


def tied(*values):
    return lax.optimization_barrier(values)


def with_core(own):
    return own + [swap_core(v) for v in own]


def assemble(pieces, kind):
    rows, cols = pieces[0].shape
    split, halves, paired = kind == "split", kind.endswith("halves"), kind == "halves"
    if split:
        shapes = [(8 * rows, 3 * D), (8 * rows, D)]
    elif halves:
        shapes = [(8 * rows, 2 * cols)]
    else:
        shapes = [(16 * rows, cols)]

    def kernel(at, *refs):
        ins, outs, (held, came, left) = refs[:16], refs[16:-3], refs[-3:]
        z, y, c, x = at[0], at[1], at[2], at[3]
        loads = [pltpu.make_async_copy(ins[j], held.at[j], came.at[j]) for j in range(16)]
        for load in loads:
            load.start()
        waits = []
        for j in range(16):
            core = c if j < 8 else 1 - c
            yy = y if j % 8 < 4 else 1 - y
            away = j % 4
            if paired and j % 8 in (4, 5):
                away = away + x - 2 * away * x
            zz = lax.rem(z - away + 4, 4)
            loads[j].wait()
            if not split:
                if halves:
                    first = pl.multiple_of((zz * 2 + yy) * rows, 16)
                    at_cols = pl.ds(pl.multiple_of(core * cols, 128), cols)
                    target = outs[0].at[pl.ds(first, rows), at_cols]
                else:
                    first = pl.multiple_of((zz * 4 + yy * 2 + core) * rows, 16)
                    target = outs[0].at[pl.ds(first, rows), :]
                store = pltpu.make_async_copy(held.at[j], target, left.at[j])
                store.start()
                waits.append((None, store))
                continue
            at_rows = pl.ds(pl.multiple_of((zz * 2 + yy) * rows, 16), rows)
            at_cols = pl.ds(pl.multiple_of(core * (2 * D), 128), D)
            store = pltpu.make_async_copy(
                held.at[j, :, pl.ds(0, D)], outs[0].at[at_rows, at_cols], left.at[j]
            )
            store.start()
            waits.append((None, store))
            for which, target in ((0, outs[0].at[at_rows, pl.ds(D, D)]), (1, outs[1].at[at_rows, :])):
                store = pltpu.make_async_copy(held.at[j, :, pl.ds(D, D)], target, left.at[16 + j])
                pl.when(core == which)(store.start)
                waits.append((core == which, store))
        for needed, store in waits:
            if needed is None:
                store.wait()
            else:
                pl.when(needed)(store.wait)

    out = pl.pallas_call(
        kernel,
        out_shape=[jax.ShapeDtypeStruct(v, pieces[0].dtype) for v in shapes],
        in_specs=[pl.BlockSpec(memory_space=pltpu.SMEM)]
        + [pl.BlockSpec(memory_space=pl.ANY)] * 16,
        out_specs=[pl.BlockSpec(memory_space=pl.ANY)] * len(shapes),
        scratch_shapes=[
            pltpu.VMEM((16, rows, cols), pieces[0].dtype),
            pltpu.SemaphoreType.DMA((16,)),
            pltpu.SemaphoreType.DMA((32,)),
        ],
        compiler_params=pltpu.CompilerParams(vmem_limit_bytes=16 * 2**20),
        cost_estimate=pl.CostEstimate(
            flops=0, bytes_accessed=64 * rows * cols, transcendentals=0
        ),
        name="assemble",
    )(jnp.stack([*place(), lax.axis_index("seq").astype(jnp.int32)]), *pieces)
    return out if split else out[0]


def take(v, axis, index):
    return lax.dynamic_index_in_dim(v, index, axis, keepdims=False)


def added(left, right):
    return b16(f32(left) + f32(right))


def by_side(side, own, other):
    own, other = f32(own), f32(other)
    return jnp.where(
        side == 0, jnp.concatenate([own, other], 0), jnp.concatenate([other, own], 0)
    )


def vector_step(value, bit, axis="batch"):
    if axis == "seq":
        return value + swap_seq(value)
    return value + lax.ppermute(value, "batch", [(b, b ^ bit) for b in range(16)])


def z_scatter(blocks):
    groups = [[q + 4 * z for z in range(4)] for q in range(4)]
    return lax.psum_scatter(
        blocks, "batch", scatter_dimension=0, tiled=True, axis_index_groups=groups
    )


def sc_sum(grad):
    return lax.psum_scatter(grad, "batch", scatter_dimension=0, tiled=True)


def per_device_pair(
    tokens,
    skip_parts,
    lengths,
    cotangent,
    skip_w,
    qkv_w,
    proj_w,
    fc1_w,
    fc2_w,
    skip_bias,
    ln1_gain,
    ln1_bias,
    proj_bias,
    ln2_gain,
    ln2_bias,
    fc1_bias,
    fc2_bias,
):
    count = tokens.shape[1]
    side = lax.axis_index("seq").astype(jnp.int32)
    index = side.reshape(1)
    at = jnp.stack([*place(), side])
    shared = jnp.where(side == 0, 256, 0)
    live = (
        (side * count + lax.broadcasted_iota(jnp.int32, (count, 1), 0)) < jnp.sum(lengths)
    ).astype(jnp.float32)

    parts = skip_parts.reshape(2, count, D)
    skip_far = swap_seq(take(parts, 0, 1 - side))
    tok_flat = tokens.reshape(count, D)

    q0 = core_pair(jnp.concatenate([qkv_w, proj_w], 1))
    s0 = skip_w
    s1, t0, s0c = next_z(s0), swap_y(s0), swap_core(s0)
    s1, t0 = tied(s1, t0)
    s2, t1 = next_z(s1), swap_y(s1)
    s2, t1, s1, q0, t0, s0c = tied(s2, t1, s1, q0, t0, s0c)
    s3, t2, q1 = next_z(s2), swap_y(s2), next_z(q0)
    s1c, t0c = swap_core(s1), swap_core(t0)
    s3, t2, s2, q0, t1, s1c, t0c = tied(s3, t2, s2, q0, t1, s1c, t0c)
    t3, r0 = swap_y(s3), swap_y(q0)
    s2c, s3c, t1c, t2c = swap_core(s2), swap_core(s3), swap_core(t1), swap_core(t2)
    s2c, s3c, t1c, t2c, t3, skip_far, q1, q0 = tied(s2c, s3c, t1c, t2c, t3, skip_far, q1, q0)
    q2, r1 = next_z(q1), swap_y(q1)
    w_skip = assemble(
        [s0, s1, s2, s3, t0, t1, t2, t3, s0c, s1c, s2c, s3c, t0c, t1c, t2c, swap_core(t3)], "rows"
    )
    skip_flat = b16(f32(take(parts, 0, side)) + f32(skip_far))
    h_zero = fwd_dot(tok_flat, w_skip[:D]) + fwd_dot(skip_flat, w_skip[D:]) + skip_bias
    normed_one, ln1_back = jax.vjp(layer_norm, h_zero, ln1_gain, ln1_bias)
    act_one = b16(normed_one)
    act_send = lax.dynamic_slice(act_one, (shared, 0), (REM, D))
    u0 = core_pair(fc1_w)
    q2, r1, r0, act_one, act_send, u0, q1 = tied(q2, r1, r0, act_one, act_send, u0, q1)
    act_far = swap_seq(act_send)
    q3, r2 = next_z(q2), swap_y(q2)
    q0c, q1c, r0c = swap_core(q0), swap_core(q1), swap_core(r0)
    q3, r2, u0, q2, q0c, q1c, r0c, r1 = tied(q3, r2, u0, q2, q0c, q1c, r0c, r1)
    r3, u1 = swap_y(q3), next_z(u0)
    q2c, q3c, r1c, r2c = swap_core(q2), swap_core(q3), swap_core(r1), swap_core(r2)
    r3, u1, q3, q2c, q3c, r1c, r2c = tied(r3, u1, q3, q2c, q3c, r1c, r2c)
    u2, v0 = next_z(u1), swap_y(u0)
    w_qkv, w_proj = assemble(
        [q0, q1, q2, q3, r0, r1, r2, r3, q0c, q1c, q2c, q3c, r0c, r1c, r2c, swap_core(r3)], "split"
    )
    u2, v0, w_qkv, w_proj, u1, u0, act_far = tied(u2, v0, w_qkv, w_proj, u1, u0, act_far)
    u3, v1 = next_z(u2), swap_y(u1)
    u0c, u1c, v0c = swap_core(u0), swap_core(u1), swap_core(v0)
    qkv = b16(fwd_dot(act_one, w_qkv))
    kv_far = b16(fwd_dot(act_far, w_qkv[:, D:]))
    u3, v1, u2, u0c, u1c, v0c, qkv, kv_far, fc2_w = tied(
        u3, v1, u2, u0c, u1c, v0c, qkv, kv_far, fc2_w
    )
    w_down = lax.all_gather(fc2_w, "batch", axis=0, tiled=True)
    v2, v3 = swap_y(u2), swap_y(u3)
    u2c, u3c, v1c = swap_core(u2), swap_core(u3), swap_core(v1)
    att, lse = attn_fwd(index, qkv, kv_far)
    v2, v3, u2c, u3c, v1c, att = tied(v2, v3, u2c, u3c, v1c, att)
    v2c, v3c = swap_core(v2), swap_core(v3)
    h_one = h_zero + fwd_dot(att, w_proj) + proj_bias
    normed_two, ln2_back = jax.vjp(layer_norm, h_one, ln2_gain, ln2_bias)
    act_two = b16(normed_two)
    w_up = assemble(
        [u0, u1, u2, u3, v0, v1, v2, v3, u0c, u1c, u2c, u3c, v0c, v1c, v2c, v3c], "ringhalves"
    )

    grad_two = f32(cotangent.reshape(count, D)) * live
    grad_low = b16(grad_two)
    gelu_low, slope, dn, dn_got = mlp_up(at, act_two, w_up, fc1_bias, grad_low)
    dn_got, gelu_low, slope, w_down = tied(dn_got, gelu_low, slope, w_down)
    dn_got = swap_core(dn_got)
    up, up_got, h_add, d_act_two, d_up_bias = mlp_back(
        at, act_two, grad_low, gelu_low, slope, w_up, w_down
    )
    dn, dn_got, up_got, d_act_two = tied(dn, dn_got, up_got, d_act_two)
    up_got = swap_core(up_got)
    dn_far = swap_seq(added(dn[1], dn_got[1]))
    dn = added(dn[0], dn_got[0])
    output = b16((h_one + h_add + fc2_bias) * live).reshape(1, count, D)
    d_h_one, d_ln2_gain, d_ln2_bias = ln2_back(d_act_two)
    d_h_one = d_h_one + grad_two
    proj_low = b16(d_h_one)
    up_got, proj_low, dn = tied(up_got, proj_low, dn)
    up_far = swap_y(added(up[1], up_got[1]))
    up = added(up[0], up_got[0])
    d_proj = b16(contract_rows(att, proj_low))
    d_att = b16(back_dot(proj_low, w_proj))
    d_att, d_proj, output, up = tied(d_att, d_proj, output, up)
    proj_part = sc_sum(d_proj)
    pick = (
        lax.broadcasted_iota(jnp.int32, (D, HEADS), 0) // HD
        == lax.broadcasted_iota(jnp.int32, (D, HEADS), 1)
    ).astype(jnp.float32)
    row_dot = lax.dot_general(
        pick, f32(d_att) * f32(att), (((0,), (1,)), ((), ())), precision=lax.Precision.HIGHEST
    )
    lse = lse[:, :HEADS].T
    d_qkv, d_far = attn_bwd(index, qkv, kv_far, d_att, lse, row_dot)
    far = b16(back_dot(d_far, w_qkv[:, D:]))
    far, d_qkv, d_far, dn, dn_far, up, up_far, proj_part = tied(
        far, d_qkv, d_far, dn, dn_far, up, up_far, proj_part
    )
    up = added(up, up_far)
    dn_send = [added(dn[1, 0:2], dn_far[1, 0:2]), added(dn[1, 2:4], dn_far[1, 2:4])]
    dn = added(dn[0], dn_far[0])
    far, d_qkv, d_far, dn, dn_send, up = tied(far, d_qkv, d_far, dn, dn_send, up)
    up_part = z_scatter(up.reshape(4 * 72, 4 * D))
    low_far = swap_seq(far[: REM // 2])
    dn_low = swap_y(dn_send[0])
    q, q_got = qkv_grad(at, act_one, act_far, d_qkv, d_far)
    d_qkv, q, q_got, low_far, dn_low, far = tied(d_qkv, q, q_got, low_far, dn_low, far)
    q_got = swap_core(q_got)
    high_far = swap_seq(far[REM // 2 :])
    dn_high = swap_y(dn_send[1])
    d_act_one = back_dot(d_qkv, w_qkv)
    q_got, d_act_one, high_far, dn_high = tied(q_got, d_act_one, high_far, dn_high)
    far = f32(jnp.concatenate([low_far, high_far], 0))
    here = lax.dynamic_slice(d_act_one, (shared, 0), (REM, D))
    d_act_one = lax.dynamic_update_slice(d_act_one, here + far, (shared, 0))
    q_send = [added(q[1, i], q_got[1, i]) for i in range(4)]
    q_y = {i: swap_y(q_send[i]) for i in (3, 2)}
    q = added(q[0], q_got[0])
    dn_part = z_scatter(added(dn, jnp.concatenate([dn_low, dn_high], 0)).reshape(4 * 144, D))
    d_h_zero, d_ln1_gain, d_ln1_bias = ln1_back(d_act_one)
    d_h_zero = d_h_zero + d_h_one
    zero_low = b16(d_h_zero)
    k, k_got = skip_back(at, tok_flat, skip_flat, zero_low)

    def onward(mine, got, so_far):
        return next_z(b16(f32(mine) + f32(got) + f32(so_far)))

    sums = jnp.concatenate(
        [
            jnp.sum(d_h_zero, axis=0),
            d_ln1_gain,
            d_ln1_bias,
            jnp.sum(d_h_one, axis=0),
            d_ln2_gain,
            d_ln2_bias,
            d_up_bias[0],
            jnp.sum(grad_two, axis=0),
        ]
    ).reshape(-1, 128)
    q_y[3], q_y[2], q, q_send, k, k_got, zero_low, sums, proj_part = tied(
        q_y[3], q_y[2], q, q_send, k, k_got, zero_low, sums, proj_part
    )
    k_got = swap_core(k_got)
    q_next = next_z(added(q[3], q_y[3]))
    q_y[1] = swap_y(q_send[1])
    proj_far = swap_seq(proj_part)
    d_tokens = back_dot(zero_low, w_skip[:D]).reshape(1, count, D)
    sums = vector_step(sums, 1)
    q_next, q_y, k, k_got, sums, zero_low, d_tokens, proj_far, up_part = tied(
        q_next, q_y, k, k_got, sums, zero_low, d_tokens, proj_far, up_part
    )
    q_next = onward(q[2], q_y[2], q_next)
    k_send = [added(k[1, i], k_got[1, i]) for i in range(4)]
    q_y[0] = swap_y(q_send[0])
    k_y = {3: swap_y(k_send[3])}
    k = added(k[0], k_got[0])
    up_far = swap_seq(up_part)
    out_proj = f32(proj_part) + f32(proj_far)
    d_skip = back_dot(zero_low, w_skip[D:]).reshape(1, count, D)
    q_next, q_y, k_y, k, k_send, sums, d_skip, up_far = tied(
        q_next, q_y, k_y, k, k_send, sums, d_skip, up_far
    )
    q_next = onward(q[1], q_y[1], q_next)
    k_next = next_z(added(k[3], k_y[3]))
    k_y[2], k_y[1] = swap_y(k_send[2]), swap_y(k_send[1])
    out_up = f32(up_part) + f32(up_far)
    sums = vector_step(sums, 0, "seq")
    q_next, k_next, k_y, sums, dn_part = tied(q_next, k_next, k_y, sums, dn_part)
    q_sum = b16(f32(q[0]) + f32(q_y[0]) + f32(q_next))
    q_got = swap_seq(q_sum)
    k_next = onward(k[2], k_y[2], k_next)
    k_y[0] = swap_y(k_send[0])
    q_got, k_next, k_y, dn_part, sums = tied(q_got, k_next, k_y, dn_part, sums)
    dn_got = swap_seq(dn_part)
    out_qkv = f32(q_sum) + f32(q_got)
    k_next = onward(k[1], k_y[1], k_next)
    sums = vector_step(sums, 2)
    k_next, k_y, sums, dn_got = tied(k_next, k_y, sums, dn_got)
    out_down = by_side(side, dn_part, dn_got)
    k_sum = b16(f32(k[0]) + f32(k_y[0]) + f32(k_next))
    out_skip = f32(k_sum) + f32(swap_seq(k_sum))
    sums = vector_step(vector_step(sums, 4), 8).reshape(-1)
    starts = [0, D, 2 * D, 3 * D, 4 * D, 5 * D, 6 * D, 10 * D, 11 * D]
    sums = [sums[a:b] for a, b in zip(starts, starts[1:])]
    grads = (out_skip, out_qkv, out_proj, out_up, out_down)
    return (output, d_tokens, d_skip, *grads, *sums)


def solution(mesh):
    in_specs = (
        P("batch", "seq", None),
        P("seq", "batch", None, None),
        P("batch", None),
        P("batch", "seq", None),
        *(P("batch", None),) * 5,
        *(P(),) * 8,
    )
    out_specs = (*(P("batch", "seq", None),) * 3, *(P("batch", None),) * 5, *(P(),) * 8)
    pair = mesh.shape["batch"] == ROWS and mesh.shape["seq"] == 2
    return jax.shard_map(
        per_device_pair if pair else per_device,
        mesh=mesh,
        in_specs=in_specs,
        out_specs=out_specs,
        check_vma=False,

    )
```

```python
import math

import jax
import jax.numpy as jnp
from jax import lax
from jax.experimental import pallas as pl
from jax.experimental.pallas import tpu as pltpu
from jax.sharding import PartitionSpec as P

HEADS = 16
HD = 72
D = 1152
ROWS = 16
EPS = 1e-05

SCALE = HD**-0.5
C2 = SCALE * math.log2(math.e)
REM = 576
TILES = {
    0: [
        (256, 576, 258, 832, [(False, 256, 576, 258, 832), (True, 0, 464, 0, 452)]),
        (0, 272, 0, 258, [(False, 0, 272, 0, 258)]),
    ],
    1: [
        (0, 464, 0, 452, [(False, 0, 464, 0, 452), (True, 0, 576, 2, 576)]),
        (448, 272, 452, 710, [(False, 448, 272, 452, 710)]),
        (704, 128, 710, 832, [(False, 704, 128, 710, 832)]),
    ],
}
NT = (((1,), (1,)), ((), ()))


def dot(a, b, dims=(((1,), (0,)), ((), ()))):
    return lax.dot_general(a, b, dims, preferred_element_type=jnp.float32)


def split(n, step):
    return [(i, min(step, n - i)) for i in range(0, n, step)]


def full(shape):
    return pl.BlockSpec(shape, lambda h, s: (0,) * len(shape), pipeline_mode=pl.Buffered(1))


def pair_window(pair):
    tile = (2 * HD * pair) // 128
    first = 2 * HD * pair - 128 * tile
    lane = lax.broadcasted_iota(jnp.int32, (1, 256), 1)
    left = (lane >= first) & (lane < first + HD)
    right = (lane >= first + HD) & (lane < first + 2 * HD)
    base = pl.multiple_of(tile * 128, 128)

    def at(offset, row, count):
        return slice(row, row + count), pl.ds(pl.multiple_of(base + offset, 128), 256)

    return at, left, right


def stacked(value, left, right):
    zero = jnp.zeros_like(value)
    return jnp.concatenate([jnp.where(left, value, zero), jnp.where(right, value, zero)], 0)


def fwd_kernel(s_ref, qkv_ref, kvr_ref, o_ref, l_ref, *, qstep):
    pair = pl.program_id(0)

    @pl.when(pair == 0)
    def _():
        o_ref[...] = jnp.zeros_like(o_ref)
        l_ref[...] = jnp.zeros_like(l_ref)

    at, left, right = pair_window(pair)

    def chunk(r0, n, qv0, qv1, keys):
        q2 = stacked(qkv_ref[at(0, r0, n)], left, right)
        scores = []
        for far, k0, kc, kv0, kv1 in keys:
            k = kvr_ref[at(0, k0, kc)] if far else qkv_ref[at(D, k0, kc)]
            s = dot(q2, k, NT)
            if kv0 > k0 or kv1 < k0 + kc:
                kp = k0 + lax.broadcasted_iota(jnp.int32, (1, kc), 1)
                s = jnp.where((kp >= kv0) & (kp < kv1), s, -1e30)
            scores.append(s)
        top = jnp.max(scores[0], axis=1, keepdims=True)
        for s in scores[1:]:
            top = jnp.maximum(top, jnp.max(s, axis=1, keepdims=True))
        top = top * C2
        total, out = 0.0, 0.0
        for s, (far, k0, kc, _, _) in zip(scores, keys):
            p = jnp.exp2(s * C2 - top)
            total = total + jnp.sum(p, axis=1, keepdims=True)
            v = kvr_ref[at(D, k0, kc)] if far else qkv_ref[at(2 * D, k0, kc)]
            out = out + dot(p.astype(jnp.bfloat16), v)
        out = out * (1.0 / total)
        lse = top + jnp.log2(total)
        out = jnp.where(left, out[:n], out[n:]).astype(jnp.bfloat16)
        head = lax.broadcasted_iota(jnp.int32, (1, 128), 1) - 2 * pair
        lse = jnp.where(head == 0, lse[:n], lse[n:])
        keep, keep_l = left | right, (head == 0) | (head == 1)
        if r0 < qv0 or r0 + n > qv1:
            row = r0 + lax.broadcasted_iota(jnp.int32, (n, 1), 0)
            valid = (row >= qv0) & (row < qv1)
            keep, keep_l = keep & valid, keep_l & valid
        o_ref[at(0, r0, n)] = jnp.where(keep, out, o_ref[at(0, r0, n)])
        l_ref[r0 : r0 + n, :] = jnp.where(keep_l, lse, l_ref[r0 : r0 + n, :])

    for side in (0, 1):

        @pl.when(s_ref[0] == side)
        def _():
            for q0, nq, qv0, qv1, keys in TILES[side]:
                for a, n in split(nq, qstep):
                    chunk(q0 + a, n, qv0, qv1, keys)


def attn_fwd(sidx, qkv, kvr, qstep=288):
    return pl.pallas_call(
        lambda *r: fwd_kernel(*r, qstep=qstep),
        out_shape=(
            jax.ShapeDtypeStruct((832, D), jnp.bfloat16),
            jax.ShapeDtypeStruct((832, 128), jnp.float32),
        ),
        grid_spec=pltpu.PrefetchScalarGridSpec(
            num_scalar_prefetch=1,
            grid=(HEADS // 2,),
            in_specs=[full((832, 3 * D)), full((REM, 2 * D))],
            out_specs=(full((832, D)), full((832, 128))),
        ),
        compiler_params=pltpu.CompilerParams(vmem_limit_bytes=60 * 2**20),
        name="attn_fwd",
    )(sidx, qkv, kvr)


def bwd_kernel(s_ref, qkv_ref, kvr_ref, do_ref, lt_ref, dt_ref, dqkv_ref, dkvr_ref, *, kstep):
    pair = pl.program_id(0)

    @pl.when(pair == 0)
    def _():
        dqkv_ref[...] = jnp.zeros_like(dqkv_ref)
        dkvr_ref[...] = jnp.zeros_like(dkvr_ref)

    at, left, right = pair_window(pair)

    def tile(q0, nq, qv0, qv1, keys):
        q2 = stacked(qkv_ref[at(0, q0, nq)], left, right)
        do2 = stacked(do_ref[at(0, q0, nq)], left, right)

        def both(ref, mask):
            rows = []
            for h in (0, 1):
                row = ref[pl.ds(2 * pair + h, 1), :][:, q0 : q0 + nq]
                if mask and (qv0 > q0 or qv1 < q0 + nq):
                    qp = q0 + lax.broadcasted_iota(jnp.int32, (1, nq), 1)
                    row = jnp.where((qp >= qv0) & (qp < qv1), row, 1e30)
                rows.append(row)
            return jnp.concatenate(rows, 1)

        lse, row_dot = both(lt_ref, True), both(dt_ref, False)
        dqt = 0.0
        for far, first, count, kv0, kv1 in keys:
            for a, kc in split(count, kstep):
                k0 = first + a
                k = kvr_ref[at(0, k0, kc)] if far else qkv_ref[at(D, k0, kc)]
                v = kvr_ref[at(D, k0, kc)] if far else qkv_ref[at(2 * D, k0, kc)]
                p = jnp.exp2(dot(k, q2, NT) * C2 - lse)
                if kv0 > k0 or kv1 < k0 + kc:
                    kp = k0 + lax.broadcasted_iota(jnp.int32, (kc, 1), 0)
                    p = jnp.where((kp >= kv0) & (kp < kv1), p, 0.0)
                ds = (p * (dot(v, do2, NT) - row_dot)).astype(jnp.bfloat16)
                dv = dot(p.astype(jnp.bfloat16), do2).astype(jnp.bfloat16)
                dk = (dot(ds, q2) * SCALE).astype(jnp.bfloat16)
                if far:
                    dkvr_ref[at(0, k0, kc)] += dk
                    dkvr_ref[at(D, k0, kc)] += dv
                else:
                    dqkv_ref[at(D, k0, kc)] += dk
                    dqkv_ref[at(2 * D, k0, kc)] += dv
                dqt = dqt + dot(k.T, ds)
        dq = (dqt * SCALE).T
        dq = jnp.where(left, dq[:nq], jnp.where(right, dq[nq:], 0.0)).astype(jnp.bfloat16)
        dqkv_ref[at(0, q0, nq)] += dq

    for side in (0, 1):

        @pl.when(s_ref[0] == side)
        def _():
            for parts in TILES[side]:
                tile(*parts)


def attn_bwd(sidx, qkv, kvr, do, lt, dt, kstep=1024):
    return pl.pallas_call(
        lambda *r: bwd_kernel(*r, kstep=kstep),
        out_shape=(
            jax.ShapeDtypeStruct((832, 3 * D), jnp.bfloat16),
            jax.ShapeDtypeStruct((REM, 2 * D), jnp.bfloat16),
        ),
        grid_spec=pltpu.PrefetchScalarGridSpec(
            num_scalar_prefetch=1,
            grid=(HEADS // 2,),
            in_specs=[
                full((832, 3 * D)),
                full((REM, 2 * D)),
                full((832, D)),
                full((16, 832)),
                full((16, 832)),
            ],
            out_specs=(full((832, 3 * D)), full((REM, 2 * D))),
        ),
        compiler_params=pltpu.CompilerParams(vmem_limit_bytes=60 * 2**20),
        name="attn_bwd",
    )(sidx, qkv, kvr, do, lt, dt)


ERFC = (0.5 * 1.061405429, -0.5 * 1.453152027, 0.5 * 1.421413741, -0.5 * 0.284496736, 0.5 * 0.254829592)


def normal_cdf(u):
    expo = jnp.exp2(u * u * (-0.5 * math.log2(math.e)))
    below = 1.0 + (0.3275911 * math.sqrt(0.5)) * jnp.abs(u)
    step = pltpu.reciprocal(below, approx=True)
    step = step * (2.0 - below * step)
    tail = ERFC[0]
    for term in ERFC[1:]:
        tail = tail * step + term
    tail = tail * step * expo
    return jnp.where(u < 0.0, tail, 1.0 - tail), expo


def mlp_up(at, act, weight, bias, grad, tile=D, chunks=4):
    rows, width = act.shape[0], weight.shape[1]
    steps = width // tile
    size = rows // chunks

    def kernel(at, a_ref, w_ref, b_ref, e_ref, g_ref, d_ref, mine, other, held):
        t = pl.program_id(0)

        def forward():
            for i in range(chunks):
                part = slice(i * size, (i + 1) * size)
                u = dot(a_ref[part], w_ref[...]) + b_ref[...]
                phi, expo = normal_cdf(u)
                g = (u * phi).astype(jnp.bfloat16)
                g_ref[part] = g
                d_ref[part] = (phi + u * expo * (1.0 / math.sqrt(2.0 * math.pi))).astype(jnp.bfloat16)

        def keep():
            held[...] = g_ref[...].T

        def back():
            for yy in (0, 1):
                both = dot(held[yy * 576 : yy * 576 + 576], e_ref[...])
                low, high = both[:288], both[288:]
                yrel = yy + at[1] - 2 * yy * at[1]
                for ref, value in (
                    (mine, jnp.where(at[2] == 0, low, high)),
                    (other, jnp.where(at[2] == 0, high, low)),
                ):
                    value = value.astype(jnp.bfloat16)
                    ref[at[3], yrel, 0] = value[:144]
                    ref[1 - at[3], yrel, 0] = value[144:]

        @pl.when(t == 0)
        def _():
            forward()
            keep()

        @pl.when((t > 0) & (t < steps))
        def _():
            back()
            forward()
            keep()

        @pl.when(t == steps)
        def _():
            back()

    out = jax.ShapeDtypeStruct((rows, width), jnp.bfloat16)
    split = jax.ShapeDtypeStruct((2, 2, 4, 144, D), jnp.bfloat16)

    def now(t):
        return jnp.minimum(t, steps - 1)

    whole = pl.BlockSpec((rows, D), lambda t, at: (0, 0), pipeline_mode=pl.Buffered(1))
    by_column = pl.BlockSpec((rows, tile), lambda t, at: (0, now(t)))
    split_spec = pl.BlockSpec((2, 2, 1, 144, D), lambda t, at: (0, 0, jnp.maximum(t - 1, 0), 0, 0))
    return pl.pallas_call(
        kernel,
        out_shape=(out, out, split, split),
        grid_spec=pltpu.PrefetchScalarGridSpec(
            num_scalar_prefetch=1,
            grid=(steps + 1,),
            in_specs=[
                whole,
                pl.BlockSpec((D, tile), lambda t, at: (0, now(t))),
                pl.BlockSpec((1, tile), lambda t, at: (0, now(t))),
                whole,
            ],
            out_specs=(by_column, by_column, split_spec, split_spec),
            scratch_shapes=[pltpu.VMEM((tile, rows), jnp.bfloat16)],
        ),
        compiler_params=pltpu.CompilerParams(vmem_limit_bytes=60 * 2**20),
        name="mlp_up",
    )(at, act, weight, bias.reshape(1, width), grad)


def ordered_transpose(at, value, held, ring=True):
    held[...] = value.astype(jnp.float32).T.reshape(held.shape)
    blocks = []
    for crel in (0, 1):
        for yrel in (0, 1):
            for zrel in range(4):
                zz = lax.rem(at[0] + zrel, 4) if ring else zrel
                yy = at[1] + yrel - 2 * at[1] * yrel
                cc = at[2] + crel - 2 * at[2] * crel
                blocks.append(held[zz * 4 + yy * 2 + cc])
    return jnp.concatenate(blocks, 0).astype(jnp.bfloat16)


def mlp_back(at, act, grad, gelu, slope, w_up, w_down, halves=1, tile=768):
    rows, width = gelu.shape
    half = rows // halves

    def kernel(at, a_ref, e_ref, g_ref, s_ref, wu_ref, wd_ref, *refs):
        mine, other, h_ref, c_ref, b_ref, a_t, du_ref, held = refs

        @pl.when(pl.program_id(0) == 0)
        def _():
            a_t[...] = ordered_transpose(at, a_ref[...], held, ring=False)
            h_ref[...] = jnp.zeros_like(h_ref)
            c_ref[...] = jnp.zeros_like(c_ref)

        bias = None
        for i in range(halves):
            part = slice(i * half, (i + 1) * half)
            du = dot(e_ref[part], wd_ref[...], NT) * s_ref[part].astype(jnp.float32)
            total = jnp.sum(du, axis=0, keepdims=True)
            bias = total if bias is None else bias + total
            du = du.astype(jnp.bfloat16)
            du_ref[part] = du
            h_ref[part] += dot(g_ref[part], wd_ref[...])
            c_ref[part] += dot(du, wu_ref[...], NT)
        b_ref[...] = bias
        for i, ref in ((0, mine), (1, other)):
            both = dot(a_t[i * 576 : i * 576 + 576], du_ref[...])
            for j in range(8):
                ref[j // 4, j % 4] = both[j * 72 : j * 72 + 72].astype(jnp.bfloat16)

    once = pl.Buffered(1)
    whole = jax.ShapeDtypeStruct((rows, D), jnp.float32)
    split = jax.ShapeDtypeStruct((2, 4, 72, width), jnp.bfloat16)
    split_spec = pl.BlockSpec((2, 4, 72, tile), lambda t, at: (0, 0, 0, t))
    whole_spec = pl.BlockSpec((rows, D), lambda t, at: (0, 0), pipeline_mode=once)
    by_column = pl.BlockSpec((rows, tile), lambda t, at: (0, t))
    weight_column = pl.BlockSpec((D, tile), lambda t, at: (0, t))
    return pl.pallas_call(
        kernel,
        out_shape=(
            split,
            split,
            whole,
            whole,
            jax.ShapeDtypeStruct((1, width), jnp.float32),
        ),
        grid_spec=pltpu.PrefetchScalarGridSpec(
            num_scalar_prefetch=1,
            grid=(width // tile,),
            in_specs=[
                whole_spec,
                whole_spec,
                by_column,
                by_column,
                weight_column,
                pl.BlockSpec((tile, D), lambda t, at: (t, 0)),
            ],
            out_specs=(
                split_spec,
                split_spec,
                whole_spec,
                whole_spec,
                pl.BlockSpec((1, tile), lambda t, at: (0, t)),
            ),
            scratch_shapes=[
                pltpu.VMEM((D, rows), jnp.bfloat16),
                pltpu.VMEM((rows, tile), jnp.bfloat16),
                pltpu.VMEM((16, 72, rows), jnp.float32),
            ],
        ),
        compiler_params=pltpu.CompilerParams(vmem_limit_bytes=62 * 2**20),
        name="mlp_back",
    )(at, act, grad, gelu, slope, w_up, w_down)


def qkv_grad(at, act, act_far, grad, grad_far):
    rows, far = act.shape[0], act_far.shape[0]

    def kernel(at, a_ref, f_ref, g_ref, h_ref, mine, other, a_t, f_t, held, held_far):
        t = pl.program_id(0)

        @pl.when(t == 0)
        def _():
            a_t[...] = ordered_transpose(at, a_ref[...], held)
            f_t[...] = ordered_transpose(at, f_ref[...], held_far)

        away = jnp.where(t > 0, h_ref[...], jnp.zeros_like(h_ref))
        for i, ref in ((0, mine), (1, other)):
            part = slice(i * 576, (i + 1) * 576)
            both = dot(a_t[part], g_ref[...]) + dot(f_t[part], away)
            for j in range(8):
                ref[j // 4, j % 4] = both[j * 72 : j * 72 + 72].astype(jnp.bfloat16)

    once = pl.Buffered(1)
    split = jax.ShapeDtypeStruct((2, 4, 72, 3 * D), jnp.bfloat16)
    split_spec = pl.BlockSpec((2, 4, 72, D), lambda t, at: (0, 0, 0, t))
    return pl.pallas_call(
        kernel,
        out_shape=(split, split),
        grid_spec=pltpu.PrefetchScalarGridSpec(
            num_scalar_prefetch=1,
            grid=(3,),
            in_specs=[
                pl.BlockSpec((rows, D), lambda t, at: (0, 0), pipeline_mode=once),
                pl.BlockSpec((far, D), lambda t, at: (0, 0), pipeline_mode=once),
                pl.BlockSpec((rows, D), lambda t, at: (0, t)),
                pl.BlockSpec((far, D), lambda t, at: (0, jnp.maximum(t - 1, 0))),
            ],
            out_specs=(split_spec, split_spec),
            scratch_shapes=[
                pltpu.VMEM((D, rows), jnp.bfloat16),
                pltpu.VMEM((D, far), jnp.bfloat16),
                pltpu.VMEM((16, 72, rows), jnp.float32),
                pltpu.VMEM((16, 72, far), jnp.float32),
            ],
        ),
        compiler_params=pltpu.CompilerParams(vmem_limit_bytes=60 * 2**20),
        name="qkv_grad",
    )(at, act, act_far, grad, grad_far)


def skip_back(at, tok, skip, grad):
    rows = tok.shape[0]

    def kernel(at, t_ref, s_ref, g_ref, mine, other, in_t):
        i = pl.program_id(0)

        @pl.when(i == 0)
        def _():
            in_t[0:D] = t_ref[...].T
            in_t[D:] = s_ref[...].T

        first = pl.multiple_of(lax.rem(at[0] + i, 4) * 576, 16)
        both = dot(in_t[pl.ds(first, 576)], g_ref[...])
        for yy in (0, 1):
            low, high = both[yy * 288 : yy * 288 + 144], both[yy * 288 + 144 : yy * 288 + 288]
            yrel = yy + at[1] - 2 * yy * at[1]
            mine[yrel, 0] = jnp.where(at[2] == 0, low, high).astype(jnp.bfloat16)
            other[yrel, 0] = jnp.where(at[2] == 0, high, low).astype(jnp.bfloat16)

    split = jax.ShapeDtypeStruct((2, 4, 144, D), jnp.bfloat16)
    split_spec = pl.BlockSpec((2, 1, 144, D), lambda t, at: (0, t, 0, 0))
    whole_spec = pl.BlockSpec((rows, D), lambda t, at: (0, 0), pipeline_mode=pl.Buffered(1))
    return pl.pallas_call(
        kernel,
        out_shape=(split, split),
        grid_spec=pltpu.PrefetchScalarGridSpec(
            num_scalar_prefetch=1,
            grid=(4,),
            in_specs=[whole_spec] * 3,
            out_specs=(split_spec, split_spec),
            scratch_shapes=[pltpu.VMEM((2 * D, rows), jnp.bfloat16)],
        ),
        compiler_params=pltpu.CompilerParams(vmem_limit_bytes=40 * 2**20),
        name="skip_back",
    )(at, tok, skip, grad)


def layer_norm(hidden, gain, shift):
    centred = hidden - jnp.mean(hidden, axis=-1, keepdims=True)
    spread = jnp.mean(centred * centred, axis=-1, keepdims=True)
    return centred * lax.rsqrt(spread + EPS) * gain + shift


def exact_gelu(value):
    return jax.nn.gelu(value, approximate=False)


def segment_ids(offsets, positions):
    hits = (positions[None, :, None] >= offsets[:, None, :]).astype(jnp.int32)
    return jnp.sum(hits, axis=-1)


def fwd_dot(left, right):
    return jnp.dot(left, right, preferred_element_type=jnp.float32)


def contract_rows(left, right):
    return lax.dot_general(
        left, right, (((0,), (0,)), ((), ())), preferred_element_type=jnp.float32
    )


def back_dot(grad_rows, weight):
    return lax.dot_general(
        grad_rows, weight, (((1,), (1,)), ((), ())), preferred_element_type=jnp.float32
    )


class RowAttention:
    def __init__(self, qkv_all, offsets, row_count, local_len):
        self.row_count, self.local_len = row_count, local_len
        self.row_len = local_len * lax.axis_size("seq")
        self.offsets = offsets
        first_pos = lax.axis_index("seq") * local_len
        self.query_seg = segment_ids(offsets, first_pos + jnp.arange(local_len, dtype=jnp.int32))
        self.scale = HD ** (-0.5)
        self.queries = qkv_all[:, :D].reshape(row_count, local_len, HEADS, HD)
        keyvals = qkv_all[:, D:].reshape(row_count, local_len, 2 * D)
        self.kv = lax.all_gather(keyvals, "seq", axis=1, tiled=True)

    def block(self, first, size):
        kv = lax.dynamic_slice_in_dim(self.kv, first, size, 1)
        shape = (self.row_count, size, HEADS, HD)
        key_seg = segment_ids(self.offsets, first + jnp.arange(size, dtype=jnp.int32))
        same = self.query_seg[:, :, None, None] == key_seg[:, None, None, :]
        return kv[:, :, :D].reshape(shape), kv[:, :, D:].reshape(shape), same

    def scores(self, keys):
        return (
            jnp.einsum("rthd,rkhd->rthk", self.queries, keys, preferred_element_type=jnp.float32)
            * self.scale
        )

    def forward(self):
        keys, values, same = self.block(0, self.row_len)
        scores = jnp.where(same, self.scores(keys), -1e30)
        top = jnp.max(scores, axis=-1)
        expo = jnp.where(same, jnp.exp(scores - top[..., None]), 0.0)
        norm = jnp.sum(expo, axis=-1)
        weighted = jnp.einsum(
            "rthk,rkhd->rthd",
            expo.astype(jnp.bfloat16),
            values,
            preferred_element_type=jnp.float32,
        )
        self.attended = weighted / norm[..., None]
        self.log_total = top + jnp.log(norm)
        return self.attended.reshape(-1, D).astype(jnp.bfloat16)

    def backward(self, d_att):
        rows, length = self.row_count, self.local_len
        d_att = d_att.reshape(rows, length, HEADS, HD)
        row_dot = jnp.sum(d_att.astype(jnp.float32) * self.attended, axis=-1)
        size = math.gcd(self.row_len, 512)

        def step(index, totals):
            d_query, d_kv = totals
            keys, values, same = self.block(index * size, size)
            weights = jnp.where(same, jnp.exp(self.scores(keys) - self.log_total[..., None]), 0.0)
            d_weights = jnp.einsum(
                "rthd,rkhd->rthk", d_att, values, preferred_element_type=jnp.float32
            )
            d_scores = (weights * (d_weights - row_dot[..., None])).astype(jnp.bfloat16)
            d_query = d_query + self.scale * jnp.einsum(
                "rthk,rkhd->rthd", d_scores, keys, preferred_element_type=jnp.float32
            )
            d_key = self.scale * jnp.einsum(
                "rthk,rthd->rkhd", d_scores, self.queries, preferred_element_type=jnp.float32
            )
            d_value = jnp.einsum(
                "rthk,rthd->rkhd",
                weights.astype(jnp.bfloat16),
                d_att,
                preferred_element_type=jnp.float32,
            )
            both = jnp.concatenate(
                [d_key.reshape(rows, size, D), d_value.reshape(rows, size, D)], axis=2
            )
            return d_query, lax.dynamic_update_slice_in_dim(d_kv, both, index * size, 1)

        start = (
            jnp.zeros((rows, length, HEADS, HD), jnp.float32),
            jnp.zeros((rows, self.row_len, 2 * D), jnp.float32),
        )
        d_query, d_kv = lax.fori_loop(0, self.row_len // size, step, start)
        d_kv = lax.psum_scatter(
            d_kv.astype(jnp.bfloat16), "seq", scatter_dimension=1, tiled=True
        ).astype(jnp.float32)
        return jnp.concatenate(
            [d_query.reshape(rows * length, D), d_kv.reshape(rows * length, 2 * D)], axis=1
        ).astype(jnp.bfloat16)


def per_device(
    tokens,
    skip_parts,
    lengths,
    cotangent,
    skip_w,
    qkv_w,
    proj_w,
    fc1_w,
    fc2_w,
    skip_bias,
    ln1_gain,
    ln1_bias,
    proj_bias,
    ln2_gain,
    ln2_bias,
    fc1_bias,
    fc2_bias,
):
    row_count, local_len, features = tokens.shape
    tok_count = row_count * local_len
    offsets = jnp.cumsum(lengths, axis=1)
    first_pos = lax.axis_index("seq") * local_len
    query_seg = segment_ids(offsets, first_pos + jnp.arange(local_len, dtype=jnp.int32))
    live_mask = (query_seg < lengths.shape[1]).astype(jnp.float32).reshape(tok_count, 1)
    skip_rows = lax.psum_scatter(skip_parts[0], "seq", scatter_dimension=1, tiled=True)
    w_skip, w_qkv, w_proj, w_up, w_down = (
        lax.all_gather(w, "batch", axis=0, tiled=True)
        for w in (skip_w, qkv_w, proj_w, fc1_w, fc2_w)
    )
    tok_flat = tokens.reshape(tok_count, features)
    skip_flat = skip_rows.reshape(tok_count, features)
    h_zero = (
        fwd_dot(tok_flat, w_skip[:features]) + fwd_dot(skip_flat, w_skip[features:]) + skip_bias
    )
    normed_one, ln1_back = jax.vjp(layer_norm, h_zero, ln1_gain, ln1_bias)
    act_one = normed_one.astype(jnp.bfloat16)
    qkv_all = fwd_dot(act_one, w_qkv).astype(jnp.bfloat16)
    attention = RowAttention(qkv_all, offsets, row_count, local_len)
    att_low = attention.forward()
    h_one = h_zero + fwd_dot(att_low, w_proj) + proj_bias
    normed_two, ln2_back = jax.vjp(layer_norm, h_one, ln2_gain, ln2_bias)
    act_two = normed_two.astype(jnp.bfloat16)
    up_proj = fwd_dot(act_two, w_up) + fc1_bias
    gelu_out, gelu_back = jax.vjp(exact_gelu, up_proj)
    gelu_low = gelu_out.astype(jnp.bfloat16)
    h_two = h_one + fwd_dot(gelu_low, w_down) + fc2_bias
    output = (h_two * live_mask).astype(jnp.bfloat16).reshape(row_count, local_len, features)
    grad_two = cotangent.reshape(tok_count, features).astype(jnp.float32) * live_mask
    grad_low = grad_two.astype(jnp.bfloat16)
    d_w_down = contract_rows(gelu_low, grad_low)
    d_gelu = back_dot(grad_low, w_down)
    d_up = gelu_back(d_gelu)[0]
    up_low = d_up.astype(jnp.bfloat16)
    d_w_up = contract_rows(act_two, up_low)
    d_act_two = back_dot(up_low, w_up)
    d_h_one, d_ln2_gain, d_ln2_bias = ln2_back(d_act_two)
    d_h_one = d_h_one + grad_two
    proj_low = d_h_one.astype(jnp.bfloat16)
    d_w_proj = contract_rows(att_low, proj_low)
    d_att = back_dot(proj_low, w_proj).astype(jnp.bfloat16)
    d_qkv = attention.backward(d_att)
    d_w_qkv = contract_rows(act_one, d_qkv)
    d_act_one = back_dot(d_qkv, w_qkv)
    d_h_zero, d_ln1_gain, d_ln1_bias = ln1_back(d_act_one)
    d_h_zero = d_h_zero + d_h_one
    zero_low = d_h_zero.astype(jnp.bfloat16)
    d_w_skip = jnp.concatenate(
        [contract_rows(tok_flat, zero_low), contract_rows(skip_flat, zero_low)], axis=0
    )
    d_tokens = back_dot(zero_low, w_skip[:features]).reshape(row_count, local_len, features)
    d_skip = back_dot(zero_low, w_skip[features:]).reshape(row_count, local_len, features)
    vector_sums = lax.psum(
        (
            jnp.sum(d_h_zero, axis=0),
            d_ln1_gain,
            d_ln1_bias,
            jnp.sum(d_h_one, axis=0),
            d_ln2_gain,
            d_ln2_bias,
            jnp.sum(d_up, axis=0),
            jnp.sum(grad_two, axis=0),
        ),
        ("batch", "seq"),
    )
    weight_grads = tuple(
        lax.psum(
            lax.psum_scatter(
                grad.astype(jnp.bfloat16), "batch", scatter_dimension=0, tiled=True
            ),
            "seq",
        ).astype(jnp.float32)
        for grad in (d_w_skip, d_w_qkv, d_w_proj, d_w_up, d_w_down)
    )
    return (output, d_tokens, d_skip, *weight_grads, *vector_sums)


YSW = [(b, b ^ 2) for b in range(16)]
CSW = [(b, b ^ 1) for b in range(16)]
ZUP = [(b, (b + 4) % 16) for b in range(16)]


def swap_y(v):
    return lax.ppermute(v, "batch", YSW)


def swap_core(v):
    return lax.ppermute(v, "batch", CSW)


def next_z(v):
    return lax.ppermute(v, "batch", ZUP)


def swap_seq(v):
    return lax.ppermute(v, "seq", [(0, 1), (1, 0)])


def place():
    b = lax.axis_index("batch").astype(jnp.int32)
    return b // 4, (b // 2) % 2, b % 2


def f32(v):
    return v.astype(jnp.float32)


def b16(v):
    return v.astype(jnp.bfloat16)


def core_pair(shard):
    core = place()[2]
    half = shard.shape[1] // 2
    low, high = shard[:, :half], shard[:, half:]
    keep = jnp.where(core == 0, low, high)
    got = swap_core(jnp.where(core == 0, high, low))
    return jnp.where(
        core == 0, jnp.concatenate([keep, got], 0), jnp.concatenate([got, keep], 0)
    )


def tied(*values):
    return lax.optimization_barrier(values)


def with_core(own):
    return own + [swap_core(v) for v in own]


def assemble(pieces, kind):
    rows, cols = pieces[0].shape
    split, halves, paired = kind == "split", kind.endswith("halves"), kind == "halves"
    if split:
        shapes = [(8 * rows, 3 * D), (8 * rows, D)]
    elif halves:
        shapes = [(8 * rows, 2 * cols)]
    else:
        shapes = [(16 * rows, cols)]

    def kernel(at, *refs):
        ins, outs, (held, came, left) = refs[:16], refs[16:-3], refs[-3:]
        z, y, c, x = at[0], at[1], at[2], at[3]
        loads = [pltpu.make_async_copy(ins[j], held.at[j], came.at[j]) for j in range(16)]
        for load in loads:
            load.start()
        waits = []
        for j in range(16):
            core = c if j < 8 else 1 - c
            yy = y if j % 8 < 4 else 1 - y
            away = j % 4
            if paired and j % 8 in (4, 5):
                away = away + x - 2 * away * x
            zz = lax.rem(z - away + 4, 4)
            loads[j].wait()
            if not split:
                if halves:
                    first = pl.multiple_of((zz * 2 + yy) * rows, 16)
                    at_cols = pl.ds(pl.multiple_of(core * cols, 128), cols)
                    target = outs[0].at[pl.ds(first, rows), at_cols]
                else:
                    first = pl.multiple_of((zz * 4 + yy * 2 + core) * rows, 16)
                    target = outs[0].at[pl.ds(first, rows), :]
                store = pltpu.make_async_copy(held.at[j], target, left.at[j])
                store.start()
                waits.append((None, store))
                continue
            at_rows = pl.ds(pl.multiple_of((zz * 2 + yy) * rows, 16), rows)
            at_cols = pl.ds(pl.multiple_of(core * (2 * D), 128), D)
            store = pltpu.make_async_copy(
                held.at[j, :, pl.ds(0, D)], outs[0].at[at_rows, at_cols], left.at[j]
            )
            store.start()
            waits.append((None, store))
            for which, target in ((0, outs[0].at[at_rows, pl.ds(D, D)]), (1, outs[1].at[at_rows, :])):
                store = pltpu.make_async_copy(held.at[j, :, pl.ds(D, D)], target, left.at[16 + j])
                pl.when(core == which)(store.start)
                waits.append((core == which, store))
        for needed, store in waits:
            if needed is None:
                store.wait()
            else:
                pl.when(needed)(store.wait)

    out = pl.pallas_call(
        kernel,
        out_shape=[jax.ShapeDtypeStruct(v, pieces[0].dtype) for v in shapes],
        in_specs=[pl.BlockSpec(memory_space=pltpu.SMEM)]
        + [pl.BlockSpec(memory_space=pl.ANY)] * 16,
        out_specs=[pl.BlockSpec(memory_space=pl.ANY)] * len(shapes),
        scratch_shapes=[
            pltpu.VMEM((16, rows, cols), pieces[0].dtype),
            pltpu.SemaphoreType.DMA((16,)),
            pltpu.SemaphoreType.DMA((32,)),
        ],
        compiler_params=pltpu.CompilerParams(vmem_limit_bytes=16 * 2**20),
        name="assemble",
    )(jnp.stack([*place(), lax.axis_index("seq").astype(jnp.int32)]), *pieces)
    return out if split else out[0]


def take(v, axis, index):
    return lax.dynamic_index_in_dim(v, index, axis, keepdims=False)


def added(left, right):
    return b16(f32(left) + f32(right))


def by_side(side, own, other):
    own, other = f32(own), f32(other)
    return jnp.where(
        side == 0, jnp.concatenate([own, other], 0), jnp.concatenate([other, own], 0)
    )


def vector_step(value, bit, axis="batch"):
    if axis == "seq":
        return value + swap_seq(value)
    return value + lax.ppermute(value, "batch", [(b, b ^ bit) for b in range(16)])


def z_scatter(blocks):
    groups = [[q + 4 * z for z in range(4)] for q in range(4)]
    return lax.psum_scatter(
        blocks, "batch", scatter_dimension=0, tiled=True, axis_index_groups=groups
    )


def sc_sum(grad):
    return lax.psum_scatter(grad, "batch", scatter_dimension=0, tiled=True)


def per_device_pair(
    tokens,
    skip_parts,
    lengths,
    cotangent,
    skip_w,
    qkv_w,
    proj_w,
    fc1_w,
    fc2_w,
    skip_bias,
    ln1_gain,
    ln1_bias,
    proj_bias,
    ln2_gain,
    ln2_bias,
    fc1_bias,
    fc2_bias,
):
    count = tokens.shape[1]
    side = lax.axis_index("seq").astype(jnp.int32)
    index = side.reshape(1)
    at = jnp.stack([*place(), side])
    shared = jnp.where(side == 0, 256, 0)
    live = (
        (side * count + lax.broadcasted_iota(jnp.int32, (count, 1), 0)) < jnp.sum(lengths)
    ).astype(jnp.float32)

    parts = skip_parts.reshape(2, count, D)
    skip_far = swap_seq(take(parts, 0, 1 - side))
    tok_flat = tokens.reshape(count, D)

    q0 = core_pair(jnp.concatenate([qkv_w, proj_w], 1))
    s0 = skip_w
    s1, t0, s0c = next_z(s0), swap_y(s0), swap_core(s0)
    s1, t0 = tied(s1, t0)
    s2, t1 = next_z(s1), swap_y(s1)
    s2, t1, s1, q0, t0, s0c = tied(s2, t1, s1, q0, t0, s0c)
    s3, t2, q1 = next_z(s2), swap_y(s2), next_z(q0)
    s1c, t0c = swap_core(s1), swap_core(t0)
    s3, t2, s2, q0, t1, s1c, t0c = tied(s3, t2, s2, q0, t1, s1c, t0c)
    t3, r0 = swap_y(s3), swap_y(q0)
    s2c, s3c, t1c, t2c = swap_core(s2), swap_core(s3), swap_core(t1), swap_core(t2)
    s2c, s3c, t1c, t2c, t3, skip_far, q1, q0 = tied(s2c, s3c, t1c, t2c, t3, skip_far, q1, q0)
    q2, r1 = next_z(q1), swap_y(q1)
    w_skip = assemble(
        [s0, s1, s2, s3, t0, t1, t2, t3, s0c, s1c, s2c, s3c, t0c, t1c, t2c, swap_core(t3)], "rows"
    )
    skip_flat = b16(f32(take(parts, 0, side)) + f32(skip_far))
    h_zero = fwd_dot(tok_flat, w_skip[:D]) + fwd_dot(skip_flat, w_skip[D:]) + skip_bias
    normed_one, ln1_back = jax.vjp(layer_norm, h_zero, ln1_gain, ln1_bias)
    act_one = b16(normed_one)
    act_send = lax.dynamic_slice(act_one, (shared, 0), (REM, D))
    u0 = core_pair(fc1_w)
    q2, r1, r0, act_one, act_send, u0, q1 = tied(q2, r1, r0, act_one, act_send, u0, q1)
    act_far = swap_seq(act_send)
    q3, r2 = next_z(q2), swap_y(q2)
    q0c, q1c, r0c = swap_core(q0), swap_core(q1), swap_core(r0)
    q3, r2, u0, q2, q0c, q1c, r0c, r1 = tied(q3, r2, u0, q2, q0c, q1c, r0c, r1)
    r3, u1 = swap_y(q3), next_z(u0)
    q2c, q3c, r1c, r2c = swap_core(q2), swap_core(q3), swap_core(r1), swap_core(r2)
    r3, u1, q3, q2c, q3c, r1c, r2c = tied(r3, u1, q3, q2c, q3c, r1c, r2c)
    u2, v0 = next_z(u1), swap_y(u0)
    w_qkv, w_proj = assemble(
        [q0, q1, q2, q3, r0, r1, r2, r3, q0c, q1c, q2c, q3c, r0c, r1c, r2c, swap_core(r3)], "split"
    )
    u2, v0, w_qkv, w_proj, u1, u0, act_far = tied(u2, v0, w_qkv, w_proj, u1, u0, act_far)
    u3, v1 = next_z(u2), swap_y(u1)
    u0c, u1c, v0c = swap_core(u0), swap_core(u1), swap_core(v0)
    qkv = b16(fwd_dot(act_one, w_qkv))
    kv_far = b16(fwd_dot(act_far, w_qkv[:, D:]))
    u3, v1, u2, u0c, u1c, v0c, qkv, kv_far, fc2_w = tied(
        u3, v1, u2, u0c, u1c, v0c, qkv, kv_far, fc2_w
    )
    w_down = lax.all_gather(fc2_w, "batch", axis=0, tiled=True)
    v2, v3 = swap_y(u2), swap_y(u3)
    u2c, u3c, v1c = swap_core(u2), swap_core(u3), swap_core(v1)
    att, lse = attn_fwd(index, qkv, kv_far)
    v2, v3, u2c, u3c, v1c, att = tied(v2, v3, u2c, u3c, v1c, att)
    v2c, v3c = swap_core(v2), swap_core(v3)
    h_one = h_zero + fwd_dot(att, w_proj) + proj_bias
    normed_two, ln2_back = jax.vjp(layer_norm, h_one, ln2_gain, ln2_bias)
    act_two = b16(normed_two)
    w_up = assemble(
        [u0, u1, u2, u3, v0, v1, v2, v3, u0c, u1c, u2c, u3c, v0c, v1c, v2c, v3c], "ringhalves"
    )

    grad_two = f32(cotangent.reshape(count, D)) * live
    grad_low = b16(grad_two)
    gelu_low, slope, dn, dn_got = mlp_up(at, act_two, w_up, fc1_bias, grad_low)
    dn_got, gelu_low, slope, w_down = tied(dn_got, gelu_low, slope, w_down)
    dn_got = swap_core(dn_got)
    up, up_got, h_add, d_act_two, d_up_bias = mlp_back(
        at, act_two, grad_low, gelu_low, slope, w_up, w_down
    )
    dn, dn_got, up_got, d_act_two = tied(dn, dn_got, up_got, d_act_two)
    up_got = swap_core(up_got)
    dn_far = swap_seq(added(dn[1], dn_got[1]))
    dn = added(dn[0], dn_got[0])
    output = b16((h_one + h_add + fc2_bias) * live).reshape(1, count, D)
    d_h_one, d_ln2_gain, d_ln2_bias = ln2_back(d_act_two)
    d_h_one = d_h_one + grad_two
    proj_low = b16(d_h_one)
    up_got, proj_low, dn = tied(up_got, proj_low, dn)
    up_far = swap_y(added(up[1], up_got[1]))
    up = added(up[0], up_got[0])
    d_proj = b16(contract_rows(att, proj_low))
    d_att = b16(back_dot(proj_low, w_proj))
    d_att, d_proj, output, up = tied(d_att, d_proj, output, up)
    proj_part = sc_sum(d_proj)
    pick = (
        lax.broadcasted_iota(jnp.int32, (D, HEADS), 0) // HD
        == lax.broadcasted_iota(jnp.int32, (D, HEADS), 1)
    ).astype(jnp.float32)
    row_dot = lax.dot_general(
        pick, f32(d_att) * f32(att), (((0,), (1,)), ((), ())), precision=lax.Precision.HIGHEST
    )
    lse = lse[:, :HEADS].T
    d_qkv, d_far = attn_bwd(index, qkv, kv_far, d_att, lse, row_dot)
    far = b16(back_dot(d_far, w_qkv[:, D:]))
    far, d_qkv, d_far, dn, dn_far, up, up_far, proj_part = tied(
        far, d_qkv, d_far, dn, dn_far, up, up_far, proj_part
    )
    up = added(up, up_far)
    dn_send = [added(dn[1, 0:2], dn_far[1, 0:2]), added(dn[1, 2:4], dn_far[1, 2:4])]
    dn = added(dn[0], dn_far[0])
    far, d_qkv, d_far, dn, dn_send, up = tied(far, d_qkv, d_far, dn, dn_send, up)
    up_part = z_scatter(up.reshape(4 * 72, 4 * D))
    low_far = swap_seq(far[: REM // 2])
    dn_low = swap_y(dn_send[0])
    q, q_got = qkv_grad(at, act_one, act_far, d_qkv, d_far)
    d_qkv, q, q_got, low_far, dn_low, far = tied(d_qkv, q, q_got, low_far, dn_low, far)
    q_got = swap_core(q_got)
    high_far = swap_seq(far[REM // 2 :])
    dn_high = swap_y(dn_send[1])
    d_act_one = back_dot(d_qkv, w_qkv)
    q_got, d_act_one, high_far, dn_high = tied(q_got, d_act_one, high_far, dn_high)
    far = f32(jnp.concatenate([low_far, high_far], 0))
    here = lax.dynamic_slice(d_act_one, (shared, 0), (REM, D))
    d_act_one = lax.dynamic_update_slice(d_act_one, here + far, (shared, 0))
    q_send = [added(q[1, i], q_got[1, i]) for i in range(4)]
    q_y = {i: swap_y(q_send[i]) for i in (3, 2)}
    q = added(q[0], q_got[0])
    dn = added(dn, jnp.concatenate([dn_low, dn_high], 0))
    dn = [take(dn, 0, (place()[0] + i) % 4) for i in range(4)]
    dn_next = next_z(dn[3])
    d_h_zero, d_ln1_gain, d_ln1_bias = ln1_back(d_act_one)
    d_h_zero = d_h_zero + d_h_one
    zero_low = b16(d_h_zero)
    k, k_got = skip_back(at, tok_flat, skip_flat, zero_low)

    def onward(mine, got, so_far):
        return next_z(b16(f32(mine) + f32(got) + f32(so_far)))

    sums = jnp.concatenate(
        [
            jnp.sum(d_h_zero, axis=0),
            d_ln1_gain,
            d_ln1_bias,
            jnp.sum(d_h_one, axis=0),
            d_ln2_gain,
            d_ln2_bias,
            d_up_bias[0],
            jnp.sum(grad_two, axis=0),
        ]
    ).reshape(-1, 128)
    q_y[3], q_y[2], q, q_send, k, k_got, zero_low, sums, proj_part, dn_next, dn = tied(
        q_y[3], q_y[2], q, q_send, k, k_got, zero_low, sums, proj_part, dn_next, dn
    )
    dn_next = next_z(added(dn[2], dn_next))
    k_got = swap_core(k_got)
    q_next = next_z(added(q[3], q_y[3]))
    q_y[1] = swap_y(q_send[1])
    proj_far = swap_seq(proj_part)
    d_tokens = back_dot(zero_low, w_skip[:D]).reshape(1, count, D)
    sums = vector_step(sums, 1)
    q_next, q_y, k, k_got, sums, zero_low, d_tokens, proj_far, up_part, dn_next = tied(
        q_next, q_y, k, k_got, sums, zero_low, d_tokens, proj_far, up_part, dn_next
    )
    dn_next = next_z(added(dn[1], dn_next))
    q_next = onward(q[2], q_y[2], q_next)
    k_send = [added(k[1, i], k_got[1, i]) for i in range(4)]
    q_y[0] = swap_y(q_send[0])
    k_y = {3: swap_y(k_send[3])}
    k = added(k[0], k_got[0])
    up_far = swap_seq(up_part)
    out_proj = f32(proj_part) + f32(proj_far)
    d_skip = back_dot(zero_low, w_skip[D:]).reshape(1, count, D)
    sums = vector_step(sums, 0, "seq")
    q_next, q_y, k_y, k, k_send, sums, d_skip, up_far, dn_next = tied(
        q_next, q_y, k_y, k, k_send, sums, d_skip, up_far, dn_next
    )
    dn_part = added(dn[0], dn_next)
    dn_got = swap_seq(dn_part)
    q_next = onward(q[1], q_y[1], q_next)
    k_next = next_z(added(k[3], k_y[3]))
    k_y[2], k_y[1] = swap_y(k_send[2]), swap_y(k_send[1])
    out_up = f32(up_part) + f32(up_far)
    sums = vector_step(sums, 2)
    q_next, k_next, k_y, sums, dn_part, dn_got = tied(
        q_next, k_next, k_y, sums, dn_part, dn_got
    )
    out_down = by_side(side, dn_part, dn_got)
    q_sum = b16(f32(q[0]) + f32(q_y[0]) + f32(q_next))
    q_got = swap_seq(q_sum)
    k_next = onward(k[2], k_y[2], k_next)
    k_y[0] = swap_y(k_send[0])
    sums = vector_step(sums, 4)
    q_got, k_next, k_y, sums = tied(q_got, k_next, k_y, sums)
    out_qkv = f32(q_sum) + f32(q_got)
    k_next = onward(k[1], k_y[1], k_next)
    sums = vector_step(sums, 8)
    k_next, k_y, sums = tied(k_next, k_y, sums)
    k_sum = b16(f32(k[0]) + f32(k_y[0]) + f32(k_next))
    out_skip = f32(k_sum) + f32(swap_seq(k_sum))
    sums = sums.reshape(-1)
    starts = [0, D, 2 * D, 3 * D, 4 * D, 5 * D, 6 * D, 10 * D, 11 * D]
    sums = [sums[a:b] for a, b in zip(starts, starts[1:])]
    grads = (out_skip, out_qkv, out_proj, out_up, out_down)
    return (output, d_tokens, d_skip, *grads, *sums)


def solution(mesh):
    in_specs = (
        P("batch", "seq", None),
        P("seq", "batch", None, None),
        P("batch", None),
        P("batch", "seq", None),
        *(P("batch", None),) * 5,
        *(P(),) * 8,
    )
    out_specs = (*(P("batch", "seq", None),) * 3, *(P("batch", None),) * 5, *(P(),) * 8)
    pair = mesh.shape["batch"] == ROWS and mesh.shape["seq"] == 2
    return jax.shard_map(
        per_device_pair if pair else per_device,
        mesh=mesh,
        in_specs=in_specs,
        out_specs=out_specs,
        check_vma=False,

    )
```

```python
import math

import jax
import jax.numpy as jnp
from jax import lax
from jax.experimental import pallas as pl
from jax.experimental.pallas import tpu as pltpu
from jax.sharding import PartitionSpec as P

HEADS = 16
HD = 72
D = 1152
ROWS = 16
EPS = 1e-05

SCALE = HD**-0.5
C2 = SCALE * math.log2(math.e)
REM = 576
TILES = {
    0: [
        (256, 576, 258, 832, [(False, 256, 576, 258, 832), (True, 0, 464, 0, 452)]),
        (0, 272, 0, 258, [(False, 0, 272, 0, 258)]),
    ],
    1: [
        (0, 464, 0, 452, [(False, 0, 464, 0, 452), (True, 0, 576, 2, 576)]),
        (448, 272, 452, 710, [(False, 448, 272, 452, 710)]),
        (704, 128, 710, 832, [(False, 704, 128, 710, 832)]),
    ],
}
NT = (((1,), (1,)), ((), ()))


def dot(a, b, dims=(((1,), (0,)), ((), ()))):
    return lax.dot_general(a, b, dims, preferred_element_type=jnp.float32)


def split(n, step):
    return [(i, min(step, n - i)) for i in range(0, n, step)]


def full(shape):
    return pl.BlockSpec(shape, lambda h, s: (0,) * len(shape), pipeline_mode=pl.Buffered(1))


def pair_window(pair):
    tile = (2 * HD * pair) // 128
    first = 2 * HD * pair - 128 * tile
    lane = lax.broadcasted_iota(jnp.int32, (1, 256), 1)
    left = (lane >= first) & (lane < first + HD)
    right = (lane >= first + HD) & (lane < first + 2 * HD)
    base = pl.multiple_of(tile * 128, 128)

    def at(offset, row, count):
        return slice(row, row + count), pl.ds(pl.multiple_of(base + offset, 128), 256)

    return at, left, right


def stacked(value, left, right):
    zero = jnp.zeros_like(value)
    return jnp.concatenate([jnp.where(left, value, zero), jnp.where(right, value, zero)], 0)


def fwd_kernel(s_ref, qkv_ref, kvr_ref, o_ref, l_ref, *, qstep):
    pair = pl.program_id(0)

    @pl.when(pair == 0)
    def _():
        o_ref[...] = jnp.zeros_like(o_ref)
        l_ref[...] = jnp.zeros_like(l_ref)

    at, left, right = pair_window(pair)

    def chunk(r0, n, qv0, qv1, keys):
        q2 = stacked(qkv_ref[at(0, r0, n)], left, right)
        scores = []
        for far, k0, kc, kv0, kv1 in keys:
            k = kvr_ref[at(0, k0, kc)] if far else qkv_ref[at(D, k0, kc)]
            s = dot(q2, k, NT)
            if kv0 > k0 or kv1 < k0 + kc:
                kp = k0 + lax.broadcasted_iota(jnp.int32, (1, kc), 1)
                s = jnp.where((kp >= kv0) & (kp < kv1), s, -1e30)
            scores.append(s)
        top = jnp.max(scores[0], axis=1, keepdims=True)
        for s in scores[1:]:
            top = jnp.maximum(top, jnp.max(s, axis=1, keepdims=True))
        top = top * C2
        total, out = 0.0, 0.0
        for s, (far, k0, kc, _, _) in zip(scores, keys):
            p = jnp.exp2(s * C2 - top)
            total = total + jnp.sum(p, axis=1, keepdims=True)
            v = kvr_ref[at(D, k0, kc)] if far else qkv_ref[at(2 * D, k0, kc)]
            out = out + dot(p.astype(jnp.bfloat16), v)
        out = out * (1.0 / total)
        lse = top + jnp.log2(total)
        out = jnp.where(left, out[:n], out[n:]).astype(jnp.bfloat16)
        head = lax.broadcasted_iota(jnp.int32, (1, 128), 1) - 2 * pair
        lse = jnp.where(head == 0, lse[:n], lse[n:])
        keep, keep_l = left | right, (head == 0) | (head == 1)
        if r0 < qv0 or r0 + n > qv1:
            row = r0 + lax.broadcasted_iota(jnp.int32, (n, 1), 0)
            valid = (row >= qv0) & (row < qv1)
            keep, keep_l = keep & valid, keep_l & valid
        o_ref[at(0, r0, n)] = jnp.where(keep, out, o_ref[at(0, r0, n)])
        l_ref[r0 : r0 + n, :] = jnp.where(keep_l, lse, l_ref[r0 : r0 + n, :])

    for side in (0, 1):

        @pl.when(s_ref[0] == side)
        def _():
            for q0, nq, qv0, qv1, keys in TILES[side]:
                for a, n in split(nq, qstep):
                    chunk(q0 + a, n, qv0, qv1, keys)


def attn_fwd(sidx, qkv, kvr, qstep=288):
    return pl.pallas_call(
        lambda *r: fwd_kernel(*r, qstep=qstep),
        out_shape=(
            jax.ShapeDtypeStruct((832, D), jnp.bfloat16),
            jax.ShapeDtypeStruct((832, 128), jnp.float32),
        ),
        grid_spec=pltpu.PrefetchScalarGridSpec(
            num_scalar_prefetch=1,
            grid=(HEADS // 2,),
            in_specs=[full((832, 3 * D)), full((REM, 2 * D))],
            out_specs=(full((832, D)), full((832, 128))),
        ),
        compiler_params=pltpu.CompilerParams(vmem_limit_bytes=60 * 2**20),
        name="attn_fwd",
    )(sidx, qkv, kvr)


def bwd_kernel(s_ref, qkv_ref, kvr_ref, do_ref, lt_ref, dt_ref, dqkv_ref, dkvr_ref, *, kstep):
    pair = pl.program_id(0)

    @pl.when(pair == 0)
    def _():
        dqkv_ref[...] = jnp.zeros_like(dqkv_ref)
        dkvr_ref[...] = jnp.zeros_like(dkvr_ref)

    at, left, right = pair_window(pair)

    def tile(q0, nq, qv0, qv1, keys):
        q2 = stacked(qkv_ref[at(0, q0, nq)], left, right)
        do2 = stacked(do_ref[at(0, q0, nq)], left, right)

        def both(ref, mask):
            rows = []
            for h in (0, 1):
                row = ref[pl.ds(2 * pair + h, 1), :][:, q0 : q0 + nq]
                if mask and (qv0 > q0 or qv1 < q0 + nq):
                    qp = q0 + lax.broadcasted_iota(jnp.int32, (1, nq), 1)
                    row = jnp.where((qp >= qv0) & (qp < qv1), row, 1e30)
                rows.append(row)
            return jnp.concatenate(rows, 1)

        lse, row_dot = both(lt_ref, True), both(dt_ref, False)
        dqt = 0.0
        for far, first, count, kv0, kv1 in keys:
            for a, kc in split(count, kstep):
                k0 = first + a
                k = kvr_ref[at(0, k0, kc)] if far else qkv_ref[at(D, k0, kc)]
                v = kvr_ref[at(D, k0, kc)] if far else qkv_ref[at(2 * D, k0, kc)]
                p = jnp.exp2(dot(k, q2, NT) * C2 - lse)
                if kv0 > k0 or kv1 < k0 + kc:
                    kp = k0 + lax.broadcasted_iota(jnp.int32, (kc, 1), 0)
                    p = jnp.where((kp >= kv0) & (kp < kv1), p, 0.0)
                ds = (p * (dot(v, do2, NT) - row_dot)).astype(jnp.bfloat16)
                dv = dot(p.astype(jnp.bfloat16), do2).astype(jnp.bfloat16)
                dk = (dot(ds, q2) * SCALE).astype(jnp.bfloat16)
                if far:
                    dkvr_ref[at(0, k0, kc)] += dk
                    dkvr_ref[at(D, k0, kc)] += dv
                else:
                    dqkv_ref[at(D, k0, kc)] += dk
                    dqkv_ref[at(2 * D, k0, kc)] += dv
                dqt = dqt + dot(k.T, ds)
        dq = (dqt * SCALE).T
        dq = jnp.where(left, dq[:nq], jnp.where(right, dq[nq:], 0.0)).astype(jnp.bfloat16)
        dqkv_ref[at(0, q0, nq)] += dq

    for side in (0, 1):

        @pl.when(s_ref[0] == side)
        def _():
            for parts in TILES[side]:
                tile(*parts)


def attn_bwd(sidx, qkv, kvr, do, lt, dt, kstep=1024):
    return pl.pallas_call(
        lambda *r: bwd_kernel(*r, kstep=kstep),
        out_shape=(
            jax.ShapeDtypeStruct((832, 3 * D), jnp.bfloat16),
            jax.ShapeDtypeStruct((REM, 2 * D), jnp.bfloat16),
        ),
        grid_spec=pltpu.PrefetchScalarGridSpec(
            num_scalar_prefetch=1,
            grid=(HEADS // 2,),
            in_specs=[
                full((832, 3 * D)),
                full((REM, 2 * D)),
                full((832, D)),
                full((16, 832)),
                full((16, 832)),
            ],
            out_specs=(full((832, 3 * D)), full((REM, 2 * D))),
        ),
        compiler_params=pltpu.CompilerParams(vmem_limit_bytes=60 * 2**20),
        name="attn_bwd",
    )(sidx, qkv, kvr, do, lt, dt)


ERFC = (0.5 * 1.061405429, -0.5 * 1.453152027, 0.5 * 1.421413741, -0.5 * 0.284496736, 0.5 * 0.254829592)


def normal_cdf(u):
    expo = jnp.exp2(u * u * (-0.5 * math.log2(math.e)))
    below = 1.0 + (0.3275911 * math.sqrt(0.5)) * jnp.abs(u)
    step = pltpu.reciprocal(below, approx=True)
    step = step * (2.0 - below * step)
    tail = ERFC[0]
    for term in ERFC[1:]:
        tail = tail * step + term
    tail = tail * step * expo
    return jnp.where(u < 0.0, tail, 1.0 - tail), expo


def mlp_up(at, act, weight, bias, grad, tile=D, chunks=4):
    rows, width = act.shape[0], weight.shape[1]
    steps = width // tile
    size = rows // chunks

    def kernel(at, a_ref, w_ref, b_ref, e_ref, g_ref, d_ref, mine, other, held):
        t = pl.program_id(0)

        def forward():
            for i in range(chunks):
                part = slice(i * size, (i + 1) * size)
                u = dot(a_ref[part], w_ref[...]) + b_ref[...]
                phi, expo = normal_cdf(u)
                g = (u * phi).astype(jnp.bfloat16)
                g_ref[part] = g
                d_ref[part] = (phi + u * expo * (1.0 / math.sqrt(2.0 * math.pi))).astype(jnp.bfloat16)

        def keep():
            held[...] = g_ref[...].T

        def back():
            for yy in (0, 1):
                both = dot(held[yy * 576 : yy * 576 + 576], e_ref[...])
                low, high = both[:288], both[288:]
                yrel = yy + at[1] - 2 * yy * at[1]
                for ref, value in (
                    (mine, jnp.where(at[2] == 0, low, high)),
                    (other, jnp.where(at[2] == 0, high, low)),
                ):
                    value = value.astype(jnp.bfloat16)
                    ref[at[3], yrel, 0] = value[:144]
                    ref[1 - at[3], yrel, 0] = value[144:]

        @pl.when(t == 0)
        def _():
            forward()
            keep()

        @pl.when((t > 0) & (t < steps))
        def _():
            back()
            forward()
            keep()

        @pl.when(t == steps)
        def _():
            back()

    out = jax.ShapeDtypeStruct((rows, width), jnp.bfloat16)
    split = jax.ShapeDtypeStruct((2, 2, 4, 144, D), jnp.bfloat16)

    def now(t):
        return jnp.minimum(t, steps - 1)

    whole = pl.BlockSpec((rows, D), lambda t, at: (0, 0), pipeline_mode=pl.Buffered(1))
    by_column = pl.BlockSpec((rows, tile), lambda t, at: (0, now(t)))
    split_spec = pl.BlockSpec((2, 2, 1, 144, D), lambda t, at: (0, 0, jnp.maximum(t - 1, 0), 0, 0))
    return pl.pallas_call(
        kernel,
        out_shape=(out, out, split, split),
        grid_spec=pltpu.PrefetchScalarGridSpec(
            num_scalar_prefetch=1,
            grid=(steps + 1,),
            in_specs=[
                whole,
                pl.BlockSpec((D, tile), lambda t, at: (0, now(t))),
                pl.BlockSpec((1, tile), lambda t, at: (0, now(t))),
                whole,
            ],
            out_specs=(by_column, by_column, split_spec, split_spec),
            scratch_shapes=[pltpu.VMEM((tile, rows), jnp.bfloat16)],
        ),
        compiler_params=pltpu.CompilerParams(vmem_limit_bytes=60 * 2**20),
        name="mlp_up",
    )(at, act, weight, bias.reshape(1, width), grad)


def ordered_transpose(at, value, held, ring=True):
    held[...] = value.astype(jnp.float32).T.reshape(held.shape)
    blocks = []
    for crel in (0, 1):
        for yrel in (0, 1):
            for zrel in range(4):
                zz = lax.rem(at[0] + zrel, 4) if ring else zrel
                yy = at[1] + yrel - 2 * at[1] * yrel
                cc = at[2] + crel - 2 * at[2] * crel
                blocks.append(held[zz * 4 + yy * 2 + cc])
    return jnp.concatenate(blocks, 0).astype(jnp.bfloat16)


def mlp_back(at, act, grad, gelu, slope, w_up, w_down, halves=1, tile=768):
    rows, width = gelu.shape
    half = rows // halves

    def kernel(at, a_ref, e_ref, g_ref, s_ref, wu_ref, wd_ref, *refs):
        mine, other, h_ref, c_ref, b_ref, a_t, du_ref, held = refs

        @pl.when(pl.program_id(0) == 0)
        def _():
            a_t[...] = ordered_transpose(at, a_ref[...], held, ring=False)
            h_ref[...] = jnp.zeros_like(h_ref)
            c_ref[...] = jnp.zeros_like(c_ref)

        bias = None
        for i in range(halves):
            part = slice(i * half, (i + 1) * half)
            du = dot(e_ref[part], wd_ref[...], NT) * s_ref[part].astype(jnp.float32)
            total = jnp.sum(du, axis=0, keepdims=True)
            bias = total if bias is None else bias + total
            du = du.astype(jnp.bfloat16)
            du_ref[part] = du
            h_ref[part] += dot(g_ref[part], wd_ref[...])
            c_ref[part] += dot(du, wu_ref[...], NT)
        b_ref[...] = bias
        for i, ref in ((0, mine), (1, other)):
            both = dot(a_t[i * 576 : i * 576 + 576], du_ref[...])
            for j in range(8):
                ref[j // 4, j % 4] = both[j * 72 : j * 72 + 72].astype(jnp.bfloat16)

    once = pl.Buffered(1)
    whole = jax.ShapeDtypeStruct((rows, D), jnp.float32)
    split = jax.ShapeDtypeStruct((2, 4, 72, width), jnp.bfloat16)
    split_spec = pl.BlockSpec((2, 4, 72, tile), lambda t, at: (0, 0, 0, t))
    whole_spec = pl.BlockSpec((rows, D), lambda t, at: (0, 0), pipeline_mode=once)
    by_column = pl.BlockSpec((rows, tile), lambda t, at: (0, t))
    weight_column = pl.BlockSpec((D, tile), lambda t, at: (0, t))
    return pl.pallas_call(
        kernel,
        out_shape=(
            split,
            split,
            whole,
            whole,
            jax.ShapeDtypeStruct((1, width), jnp.float32),
        ),
        grid_spec=pltpu.PrefetchScalarGridSpec(
            num_scalar_prefetch=1,
            grid=(width // tile,),
            in_specs=[
                whole_spec,
                whole_spec,
                by_column,
                by_column,
                weight_column,
                pl.BlockSpec((tile, D), lambda t, at: (t, 0)),
            ],
            out_specs=(
                split_spec,
                split_spec,
                whole_spec,
                whole_spec,
                pl.BlockSpec((1, tile), lambda t, at: (0, t)),
            ),
            scratch_shapes=[
                pltpu.VMEM((D, rows), jnp.bfloat16),
                pltpu.VMEM((rows, tile), jnp.bfloat16),
                pltpu.VMEM((16, 72, rows), jnp.float32),
            ],
        ),
        compiler_params=pltpu.CompilerParams(vmem_limit_bytes=62 * 2**20),
        name="mlp_back",
    )(at, act, grad, gelu, slope, w_up, w_down)


def qkv_grad(at, act, act_far, grad, grad_far):
    rows, far = act.shape[0], act_far.shape[0]

    def kernel(at, a_ref, f_ref, g_ref, h_ref, mine, other, a_t, f_t, held, held_far):
        t = pl.program_id(0)

        @pl.when(t == 0)
        def _():
            a_t[...] = ordered_transpose(at, a_ref[...], held)
            f_t[...] = ordered_transpose(at, f_ref[...], held_far)

        away = jnp.where(t > 0, h_ref[...], jnp.zeros_like(h_ref))
        for i, ref in ((0, mine), (1, other)):
            part = slice(i * 576, (i + 1) * 576)
            both = dot(a_t[part], g_ref[...]) + dot(f_t[part], away)
            for j in range(8):
                ref[j // 4, j % 4] = both[j * 72 : j * 72 + 72].astype(jnp.bfloat16)

    once = pl.Buffered(1)
    split = jax.ShapeDtypeStruct((2, 4, 72, 3 * D), jnp.bfloat16)
    split_spec = pl.BlockSpec((2, 4, 72, D), lambda t, at: (0, 0, 0, t))
    return pl.pallas_call(
        kernel,
        out_shape=(split, split),
        grid_spec=pltpu.PrefetchScalarGridSpec(
            num_scalar_prefetch=1,
            grid=(3,),
            in_specs=[
                pl.BlockSpec((rows, D), lambda t, at: (0, 0), pipeline_mode=once),
                pl.BlockSpec((far, D), lambda t, at: (0, 0), pipeline_mode=once),
                pl.BlockSpec((rows, D), lambda t, at: (0, t)),
                pl.BlockSpec((far, D), lambda t, at: (0, jnp.maximum(t - 1, 0))),
            ],
            out_specs=(split_spec, split_spec),
            scratch_shapes=[
                pltpu.VMEM((D, rows), jnp.bfloat16),
                pltpu.VMEM((D, far), jnp.bfloat16),
                pltpu.VMEM((16, 72, rows), jnp.float32),
                pltpu.VMEM((16, 72, far), jnp.float32),
            ],
        ),
        compiler_params=pltpu.CompilerParams(vmem_limit_bytes=60 * 2**20),
        name="qkv_grad",
    )(at, act, act_far, grad, grad_far)


def skip_back(at, tok, skip, grad):
    rows = tok.shape[0]

    def kernel(at, t_ref, s_ref, g_ref, mine, other, in_t):
        i = pl.program_id(0)

        @pl.when(i == 0)
        def _():
            in_t[0:D] = t_ref[...].T
            in_t[D:] = s_ref[...].T

        first = pl.multiple_of(lax.rem(at[0] + i, 4) * 576, 16)
        both = dot(in_t[pl.ds(first, 576)], g_ref[...])
        for yy in (0, 1):
            low, high = both[yy * 288 : yy * 288 + 144], both[yy * 288 + 144 : yy * 288 + 288]
            yrel = yy + at[1] - 2 * yy * at[1]
            mine[yrel, 0] = jnp.where(at[2] == 0, low, high).astype(jnp.bfloat16)
            other[yrel, 0] = jnp.where(at[2] == 0, high, low).astype(jnp.bfloat16)

    split = jax.ShapeDtypeStruct((2, 4, 144, D), jnp.bfloat16)
    split_spec = pl.BlockSpec((2, 1, 144, D), lambda t, at: (0, t, 0, 0))
    whole_spec = pl.BlockSpec((rows, D), lambda t, at: (0, 0), pipeline_mode=pl.Buffered(1))
    return pl.pallas_call(
        kernel,
        out_shape=(split, split),
        grid_spec=pltpu.PrefetchScalarGridSpec(
            num_scalar_prefetch=1,
            grid=(4,),
            in_specs=[whole_spec] * 3,
            out_specs=(split_spec, split_spec),
            scratch_shapes=[pltpu.VMEM((2 * D, rows), jnp.bfloat16)],
        ),
        compiler_params=pltpu.CompilerParams(vmem_limit_bytes=40 * 2**20),
        name="skip_back",
    )(at, tok, skip, grad)


def layer_norm(hidden, gain, shift):
    centred = hidden - jnp.mean(hidden, axis=-1, keepdims=True)
    spread = jnp.mean(centred * centred, axis=-1, keepdims=True)
    return centred * lax.rsqrt(spread + EPS) * gain + shift


def exact_gelu(value):
    return jax.nn.gelu(value, approximate=False)


def segment_ids(offsets, positions):
    hits = (positions[None, :, None] >= offsets[:, None, :]).astype(jnp.int32)
    return jnp.sum(hits, axis=-1)


def fwd_dot(left, right):
    return jnp.dot(left, right, preferred_element_type=jnp.float32)


def contract_rows(left, right):
    return lax.dot_general(
        left, right, (((0,), (0,)), ((), ())), preferred_element_type=jnp.float32
    )


def back_dot(grad_rows, weight):
    return lax.dot_general(
        grad_rows, weight, (((1,), (1,)), ((), ())), preferred_element_type=jnp.float32
    )


class RowAttention:
    def __init__(self, qkv_all, offsets, row_count, local_len):
        self.row_count, self.local_len = row_count, local_len
        self.row_len = local_len * lax.axis_size("seq")
        self.offsets = offsets
        first_pos = lax.axis_index("seq") * local_len
        self.query_seg = segment_ids(offsets, first_pos + jnp.arange(local_len, dtype=jnp.int32))
        self.scale = HD ** (-0.5)
        self.queries = qkv_all[:, :D].reshape(row_count, local_len, HEADS, HD)
        keyvals = qkv_all[:, D:].reshape(row_count, local_len, 2 * D)
        self.kv = lax.all_gather(keyvals, "seq", axis=1, tiled=True)

    def block(self, first, size):
        kv = lax.dynamic_slice_in_dim(self.kv, first, size, 1)
        shape = (self.row_count, size, HEADS, HD)
        key_seg = segment_ids(self.offsets, first + jnp.arange(size, dtype=jnp.int32))
        same = self.query_seg[:, :, None, None] == key_seg[:, None, None, :]
        return kv[:, :, :D].reshape(shape), kv[:, :, D:].reshape(shape), same

    def scores(self, keys):
        return (
            jnp.einsum("rthd,rkhd->rthk", self.queries, keys, preferred_element_type=jnp.float32)
            * self.scale
        )

    def forward(self):
        keys, values, same = self.block(0, self.row_len)
        scores = jnp.where(same, self.scores(keys), -1e30)
        top = jnp.max(scores, axis=-1)
        expo = jnp.where(same, jnp.exp(scores - top[..., None]), 0.0)
        norm = jnp.sum(expo, axis=-1)
        weighted = jnp.einsum(
            "rthk,rkhd->rthd",
            expo.astype(jnp.bfloat16),
            values,
            preferred_element_type=jnp.float32,
        )
        self.attended = weighted / norm[..., None]
        self.log_total = top + jnp.log(norm)
        return self.attended.reshape(-1, D).astype(jnp.bfloat16)

    def backward(self, d_att):
        rows, length = self.row_count, self.local_len
        d_att = d_att.reshape(rows, length, HEADS, HD)
        row_dot = jnp.sum(d_att.astype(jnp.float32) * self.attended, axis=-1)
        size = math.gcd(self.row_len, 512)

        def step(index, totals):
            d_query, d_kv = totals
            keys, values, same = self.block(index * size, size)
            weights = jnp.where(same, jnp.exp(self.scores(keys) - self.log_total[..., None]), 0.0)
            d_weights = jnp.einsum(
                "rthd,rkhd->rthk", d_att, values, preferred_element_type=jnp.float32
            )
            d_scores = (weights * (d_weights - row_dot[..., None])).astype(jnp.bfloat16)
            d_query = d_query + self.scale * jnp.einsum(
                "rthk,rkhd->rthd", d_scores, keys, preferred_element_type=jnp.float32
            )
            d_key = self.scale * jnp.einsum(
                "rthk,rthd->rkhd", d_scores, self.queries, preferred_element_type=jnp.float32
            )
            d_value = jnp.einsum(
                "rthk,rthd->rkhd",
                weights.astype(jnp.bfloat16),
                d_att,
                preferred_element_type=jnp.float32,
            )
            both = jnp.concatenate(
                [d_key.reshape(rows, size, D), d_value.reshape(rows, size, D)], axis=2
            )
            return d_query, lax.dynamic_update_slice_in_dim(d_kv, both, index * size, 1)

        start = (
            jnp.zeros((rows, length, HEADS, HD), jnp.float32),
            jnp.zeros((rows, self.row_len, 2 * D), jnp.float32),
        )
        d_query, d_kv = lax.fori_loop(0, self.row_len // size, step, start)
        d_kv = lax.psum_scatter(
            d_kv.astype(jnp.bfloat16), "seq", scatter_dimension=1, tiled=True
        ).astype(jnp.float32)
        return jnp.concatenate(
            [d_query.reshape(rows * length, D), d_kv.reshape(rows * length, 2 * D)], axis=1
        ).astype(jnp.bfloat16)


def per_device(
    tokens,
    skip_parts,
    lengths,
    cotangent,
    skip_w,
    qkv_w,
    proj_w,
    fc1_w,
    fc2_w,
    skip_bias,
    ln1_gain,
    ln1_bias,
    proj_bias,
    ln2_gain,
    ln2_bias,
    fc1_bias,
    fc2_bias,
):
    row_count, local_len, features = tokens.shape
    tok_count = row_count * local_len
    offsets = jnp.cumsum(lengths, axis=1)
    first_pos = lax.axis_index("seq") * local_len
    query_seg = segment_ids(offsets, first_pos + jnp.arange(local_len, dtype=jnp.int32))
    live_mask = (query_seg < lengths.shape[1]).astype(jnp.float32).reshape(tok_count, 1)
    skip_rows = lax.psum_scatter(skip_parts[0], "seq", scatter_dimension=1, tiled=True)
    w_skip, w_qkv, w_proj, w_up, w_down = (
        lax.all_gather(w, "batch", axis=0, tiled=True)
        for w in (skip_w, qkv_w, proj_w, fc1_w, fc2_w)
    )
    tok_flat = tokens.reshape(tok_count, features)
    skip_flat = skip_rows.reshape(tok_count, features)
    h_zero = (
        fwd_dot(tok_flat, w_skip[:features]) + fwd_dot(skip_flat, w_skip[features:]) + skip_bias
    )
    normed_one, ln1_back = jax.vjp(layer_norm, h_zero, ln1_gain, ln1_bias)
    act_one = normed_one.astype(jnp.bfloat16)
    qkv_all = fwd_dot(act_one, w_qkv).astype(jnp.bfloat16)
    attention = RowAttention(qkv_all, offsets, row_count, local_len)
    att_low = attention.forward()
    h_one = h_zero + fwd_dot(att_low, w_proj) + proj_bias
    normed_two, ln2_back = jax.vjp(layer_norm, h_one, ln2_gain, ln2_bias)
    act_two = normed_two.astype(jnp.bfloat16)
    up_proj = fwd_dot(act_two, w_up) + fc1_bias
    gelu_out, gelu_back = jax.vjp(exact_gelu, up_proj)
    gelu_low = gelu_out.astype(jnp.bfloat16)
    h_two = h_one + fwd_dot(gelu_low, w_down) + fc2_bias
    output = (h_two * live_mask).astype(jnp.bfloat16).reshape(row_count, local_len, features)
    grad_two = cotangent.reshape(tok_count, features).astype(jnp.float32) * live_mask
    grad_low = grad_two.astype(jnp.bfloat16)
    d_w_down = contract_rows(gelu_low, grad_low)
    d_gelu = back_dot(grad_low, w_down)
    d_up = gelu_back(d_gelu)[0]
    up_low = d_up.astype(jnp.bfloat16)
    d_w_up = contract_rows(act_two, up_low)
    d_act_two = back_dot(up_low, w_up)
    d_h_one, d_ln2_gain, d_ln2_bias = ln2_back(d_act_two)
    d_h_one = d_h_one + grad_two
    proj_low = d_h_one.astype(jnp.bfloat16)
    d_w_proj = contract_rows(att_low, proj_low)
    d_att = back_dot(proj_low, w_proj).astype(jnp.bfloat16)
    d_qkv = attention.backward(d_att)
    d_w_qkv = contract_rows(act_one, d_qkv)
    d_act_one = back_dot(d_qkv, w_qkv)
    d_h_zero, d_ln1_gain, d_ln1_bias = ln1_back(d_act_one)
    d_h_zero = d_h_zero + d_h_one
    zero_low = d_h_zero.astype(jnp.bfloat16)
    d_w_skip = jnp.concatenate(
        [contract_rows(tok_flat, zero_low), contract_rows(skip_flat, zero_low)], axis=0
    )
    d_tokens = back_dot(zero_low, w_skip[:features]).reshape(row_count, local_len, features)
    d_skip = back_dot(zero_low, w_skip[features:]).reshape(row_count, local_len, features)
    vector_sums = lax.psum(
        (
            jnp.sum(d_h_zero, axis=0),
            d_ln1_gain,
            d_ln1_bias,
            jnp.sum(d_h_one, axis=0),
            d_ln2_gain,
            d_ln2_bias,
            jnp.sum(d_up, axis=0),
            jnp.sum(grad_two, axis=0),
        ),
        ("batch", "seq"),
    )
    weight_grads = tuple(
        lax.psum(
            lax.psum_scatter(
                grad.astype(jnp.bfloat16), "batch", scatter_dimension=0, tiled=True
            ),
            "seq",
        ).astype(jnp.float32)
        for grad in (d_w_skip, d_w_qkv, d_w_proj, d_w_up, d_w_down)
    )
    return (output, d_tokens, d_skip, *weight_grads, *vector_sums)


YSW = [(b, b ^ 2) for b in range(16)]
CSW = [(b, b ^ 1) for b in range(16)]
ZUP = [(b, (b + 4) % 16) for b in range(16)]


def swap_y(v):
    return lax.ppermute(v, "batch", YSW)


def swap_core(v):
    return lax.ppermute(v, "batch", CSW)


def next_z(v):
    return lax.ppermute(v, "batch", ZUP)


def swap_seq(v):
    return lax.ppermute(v, "seq", [(0, 1), (1, 0)])


def place():
    b = lax.axis_index("batch").astype(jnp.int32)
    return b // 4, (b // 2) % 2, b % 2


def f32(v):
    return v.astype(jnp.float32)


def b16(v):
    return v.astype(jnp.bfloat16)


def core_pair(shard):
    core = place()[2]
    half = shard.shape[1] // 2
    low, high = shard[:, :half], shard[:, half:]
    keep = jnp.where(core == 0, low, high)
    got = swap_core(jnp.where(core == 0, high, low))
    return jnp.where(
        core == 0, jnp.concatenate([keep, got], 0), jnp.concatenate([got, keep], 0)
    )


def tied(*values):
    return lax.optimization_barrier(values)


def with_core(own):
    return own + [swap_core(v) for v in own]


def assemble(pieces, kind):
    rows, cols = pieces[0].shape
    split, halves, paired = kind == "split", kind.endswith("halves"), kind == "halves"
    if split:
        shapes = [(8 * rows, 3 * D), (8 * rows, D)]
    elif halves:
        shapes = [(8 * rows, 2 * cols)]
    else:
        shapes = [(16 * rows, cols)]

    def kernel(at, *refs):
        ins, outs, (held, came, left) = refs[:16], refs[16:-3], refs[-3:]
        z, y, c, x = at[0], at[1], at[2], at[3]
        loads = [pltpu.make_async_copy(ins[j], held.at[j], came.at[j]) for j in range(16)]
        for load in loads:
            load.start()
        waits = []
        for j in range(16):
            core = c if j < 8 else 1 - c
            yy = y if j % 8 < 4 else 1 - y
            away = j % 4
            if paired and j % 8 in (4, 5):
                away = away + x - 2 * away * x
            zz = lax.rem(z - away + 4, 4)
            loads[j].wait()
            if not split:
                if halves:
                    first = pl.multiple_of((zz * 2 + yy) * rows, 16)
                    at_cols = pl.ds(pl.multiple_of(core * cols, 128), cols)
                    target = outs[0].at[pl.ds(first, rows), at_cols]
                else:
                    first = pl.multiple_of((zz * 4 + yy * 2 + core) * rows, 16)
                    target = outs[0].at[pl.ds(first, rows), :]
                store = pltpu.make_async_copy(held.at[j], target, left.at[j])
                store.start()
                waits.append((None, store))
                continue
            at_rows = pl.ds(pl.multiple_of((zz * 2 + yy) * rows, 16), rows)
            at_cols = pl.ds(pl.multiple_of(core * (2 * D), 128), D)
            store = pltpu.make_async_copy(
                held.at[j, :, pl.ds(0, D)], outs[0].at[at_rows, at_cols], left.at[j]
            )
            store.start()
            waits.append((None, store))
            for which, target in ((0, outs[0].at[at_rows, pl.ds(D, D)]), (1, outs[1].at[at_rows, :])):
                store = pltpu.make_async_copy(held.at[j, :, pl.ds(D, D)], target, left.at[16 + j])
                pl.when(core == which)(store.start)
                waits.append((core == which, store))
        for needed, store in waits:
            if needed is None:
                store.wait()
            else:
                pl.when(needed)(store.wait)

    out = pl.pallas_call(
        kernel,
        out_shape=[jax.ShapeDtypeStruct(v, pieces[0].dtype) for v in shapes],
        in_specs=[pl.BlockSpec(memory_space=pltpu.SMEM)]
        + [pl.BlockSpec(memory_space=pl.ANY)] * 16,
        out_specs=[pl.BlockSpec(memory_space=pl.ANY)] * len(shapes),
        scratch_shapes=[
            pltpu.VMEM((16, rows, cols), pieces[0].dtype),
            pltpu.SemaphoreType.DMA((16,)),
            pltpu.SemaphoreType.DMA((32,)),
        ],
        compiler_params=pltpu.CompilerParams(vmem_limit_bytes=16 * 2**20),
        name="assemble",
    )(jnp.stack([*place(), lax.axis_index("seq").astype(jnp.int32)]), *pieces)
    return out if split else out[0]


def take(v, axis, index):
    return lax.dynamic_index_in_dim(v, index, axis, keepdims=False)


def added(left, right):
    return b16(f32(left) + f32(right))


def by_side(side, own, other):
    own, other = f32(own), f32(other)
    return jnp.where(
        side == 0, jnp.concatenate([own, other], 0), jnp.concatenate([other, own], 0)
    )


def vector_step(value, bit, axis="batch"):
    if axis == "seq":
        return value + swap_seq(value)
    return value + lax.ppermute(value, "batch", [(b, b ^ bit) for b in range(16)])


def z_scatter(blocks):
    groups = [[q + 4 * z for z in range(4)] for q in range(4)]
    return lax.psum_scatter(
        blocks, "batch", scatter_dimension=0, tiled=True, axis_index_groups=groups
    )


def sc_sum(grad):
    return lax.psum_scatter(grad, "batch", scatter_dimension=0, tiled=True)


def per_device_pair(
    tokens,
    skip_parts,
    lengths,
    cotangent,
    skip_w,
    qkv_w,
    proj_w,
    fc1_w,
    fc2_w,
    skip_bias,
    ln1_gain,
    ln1_bias,
    proj_bias,
    ln2_gain,
    ln2_bias,
    fc1_bias,
    fc2_bias,
):
    count = tokens.shape[1]
    side = lax.axis_index("seq").astype(jnp.int32)
    index = side.reshape(1)
    at = jnp.stack([*place(), side])
    shared = jnp.where(side == 0, 256, 0)
    live = (
        (side * count + lax.broadcasted_iota(jnp.int32, (count, 1), 0)) < jnp.sum(lengths)
    ).astype(jnp.float32)

    parts = skip_parts.reshape(2, count, D)
    skip_far = swap_seq(take(parts, 0, 1 - side))
    tok_flat = tokens.reshape(count, D)

    q0 = core_pair(jnp.concatenate([qkv_w, proj_w], 1))
    s0 = skip_w
    s1, t0, s0c = next_z(s0), swap_y(s0), swap_core(s0)
    s1, t0 = tied(s1, t0)
    s2, t1 = next_z(s1), swap_y(s1)
    s2, t1, s1, q0, t0, s0c = tied(s2, t1, s1, q0, t0, s0c)
    s3, t2, q1 = next_z(s2), swap_y(s2), next_z(q0)
    s1c, t0c = swap_core(s1), swap_core(t0)
    s3, t2, s2, q0, t1, s1c, t0c = tied(s3, t2, s2, q0, t1, s1c, t0c)
    t3, r0 = swap_y(s3), swap_y(q0)
    s2c, s3c, t1c, t2c = swap_core(s2), swap_core(s3), swap_core(t1), swap_core(t2)
    s2c, s3c, t1c, t2c, t3, skip_far, q1, q0 = tied(s2c, s3c, t1c, t2c, t3, skip_far, q1, q0)
    q2, r1 = next_z(q1), swap_y(q1)
    w_skip = assemble(
        [s0, s1, s2, s3, t0, t1, t2, t3, s0c, s1c, s2c, s3c, t0c, t1c, t2c, swap_core(t3)], "rows"
    )
    skip_flat = b16(f32(take(parts, 0, side)) + f32(skip_far))
    h_zero = fwd_dot(tok_flat, w_skip[:D]) + fwd_dot(skip_flat, w_skip[D:]) + skip_bias
    normed_one, ln1_back = jax.vjp(layer_norm, h_zero, ln1_gain, ln1_bias)
    act_one = b16(normed_one)
    act_send = lax.dynamic_slice(act_one, (shared, 0), (REM, D))
    u0 = core_pair(fc1_w)
    q2, r1, r0, act_one, act_send, u0, q1 = tied(q2, r1, r0, act_one, act_send, u0, q1)
    act_far = swap_seq(act_send)
    q3, r2 = next_z(q2), swap_y(q2)
    q0c, q1c, r0c = swap_core(q0), swap_core(q1), swap_core(r0)
    q3, r2, u0, q2, q0c, q1c, r0c, r1 = tied(q3, r2, u0, q2, q0c, q1c, r0c, r1)
    r3, u1 = swap_y(q3), next_z(u0)
    q2c, q3c, r1c, r2c = swap_core(q2), swap_core(q3), swap_core(r1), swap_core(r2)
    r3, u1, q3, q2c, q3c, r1c, r2c = tied(r3, u1, q3, q2c, q3c, r1c, r2c)
    u2, v0 = next_z(u1), swap_y(u0)
    w_qkv, w_proj = assemble(
        [q0, q1, q2, q3, r0, r1, r2, r3, q0c, q1c, q2c, q3c, r0c, r1c, r2c, swap_core(r3)], "split"
    )
    u2, v0, w_qkv, w_proj, u1, u0, act_far = tied(u2, v0, w_qkv, w_proj, u1, u0, act_far)
    u3, v1 = next_z(u2), swap_y(u1)
    u0c, u1c, v0c = swap_core(u0), swap_core(u1), swap_core(v0)
    qkv = b16(fwd_dot(act_one, w_qkv))
    kv_far = b16(fwd_dot(act_far, w_qkv[:, D:]))
    u3, v1, u2, u0c, u1c, v0c, qkv, kv_far, fc2_w = tied(
        u3, v1, u2, u0c, u1c, v0c, qkv, kv_far, fc2_w
    )
    w_down = lax.all_gather(fc2_w, "batch", axis=0, tiled=True)
    v2, v3 = swap_y(u2), swap_y(u3)
    u2c, u3c, v1c = swap_core(u2), swap_core(u3), swap_core(v1)
    att, lse = attn_fwd(index, qkv, kv_far)
    v2, v3, u2c, u3c, v1c, att = tied(v2, v3, u2c, u3c, v1c, att)
    v2c, v3c = swap_core(v2), swap_core(v3)
    h_one = h_zero + fwd_dot(att, w_proj) + proj_bias
    normed_two, ln2_back = jax.vjp(layer_norm, h_one, ln2_gain, ln2_bias)
    act_two = b16(normed_two)
    w_up = assemble(
        [u0, u1, u2, u3, v0, v1, v2, v3, u0c, u1c, u2c, u3c, v0c, v1c, v2c, v3c], "ringhalves"
    )

    grad_two = f32(cotangent.reshape(count, D)) * live
    grad_low = b16(grad_two)
    gelu_low, slope, dn, dn_got = mlp_up(at, act_two, w_up, fc1_bias, grad_low)
    dn_got, gelu_low, slope, w_down = tied(dn_got, gelu_low, slope, w_down)
    dn_got = swap_core(dn_got)
    up, up_got, h_add, d_act_two, d_up_bias = mlp_back(
        at, act_two, grad_low, gelu_low, slope, w_up, w_down
    )
    dn, dn_got, up_got, d_act_two = tied(dn, dn_got, up_got, d_act_two)
    up_got = swap_core(up_got)
    dn_far = swap_seq(added(dn[1], dn_got[1]))
    dn = added(dn[0], dn_got[0])
    output = b16((h_one + h_add + fc2_bias) * live).reshape(1, count, D)
    d_h_one, d_ln2_gain, d_ln2_bias = ln2_back(d_act_two)
    d_h_one = d_h_one + grad_two
    proj_low = b16(d_h_one)
    up_got, proj_low, dn = tied(up_got, proj_low, dn)
    up_far = swap_y(added(up[1], up_got[1]))
    up = added(up[0], up_got[0])
    d_proj = b16(contract_rows(att, proj_low))
    d_att = b16(back_dot(proj_low, w_proj))
    d_att, d_proj, output, up = tied(d_att, d_proj, output, up)
    proj_part = sc_sum(d_proj)
    pick = (
        lax.broadcasted_iota(jnp.int32, (D, HEADS), 0) // HD
        == lax.broadcasted_iota(jnp.int32, (D, HEADS), 1)
    ).astype(jnp.float32)
    row_dot = lax.dot_general(
        pick, f32(d_att) * f32(att), (((0,), (1,)), ((), ())), precision=lax.Precision.HIGHEST
    )
    lse = lse[:, :HEADS].T
    d_qkv, d_far = attn_bwd(index, qkv, kv_far, d_att, lse, row_dot)
    far = b16(back_dot(d_far, w_qkv[:, D:]))
    far, d_qkv, d_far, dn, dn_far = tied(far, d_qkv, d_far, dn, dn_far)
    dn_send = [added(dn[1, 0:2], dn_far[1, 0:2]), added(dn[1, 2:4], dn_far[1, 2:4])]
    dn = added(dn[0], dn_far[0])
    dn, dn_send, up_far = tied(dn, dn_send, up_far)
    up = added(up, up_far)
    far, d_qkv, d_far, dn, dn_send, up = tied(far, d_qkv, d_far, dn, dn_send, up)
    up_part = z_scatter(up.reshape(4 * 72, 4 * D))
    low_far = swap_seq(far[: REM // 2])
    dn_low = swap_y(dn_send[0])
    q, q_got = qkv_grad(at, act_one, act_far, d_qkv, d_far)
    d_qkv, q, q_got, low_far, dn_low, far = tied(d_qkv, q, q_got, low_far, dn_low, far)
    q_got = swap_core(q_got)
    high_far = swap_seq(far[REM // 2 :])
    dn_high = swap_y(dn_send[1])
    d_act_one = back_dot(d_qkv, w_qkv)
    q_got, d_act_one, high_far, dn_high = tied(q_got, d_act_one, high_far, dn_high)
    far = f32(jnp.concatenate([low_far, high_far], 0))
    here = lax.dynamic_slice(d_act_one, (shared, 0), (REM, D))
    d_act_one = lax.dynamic_update_slice(d_act_one, here + far, (shared, 0))
    q_send = [added(q[1, i], q_got[1, i]) for i in range(4)]
    q_y = {i: swap_y(q_send[i]) for i in (3, 2)}
    q = added(q[0], q_got[0])
    dn = added(dn, jnp.concatenate([dn_low, dn_high], 0))
    dn = [take(dn, 0, (place()[0] + i) % 4) for i in range(4)]
    dn_next = next_z(dn[3])
    d_h_zero, d_ln1_gain, d_ln1_bias = ln1_back(d_act_one)
    d_h_zero = d_h_zero + d_h_one
    zero_low = b16(d_h_zero)
    k, k_got = skip_back(at, tok_flat, skip_flat, zero_low)

    def onward(mine, got, so_far):
        return next_z(b16(f32(mine) + f32(got) + f32(so_far)))

    sums = jnp.concatenate(
        [
            jnp.sum(d_h_zero, axis=0),
            d_ln1_gain,
            d_ln1_bias,
            jnp.sum(d_h_one, axis=0),
            d_ln2_gain,
            d_ln2_bias,
            d_up_bias[0],
            jnp.sum(grad_two, axis=0),
        ]
    ).reshape(-1, 128)
    q_y[3], q_y[2], q, q_send, k, k_got, zero_low, sums, proj_part, dn_next, dn = tied(
        q_y[3], q_y[2], q, q_send, k, k_got, zero_low, sums, proj_part, dn_next, dn
    )
    dn_next = next_z(added(dn[2], dn_next))
    k_got = swap_core(k_got)
    q_next = next_z(added(q[3], q_y[3]))
    q_y[1] = swap_y(q_send[1])
    proj_far = swap_seq(proj_part)
    d_tokens = back_dot(zero_low, w_skip[:D]).reshape(1, count, D)
    sums = vector_step(sums, 1)
    q_next, q_y, k, k_got, sums, zero_low, d_tokens, proj_far, up_part, dn_next = tied(
        q_next, q_y, k, k_got, sums, zero_low, d_tokens, proj_far, up_part, dn_next
    )
    dn_next = next_z(added(dn[1], dn_next))
    q_next = onward(q[2], q_y[2], q_next)
    k_send = [added(k[1, i], k_got[1, i]) for i in range(4)]
    q_y[0] = swap_y(q_send[0])
    k_y = {3: swap_y(k_send[3])}
    k = added(k[0], k_got[0])
    up_far = swap_seq(up_part)
    out_proj = f32(proj_part) + f32(proj_far)
    d_skip = back_dot(zero_low, w_skip[D:]).reshape(1, count, D)
    sums = vector_step(sums, 0, "seq")
    q_next, q_y, k_y, k, k_send, sums, d_skip, up_far, dn_next = tied(
        q_next, q_y, k_y, k, k_send, sums, d_skip, up_far, dn_next
    )
    dn_part = added(dn[0], dn_next)
    dn_got = swap_seq(dn_part)
    q_next = onward(q[1], q_y[1], q_next)
    k_next = next_z(added(k[3], k_y[3]))
    k_y[2], k_y[1] = swap_y(k_send[2]), swap_y(k_send[1])
    out_up = f32(up_part) + f32(up_far)
    sums = vector_step(sums, 2)
    q_next, k_next, k_y, sums, dn_part, dn_got = tied(
        q_next, k_next, k_y, sums, dn_part, dn_got
    )
    out_down = by_side(side, dn_part, dn_got)
    q_sum = b16(f32(q[0]) + f32(q_y[0]) + f32(q_next))
    q_got = swap_seq(q_sum)
    k_next = onward(k[2], k_y[2], k_next)
    k_y[0] = swap_y(k_send[0])
    sums = vector_step(sums, 4)
    q_got, k_next, k_y, sums = tied(q_got, k_next, k_y, sums)
    out_qkv = f32(q_sum) + f32(q_got)
    k_next = onward(k[1], k_y[1], k_next)
    sums = vector_step(sums, 8)
    k_next, k_y, sums = tied(k_next, k_y, sums)
    k_sum = b16(f32(k[0]) + f32(k_y[0]) + f32(k_next))
    out_skip = f32(k_sum) + f32(swap_seq(k_sum))
    sums = sums.reshape(-1)
    starts = [0, D, 2 * D, 3 * D, 4 * D, 5 * D, 6 * D, 10 * D, 11 * D]
    sums = [sums[a:b] for a, b in zip(starts, starts[1:])]
    grads = (out_skip, out_qkv, out_proj, out_up, out_down)
    return (output, d_tokens, d_skip, *grads, *sums)


def solution(mesh):
    in_specs = (
        P("batch", "seq", None),
        P("seq", "batch", None, None),
        P("batch", None),
        P("batch", "seq", None),
        *(P("batch", None),) * 5,
        *(P(),) * 8,
    )
    out_specs = (*(P("batch", "seq", None),) * 3, *(P("batch", None),) * 5, *(P(),) * 8)
    pair = mesh.shape["batch"] == ROWS and mesh.shape["seq"] == 2
    return jax.shard_map(
        per_device_pair if pair else per_device,
        mesh=mesh,
        in_specs=in_specs,
        out_specs=out_specs,
        check_vma=False,

    )
```

```python
import math

import jax
import jax.numpy as jnp
from jax import lax
from jax.experimental import pallas as pl
from jax.experimental.pallas import tpu as pltpu
from jax.sharding import PartitionSpec as P

HEADS = 16
HD = 72
D = 1152
ROWS = 16
EPS = 1e-05

SCALE = HD**-0.5
C2 = SCALE * math.log2(math.e)
REM = 576
TILES = {
    0: [
        (256, 576, 258, 832, [(False, 256, 576, 258, 832), (True, 0, 464, 0, 452)]),
        (0, 272, 0, 258, [(False, 0, 272, 0, 258)]),
    ],
    1: [
        (0, 464, 0, 452, [(False, 0, 464, 0, 452), (True, 0, 576, 2, 576)]),
        (448, 272, 452, 710, [(False, 448, 272, 452, 710)]),
        (704, 128, 710, 832, [(False, 704, 128, 710, 832)]),
    ],
}
NT = (((1,), (1,)), ((), ()))


def dot(a, b, dims=(((1,), (0,)), ((), ()))):
    return lax.dot_general(a, b, dims, preferred_element_type=jnp.float32)


def split(n, step):
    return [(i, min(step, n - i)) for i in range(0, n, step)]


def full(shape):
    return pl.BlockSpec(shape, lambda h, s: (0,) * len(shape), pipeline_mode=pl.Buffered(1))


def pair_window(pair):
    tile = (2 * HD * pair) // 128
    first = 2 * HD * pair - 128 * tile
    lane = lax.broadcasted_iota(jnp.int32, (1, 256), 1)
    left = (lane >= first) & (lane < first + HD)
    right = (lane >= first + HD) & (lane < first + 2 * HD)
    base = pl.multiple_of(tile * 128, 128)

    def at(offset, row, count):
        return slice(row, row + count), pl.ds(pl.multiple_of(base + offset, 128), 256)

    return at, left, right


def stacked(value, left, right):
    zero = jnp.zeros_like(value)
    return jnp.concatenate([jnp.where(left, value, zero), jnp.where(right, value, zero)], 0)


def fwd_kernel(s_ref, qkv_ref, kvr_ref, o_ref, l_ref, *, qstep):
    pair = pl.program_id(0)

    @pl.when(pair == 0)
    def _():
        o_ref[...] = jnp.zeros_like(o_ref)
        l_ref[...] = jnp.zeros_like(l_ref)

    at, left, right = pair_window(pair)

    def chunk(r0, n, qv0, qv1, keys):
        q2 = stacked(qkv_ref[at(0, r0, n)], left, right)
        scores = []
        for far, k0, kc, kv0, kv1 in keys:
            k = kvr_ref[at(0, k0, kc)] if far else qkv_ref[at(D, k0, kc)]
            s = dot(q2, k, NT)
            if kv0 > k0 or kv1 < k0 + kc:
                kp = k0 + lax.broadcasted_iota(jnp.int32, (1, kc), 1)
                s = jnp.where((kp >= kv0) & (kp < kv1), s, -1e30)
            scores.append(s)
        top = jnp.max(scores[0], axis=1, keepdims=True)
        for s in scores[1:]:
            top = jnp.maximum(top, jnp.max(s, axis=1, keepdims=True))
        top = top * C2
        total, out = 0.0, 0.0
        for s, (far, k0, kc, _, _) in zip(scores, keys):
            p = jnp.exp2(s * C2 - top)
            total = total + jnp.sum(p, axis=1, keepdims=True)
            v = kvr_ref[at(D, k0, kc)] if far else qkv_ref[at(2 * D, k0, kc)]
            out = out + dot(p.astype(jnp.bfloat16), v)
        out = out * (1.0 / total)
        lse = top + jnp.log2(total)
        out = jnp.where(left, out[:n], out[n:]).astype(jnp.bfloat16)
        head = lax.broadcasted_iota(jnp.int32, (1, 128), 1) - 2 * pair
        lse = jnp.where(head == 0, lse[:n], lse[n:])
        keep, keep_l = left | right, (head == 0) | (head == 1)
        if r0 < qv0 or r0 + n > qv1:
            row = r0 + lax.broadcasted_iota(jnp.int32, (n, 1), 0)
            valid = (row >= qv0) & (row < qv1)
            keep, keep_l = keep & valid, keep_l & valid
        o_ref[at(0, r0, n)] = jnp.where(keep, out, o_ref[at(0, r0, n)])
        l_ref[r0 : r0 + n, :] = jnp.where(keep_l, lse, l_ref[r0 : r0 + n, :])

    for side in (0, 1):

        @pl.when(s_ref[0] == side)
        def _():
            for q0, nq, qv0, qv1, keys in TILES[side]:
                for a, n in split(nq, qstep):
                    chunk(q0 + a, n, qv0, qv1, keys)


def attn_fwd(sidx, qkv, kvr, qstep=288):
    return pl.pallas_call(
        lambda *r: fwd_kernel(*r, qstep=qstep),
        out_shape=(
            jax.ShapeDtypeStruct((832, D), jnp.bfloat16),
            jax.ShapeDtypeStruct((832, 128), jnp.float32),
        ),
        grid_spec=pltpu.PrefetchScalarGridSpec(
            num_scalar_prefetch=1,
            grid=(HEADS // 2,),
            in_specs=[full((832, 3 * D)), full((REM, 2 * D))],
            out_specs=(full((832, D)), full((832, 128))),
        ),
        compiler_params=pltpu.CompilerParams(vmem_limit_bytes=60 * 2**20),
        name="attn_fwd",
    )(sidx, qkv, kvr)


def bwd_kernel(s_ref, qkv_ref, kvr_ref, do_ref, lt_ref, dt_ref, dqkv_ref, dkvr_ref, *, kstep):
    pair = pl.program_id(0)

    @pl.when(pair == 0)
    def _():
        dqkv_ref[...] = jnp.zeros_like(dqkv_ref)
        dkvr_ref[...] = jnp.zeros_like(dkvr_ref)

    at, left, right = pair_window(pair)

    def tile(q0, nq, qv0, qv1, keys):
        q2 = stacked(qkv_ref[at(0, q0, nq)], left, right)
        do2 = stacked(do_ref[at(0, q0, nq)], left, right)

        def both(ref, mask):
            rows = []
            for h in (0, 1):
                row = ref[pl.ds(2 * pair + h, 1), :][:, q0 : q0 + nq]
                if mask and (qv0 > q0 or qv1 < q0 + nq):
                    qp = q0 + lax.broadcasted_iota(jnp.int32, (1, nq), 1)
                    row = jnp.where((qp >= qv0) & (qp < qv1), row, 1e30)
                rows.append(row)
            return jnp.concatenate(rows, 1)

        lse, row_dot = both(lt_ref, True), both(dt_ref, False)
        dqt = 0.0
        for far, first, count, kv0, kv1 in keys:
            for a, kc in split(count, kstep):
                k0 = first + a
                k = kvr_ref[at(0, k0, kc)] if far else qkv_ref[at(D, k0, kc)]
                v = kvr_ref[at(D, k0, kc)] if far else qkv_ref[at(2 * D, k0, kc)]
                p = jnp.exp2(dot(k, q2, NT) * C2 - lse)
                if kv0 > k0 or kv1 < k0 + kc:
                    kp = k0 + lax.broadcasted_iota(jnp.int32, (kc, 1), 0)
                    p = jnp.where((kp >= kv0) & (kp < kv1), p, 0.0)
                ds = (p * (dot(v, do2, NT) - row_dot)).astype(jnp.bfloat16)
                dv = dot(p.astype(jnp.bfloat16), do2).astype(jnp.bfloat16)
                dk = (dot(ds, q2) * SCALE).astype(jnp.bfloat16)
                if far:
                    dkvr_ref[at(0, k0, kc)] += dk
                    dkvr_ref[at(D, k0, kc)] += dv
                else:
                    dqkv_ref[at(D, k0, kc)] += dk
                    dqkv_ref[at(2 * D, k0, kc)] += dv
                dqt = dqt + dot(k.T, ds)
        dq = (dqt * SCALE).T
        dq = jnp.where(left, dq[:nq], jnp.where(right, dq[nq:], 0.0)).astype(jnp.bfloat16)
        dqkv_ref[at(0, q0, nq)] += dq

    for side in (0, 1):

        @pl.when(s_ref[0] == side)
        def _():
            for parts in TILES[side]:
                tile(*parts)


def attn_bwd(sidx, qkv, kvr, do, lt, dt, kstep=1024):
    return pl.pallas_call(
        lambda *r: bwd_kernel(*r, kstep=kstep),
        out_shape=(
            jax.ShapeDtypeStruct((832, 3 * D), jnp.bfloat16),
            jax.ShapeDtypeStruct((REM, 2 * D), jnp.bfloat16),
        ),
        grid_spec=pltpu.PrefetchScalarGridSpec(
            num_scalar_prefetch=1,
            grid=(HEADS // 2,),
            in_specs=[
                full((832, 3 * D)),
                full((REM, 2 * D)),
                full((832, D)),
                full((16, 832)),
                full((16, 832)),
            ],
            out_specs=(full((832, 3 * D)), full((REM, 2 * D))),
        ),
        compiler_params=pltpu.CompilerParams(vmem_limit_bytes=60 * 2**20),
        name="attn_bwd",
    )(sidx, qkv, kvr, do, lt, dt)


ERFC = (0.5 * 1.061405429, -0.5 * 1.453152027, 0.5 * 1.421413741, -0.5 * 0.284496736, 0.5 * 0.254829592)


def normal_cdf(u):
    expo = jnp.exp2(u * u * (-0.5 * math.log2(math.e)))
    below = 1.0 + (0.3275911 * math.sqrt(0.5)) * jnp.abs(u)
    step = pltpu.reciprocal(below, approx=True)
    step = step * (2.0 - below * step)
    tail = ERFC[0]
    for term in ERFC[1:]:
        tail = tail * step + term
    tail = tail * step * expo
    return jnp.where(u < 0.0, tail, 1.0 - tail), expo


def mlp_up(at, act, weight, bias, grad, tile=D, chunks=4):
    rows, width = act.shape[0], weight.shape[1]
    steps = width // tile
    size = rows // chunks

    def kernel(at, a_ref, w_ref, b_ref, e_ref, g_ref, d_ref, mine, other, held):
        t = pl.program_id(0)

        def forward():
            for i in range(chunks):
                part = slice(i * size, (i + 1) * size)
                u = dot(a_ref[part], w_ref[...]) + b_ref[...]
                phi, expo = normal_cdf(u)
                g = (u * phi).astype(jnp.bfloat16)
                g_ref[part] = g
                d_ref[part] = (phi + u * expo * (1.0 / math.sqrt(2.0 * math.pi))).astype(jnp.bfloat16)

        def keep():
            held[...] = g_ref[...].T

        def back():
            for yy in (0, 1):
                both = dot(held[yy * 576 : yy * 576 + 576], e_ref[...])
                low, high = both[:288], both[288:]
                yrel = yy + at[1] - 2 * yy * at[1]
                for ref, value in (
                    (mine, jnp.where(at[2] == 0, low, high)),
                    (other, jnp.where(at[2] == 0, high, low)),
                ):
                    value = value.astype(jnp.bfloat16)
                    ref[at[3], yrel, 0] = value[:144]
                    ref[1 - at[3], yrel, 0] = value[144:]

        @pl.when(t == 0)
        def _():
            forward()
            keep()

        @pl.when((t > 0) & (t < steps))
        def _():
            back()
            forward()
            keep()

        @pl.when(t == steps)
        def _():
            back()

    out = jax.ShapeDtypeStruct((rows, width), jnp.bfloat16)
    split = jax.ShapeDtypeStruct((2, 2, 4, 144, D), jnp.bfloat16)

    def now(t):
        return jnp.minimum(t, steps - 1)

    whole = pl.BlockSpec((rows, D), lambda t, at: (0, 0), pipeline_mode=pl.Buffered(1))
    by_column = pl.BlockSpec((rows, tile), lambda t, at: (0, now(t)))
    split_spec = pl.BlockSpec((2, 2, 1, 144, D), lambda t, at: (0, 0, jnp.maximum(t - 1, 0), 0, 0))
    return pl.pallas_call(
        kernel,
        out_shape=(out, out, split, split),
        grid_spec=pltpu.PrefetchScalarGridSpec(
            num_scalar_prefetch=1,
            grid=(steps + 1,),
            in_specs=[
                whole,
                pl.BlockSpec((D, tile), lambda t, at: (0, now(t))),
                pl.BlockSpec((1, tile), lambda t, at: (0, now(t))),
                whole,
            ],
            out_specs=(by_column, by_column, split_spec, split_spec),
            scratch_shapes=[pltpu.VMEM((tile, rows), jnp.bfloat16)],
        ),
        compiler_params=pltpu.CompilerParams(vmem_limit_bytes=60 * 2**20),
        name="mlp_up",
    )(at, act, weight, bias.reshape(1, width), grad)


def ordered_transpose(at, value, held, ring=True):
    held[...] = value.astype(jnp.float32).T.reshape(held.shape)
    blocks = []
    for crel in (0, 1):
        for yrel in (0, 1):
            for zrel in range(4):
                zz = lax.rem(at[0] + zrel, 4) if ring else zrel
                yy = at[1] + yrel - 2 * at[1] * yrel
                cc = at[2] + crel - 2 * at[2] * crel
                blocks.append(held[zz * 4 + yy * 2 + cc])
    return jnp.concatenate(blocks, 0).astype(jnp.bfloat16)


def mlp_back(at, act, grad, gelu, slope, w_up, w_down, halves=1, tile=768):
    rows, width = gelu.shape
    half = rows // halves

    def kernel(at, a_ref, e_ref, g_ref, s_ref, wu_ref, wd_ref, *refs):
        mine, other, h_ref, c_ref, b_ref, a_t, du_ref, held = refs

        @pl.when(pl.program_id(0) == 0)
        def _():
            a_t[...] = ordered_transpose(at, a_ref[...], held, ring=False)
            h_ref[...] = jnp.zeros_like(h_ref)
            c_ref[...] = jnp.zeros_like(c_ref)

        bias = None
        for i in range(halves):
            part = slice(i * half, (i + 1) * half)
            du = dot(e_ref[part], wd_ref[...], NT) * s_ref[part].astype(jnp.float32)
            total = jnp.sum(du, axis=0, keepdims=True)
            bias = total if bias is None else bias + total
            du = du.astype(jnp.bfloat16)
            du_ref[part] = du
            h_ref[part] += dot(g_ref[part], wd_ref[...])
            c_ref[part] += dot(du, wu_ref[...], NT)
        b_ref[...] = bias
        for i, ref in ((0, mine), (1, other)):
            both = dot(a_t[i * 576 : i * 576 + 576], du_ref[...])
            for j in range(8):
                ref[j // 4, j % 4] = both[j * 72 : j * 72 + 72].astype(jnp.bfloat16)

    once = pl.Buffered(1)
    whole = jax.ShapeDtypeStruct((rows, D), jnp.float32)
    split = jax.ShapeDtypeStruct((2, 4, 72, width), jnp.bfloat16)
    split_spec = pl.BlockSpec((2, 4, 72, tile), lambda t, at: (0, 0, 0, t))
    whole_spec = pl.BlockSpec((rows, D), lambda t, at: (0, 0), pipeline_mode=once)
    by_column = pl.BlockSpec((rows, tile), lambda t, at: (0, t))
    weight_column = pl.BlockSpec((D, tile), lambda t, at: (0, t))
    return pl.pallas_call(
        kernel,
        out_shape=(
            split,
            split,
            whole,
            whole,
            jax.ShapeDtypeStruct((1, width), jnp.float32),
        ),
        grid_spec=pltpu.PrefetchScalarGridSpec(
            num_scalar_prefetch=1,
            grid=(width // tile,),
            in_specs=[
                whole_spec,
                whole_spec,
                by_column,
                by_column,
                weight_column,
                pl.BlockSpec((tile, D), lambda t, at: (t, 0)),
            ],
            out_specs=(
                split_spec,
                split_spec,
                whole_spec,
                whole_spec,
                pl.BlockSpec((1, tile), lambda t, at: (0, t)),
            ),
            scratch_shapes=[
                pltpu.VMEM((D, rows), jnp.bfloat16),
                pltpu.VMEM((rows, tile), jnp.bfloat16),
                pltpu.VMEM((16, 72, rows), jnp.float32),
            ],
        ),
        compiler_params=pltpu.CompilerParams(vmem_limit_bytes=62 * 2**20),
        name="mlp_back",
    )(at, act, grad, gelu, slope, w_up, w_down)


def qkv_grad(at, act, act_far, grad, grad_far):
    rows, far = act.shape[0], act_far.shape[0]

    def kernel(at, a_ref, f_ref, g_ref, h_ref, mine, other, a_t, f_t, held, held_far):
        t = pl.program_id(0)

        @pl.when(t == 0)
        def _():
            a_t[...] = ordered_transpose(at, a_ref[...], held)
            f_t[...] = ordered_transpose(at, f_ref[...], held_far)

        away = jnp.where(t > 0, h_ref[...], jnp.zeros_like(h_ref))
        for i, ref in ((0, mine), (1, other)):
            part = slice(i * 576, (i + 1) * 576)
            both = dot(a_t[part], g_ref[...]) + dot(f_t[part], away)
            for j in range(8):
                ref[j // 4, j % 4] = both[j * 72 : j * 72 + 72].astype(jnp.bfloat16)

    once = pl.Buffered(1)
    split = jax.ShapeDtypeStruct((2, 4, 72, 3 * D), jnp.bfloat16)
    split_spec = pl.BlockSpec((2, 4, 72, D), lambda t, at: (0, 0, 0, t))
    return pl.pallas_call(
        kernel,
        out_shape=(split, split),
        grid_spec=pltpu.PrefetchScalarGridSpec(
            num_scalar_prefetch=1,
            grid=(3,),
            in_specs=[
                pl.BlockSpec((rows, D), lambda t, at: (0, 0), pipeline_mode=once),
                pl.BlockSpec((far, D), lambda t, at: (0, 0), pipeline_mode=once),
                pl.BlockSpec((rows, D), lambda t, at: (0, t)),
                pl.BlockSpec((far, D), lambda t, at: (0, jnp.maximum(t - 1, 0))),
            ],
            out_specs=(split_spec, split_spec),
            scratch_shapes=[
                pltpu.VMEM((D, rows), jnp.bfloat16),
                pltpu.VMEM((D, far), jnp.bfloat16),
                pltpu.VMEM((16, 72, rows), jnp.float32),
                pltpu.VMEM((16, 72, far), jnp.float32),
            ],
        ),
        compiler_params=pltpu.CompilerParams(vmem_limit_bytes=60 * 2**20),
        name="qkv_grad",
    )(at, act, act_far, grad, grad_far)


def skip_back(at, tok, skip, grad):
    rows = tok.shape[0]

    def kernel(at, t_ref, s_ref, g_ref, mine, other, in_t):
        i = pl.program_id(0)

        @pl.when(i == 0)
        def _():
            in_t[0:D] = t_ref[...].T
            in_t[D:] = s_ref[...].T

        first = pl.multiple_of(lax.rem(at[0] + i, 4) * 576, 16)
        both = dot(in_t[pl.ds(first, 576)], g_ref[...])
        for yy in (0, 1):
            low, high = both[yy * 288 : yy * 288 + 144], both[yy * 288 + 144 : yy * 288 + 288]
            yrel = yy + at[1] - 2 * yy * at[1]
            mine[yrel, 0] = jnp.where(at[2] == 0, low, high).astype(jnp.bfloat16)
            other[yrel, 0] = jnp.where(at[2] == 0, high, low).astype(jnp.bfloat16)

    split = jax.ShapeDtypeStruct((2, 4, 144, D), jnp.bfloat16)
    split_spec = pl.BlockSpec((2, 1, 144, D), lambda t, at: (0, t, 0, 0))
    whole_spec = pl.BlockSpec((rows, D), lambda t, at: (0, 0), pipeline_mode=pl.Buffered(1))
    return pl.pallas_call(
        kernel,
        out_shape=(split, split),
        grid_spec=pltpu.PrefetchScalarGridSpec(
            num_scalar_prefetch=1,
            grid=(4,),
            in_specs=[whole_spec] * 3,
            out_specs=(split_spec, split_spec),
            scratch_shapes=[pltpu.VMEM((2 * D, rows), jnp.bfloat16)],
        ),
        compiler_params=pltpu.CompilerParams(vmem_limit_bytes=40 * 2**20),
        name="skip_back",
    )(at, tok, skip, grad)


def layer_norm(hidden, gain, shift):
    centred = hidden - jnp.mean(hidden, axis=-1, keepdims=True)
    spread = jnp.mean(centred * centred, axis=-1, keepdims=True)
    return centred * lax.rsqrt(spread + EPS) * gain + shift


def exact_gelu(value):
    return jax.nn.gelu(value, approximate=False)


def segment_ids(offsets, positions):
    hits = (positions[None, :, None] >= offsets[:, None, :]).astype(jnp.int32)
    return jnp.sum(hits, axis=-1)


def fwd_dot(left, right):
    return jnp.dot(left, right, preferred_element_type=jnp.float32)


def contract_rows(left, right):
    return lax.dot_general(
        left, right, (((0,), (0,)), ((), ())), preferred_element_type=jnp.float32
    )


def back_dot(grad_rows, weight):
    return lax.dot_general(
        grad_rows, weight, (((1,), (1,)), ((), ())), preferred_element_type=jnp.float32
    )


class RowAttention:
    def __init__(self, qkv_all, offsets, row_count, local_len):
        self.row_count, self.local_len = row_count, local_len
        self.row_len = local_len * lax.axis_size("seq")
        self.offsets = offsets
        first_pos = lax.axis_index("seq") * local_len
        self.query_seg = segment_ids(offsets, first_pos + jnp.arange(local_len, dtype=jnp.int32))
        self.scale = HD ** (-0.5)
        self.queries = qkv_all[:, :D].reshape(row_count, local_len, HEADS, HD)
        keyvals = qkv_all[:, D:].reshape(row_count, local_len, 2 * D)
        self.kv = lax.all_gather(keyvals, "seq", axis=1, tiled=True)

    def block(self, first, size):
        kv = lax.dynamic_slice_in_dim(self.kv, first, size, 1)
        shape = (self.row_count, size, HEADS, HD)
        key_seg = segment_ids(self.offsets, first + jnp.arange(size, dtype=jnp.int32))
        same = self.query_seg[:, :, None, None] == key_seg[:, None, None, :]
        return kv[:, :, :D].reshape(shape), kv[:, :, D:].reshape(shape), same

    def scores(self, keys):
        return (
            jnp.einsum("rthd,rkhd->rthk", self.queries, keys, preferred_element_type=jnp.float32)
            * self.scale
        )

    def forward(self):
        keys, values, same = self.block(0, self.row_len)
        scores = jnp.where(same, self.scores(keys), -1e30)
        top = jnp.max(scores, axis=-1)
        expo = jnp.where(same, jnp.exp(scores - top[..., None]), 0.0)
        norm = jnp.sum(expo, axis=-1)
        weighted = jnp.einsum(
            "rthk,rkhd->rthd",
            expo.astype(jnp.bfloat16),
            values,
            preferred_element_type=jnp.float32,
        )
        self.attended = weighted / norm[..., None]
        self.log_total = top + jnp.log(norm)
        return self.attended.reshape(-1, D).astype(jnp.bfloat16)

    def backward(self, d_att):
        rows, length = self.row_count, self.local_len
        d_att = d_att.reshape(rows, length, HEADS, HD)
        row_dot = jnp.sum(d_att.astype(jnp.float32) * self.attended, axis=-1)
        size = math.gcd(self.row_len, 512)

        def step(index, totals):
            d_query, d_kv = totals
            keys, values, same = self.block(index * size, size)
            weights = jnp.where(same, jnp.exp(self.scores(keys) - self.log_total[..., None]), 0.0)
            d_weights = jnp.einsum(
                "rthd,rkhd->rthk", d_att, values, preferred_element_type=jnp.float32
            )
            d_scores = (weights * (d_weights - row_dot[..., None])).astype(jnp.bfloat16)
            d_query = d_query + self.scale * jnp.einsum(
                "rthk,rkhd->rthd", d_scores, keys, preferred_element_type=jnp.float32
            )
            d_key = self.scale * jnp.einsum(
                "rthk,rthd->rkhd", d_scores, self.queries, preferred_element_type=jnp.float32
            )
            d_value = jnp.einsum(
                "rthk,rthd->rkhd",
                weights.astype(jnp.bfloat16),
                d_att,
                preferred_element_type=jnp.float32,
            )
            both = jnp.concatenate(
                [d_key.reshape(rows, size, D), d_value.reshape(rows, size, D)], axis=2
            )
            return d_query, lax.dynamic_update_slice_in_dim(d_kv, both, index * size, 1)

        start = (
            jnp.zeros((rows, length, HEADS, HD), jnp.float32),
            jnp.zeros((rows, self.row_len, 2 * D), jnp.float32),
        )
        d_query, d_kv = lax.fori_loop(0, self.row_len // size, step, start)
        d_kv = lax.psum_scatter(
            d_kv.astype(jnp.bfloat16), "seq", scatter_dimension=1, tiled=True
        ).astype(jnp.float32)
        return jnp.concatenate(
            [d_query.reshape(rows * length, D), d_kv.reshape(rows * length, 2 * D)], axis=1
        ).astype(jnp.bfloat16)


def per_device(
    tokens,
    skip_parts,
    lengths,
    cotangent,
    skip_w,
    qkv_w,
    proj_w,
    fc1_w,
    fc2_w,
    skip_bias,
    ln1_gain,
    ln1_bias,
    proj_bias,
    ln2_gain,
    ln2_bias,
    fc1_bias,
    fc2_bias,
):
    row_count, local_len, features = tokens.shape
    tok_count = row_count * local_len
    offsets = jnp.cumsum(lengths, axis=1)
    first_pos = lax.axis_index("seq") * local_len
    query_seg = segment_ids(offsets, first_pos + jnp.arange(local_len, dtype=jnp.int32))
    live_mask = (query_seg < lengths.shape[1]).astype(jnp.float32).reshape(tok_count, 1)
    skip_rows = lax.psum_scatter(skip_parts[0], "seq", scatter_dimension=1, tiled=True)
    w_skip, w_qkv, w_proj, w_up, w_down = (
        lax.all_gather(w, "batch", axis=0, tiled=True)
        for w in (skip_w, qkv_w, proj_w, fc1_w, fc2_w)
    )
    tok_flat = tokens.reshape(tok_count, features)
    skip_flat = skip_rows.reshape(tok_count, features)
    h_zero = (
        fwd_dot(tok_flat, w_skip[:features]) + fwd_dot(skip_flat, w_skip[features:]) + skip_bias
    )
    normed_one, ln1_back = jax.vjp(layer_norm, h_zero, ln1_gain, ln1_bias)
    act_one = normed_one.astype(jnp.bfloat16)
    qkv_all = fwd_dot(act_one, w_qkv).astype(jnp.bfloat16)
    attention = RowAttention(qkv_all, offsets, row_count, local_len)
    att_low = attention.forward()
    h_one = h_zero + fwd_dot(att_low, w_proj) + proj_bias
    normed_two, ln2_back = jax.vjp(layer_norm, h_one, ln2_gain, ln2_bias)
    act_two = normed_two.astype(jnp.bfloat16)
    up_proj = fwd_dot(act_two, w_up) + fc1_bias
    gelu_out, gelu_back = jax.vjp(exact_gelu, up_proj)
    gelu_low = gelu_out.astype(jnp.bfloat16)
    h_two = h_one + fwd_dot(gelu_low, w_down) + fc2_bias
    output = (h_two * live_mask).astype(jnp.bfloat16).reshape(row_count, local_len, features)
    grad_two = cotangent.reshape(tok_count, features).astype(jnp.float32) * live_mask
    grad_low = grad_two.astype(jnp.bfloat16)
    d_w_down = contract_rows(gelu_low, grad_low)
    d_gelu = back_dot(grad_low, w_down)
    d_up = gelu_back(d_gelu)[0]
    up_low = d_up.astype(jnp.bfloat16)
    d_w_up = contract_rows(act_two, up_low)
    d_act_two = back_dot(up_low, w_up)
    d_h_one, d_ln2_gain, d_ln2_bias = ln2_back(d_act_two)
    d_h_one = d_h_one + grad_two
    proj_low = d_h_one.astype(jnp.bfloat16)
    d_w_proj = contract_rows(att_low, proj_low)
    d_att = back_dot(proj_low, w_proj).astype(jnp.bfloat16)
    d_qkv = attention.backward(d_att)
    d_w_qkv = contract_rows(act_one, d_qkv)
    d_act_one = back_dot(d_qkv, w_qkv)
    d_h_zero, d_ln1_gain, d_ln1_bias = ln1_back(d_act_one)
    d_h_zero = d_h_zero + d_h_one
    zero_low = d_h_zero.astype(jnp.bfloat16)
    d_w_skip = jnp.concatenate(
        [contract_rows(tok_flat, zero_low), contract_rows(skip_flat, zero_low)], axis=0
    )
    d_tokens = back_dot(zero_low, w_skip[:features]).reshape(row_count, local_len, features)
    d_skip = back_dot(zero_low, w_skip[features:]).reshape(row_count, local_len, features)
    vector_sums = lax.psum(
        (
            jnp.sum(d_h_zero, axis=0),
            d_ln1_gain,
            d_ln1_bias,
            jnp.sum(d_h_one, axis=0),
            d_ln2_gain,
            d_ln2_bias,
            jnp.sum(d_up, axis=0),
            jnp.sum(grad_two, axis=0),
        ),
        ("batch", "seq"),
    )
    weight_grads = tuple(
        lax.psum(
            lax.psum_scatter(
                grad.astype(jnp.bfloat16), "batch", scatter_dimension=0, tiled=True
            ),
            "seq",
        ).astype(jnp.float32)
        for grad in (d_w_skip, d_w_qkv, d_w_proj, d_w_up, d_w_down)
    )
    return (output, d_tokens, d_skip, *weight_grads, *vector_sums)


YSW = [(b, b ^ 2) for b in range(16)]
CSW = [(b, b ^ 1) for b in range(16)]
ZUP = [(b, (b + 4) % 16) for b in range(16)]


def swap_y(v):
    return lax.ppermute(v, "batch", YSW)


def swap_core(v):
    return lax.ppermute(v, "batch", CSW)


def next_z(v):
    return lax.ppermute(v, "batch", ZUP)


def swap_seq(v):
    return lax.ppermute(v, "seq", [(0, 1), (1, 0)])


def place():
    b = lax.axis_index("batch").astype(jnp.int32)
    return b // 4, (b // 2) % 2, b % 2


def f32(v):
    return v.astype(jnp.float32)


def b16(v):
    return v.astype(jnp.bfloat16)


def core_pair(shard):
    core = place()[2]
    half = shard.shape[1] // 2
    low, high = shard[:, :half], shard[:, half:]
    keep = jnp.where(core == 0, low, high)
    got = swap_core(jnp.where(core == 0, high, low))
    return jnp.where(
        core == 0, jnp.concatenate([keep, got], 0), jnp.concatenate([got, keep], 0)
    )


def tied(*values):
    return lax.optimization_barrier(values)


def with_core(own):
    return own + [swap_core(v) for v in own]


def assemble(pieces, kind):
    rows, cols = pieces[0].shape
    split, halves, paired = kind == "split", kind.endswith("halves"), kind == "halves"
    if split:
        shapes = [(8 * rows, 3 * D), (8 * rows, D)]
    elif halves:
        shapes = [(8 * rows, 2 * cols)]
    else:
        shapes = [(16 * rows, cols)]

    def kernel(at, *refs):
        ins, outs, (held, came, left) = refs[:16], refs[16:-3], refs[-3:]
        z, y, c, x = at[0], at[1], at[2], at[3]
        loads = [pltpu.make_async_copy(ins[j], held.at[j], came.at[j]) for j in range(16)]
        for load in loads:
            load.start()
        waits = []
        for j in range(16):
            core = c if j < 8 else 1 - c
            yy = y if j % 8 < 4 else 1 - y
            away = j % 4
            if paired and j % 8 in (4, 5):
                away = away + x - 2 * away * x
            zz = lax.rem(z - away + 4, 4)
            loads[j].wait()
            if not split:
                if halves:
                    first = pl.multiple_of((zz * 2 + yy) * rows, 16)
                    at_cols = pl.ds(pl.multiple_of(core * cols, 128), cols)
                    target = outs[0].at[pl.ds(first, rows), at_cols]
                else:
                    first = pl.multiple_of((zz * 4 + yy * 2 + core) * rows, 16)
                    target = outs[0].at[pl.ds(first, rows), :]
                store = pltpu.make_async_copy(held.at[j], target, left.at[j])
                store.start()
                waits.append((None, store))
                continue
            at_rows = pl.ds(pl.multiple_of((zz * 2 + yy) * rows, 16), rows)
            at_cols = pl.ds(pl.multiple_of(core * (2 * D), 128), D)
            store = pltpu.make_async_copy(
                held.at[j, :, pl.ds(0, D)], outs[0].at[at_rows, at_cols], left.at[j]
            )
            store.start()
            waits.append((None, store))
            for which, target in ((0, outs[0].at[at_rows, pl.ds(D, D)]), (1, outs[1].at[at_rows, :])):
                store = pltpu.make_async_copy(held.at[j, :, pl.ds(D, D)], target, left.at[16 + j])
                pl.when(core == which)(store.start)
                waits.append((core == which, store))
        for needed, store in waits:
            if needed is None:
                store.wait()
            else:
                pl.when(needed)(store.wait)

    out = pl.pallas_call(
        kernel,
        out_shape=[jax.ShapeDtypeStruct(v, pieces[0].dtype) for v in shapes],
        in_specs=[pl.BlockSpec(memory_space=pltpu.SMEM)]
        + [pl.BlockSpec(memory_space=pl.ANY)] * 16,
        out_specs=[pl.BlockSpec(memory_space=pl.ANY)] * len(shapes),
        scratch_shapes=[
            pltpu.VMEM((16, rows, cols), pieces[0].dtype),
            pltpu.SemaphoreType.DMA((16,)),
            pltpu.SemaphoreType.DMA((32,)),
        ],
        compiler_params=pltpu.CompilerParams(vmem_limit_bytes=16 * 2**20),
        name="assemble",
    )(jnp.stack([*place(), lax.axis_index("seq").astype(jnp.int32)]), *pieces)
    return out if split else out[0]


def take(v, axis, index):
    return lax.dynamic_index_in_dim(v, index, axis, keepdims=False)


def added(left, right):
    return b16(f32(left) + f32(right))


def by_side(side, own, other):
    own, other = f32(own), f32(other)
    return jnp.where(
        side == 0, jnp.concatenate([own, other], 0), jnp.concatenate([other, own], 0)
    )


def vector_step(value, bit, axis="batch"):
    if axis == "seq":
        return value + swap_seq(value)
    return value + lax.ppermute(value, "batch", [(b, b ^ bit) for b in range(16)])


def z_scatter(blocks):
    groups = [[q + 4 * z for z in range(4)] for q in range(4)]
    return lax.psum_scatter(
        blocks, "batch", scatter_dimension=0, tiled=True, axis_index_groups=groups
    )


def sc_sum(grad):
    return lax.psum_scatter(grad, "batch", scatter_dimension=0, tiled=True)


def per_device_pair(
    tokens,
    skip_parts,
    lengths,
    cotangent,
    skip_w,
    qkv_w,
    proj_w,
    fc1_w,
    fc2_w,
    skip_bias,
    ln1_gain,
    ln1_bias,
    proj_bias,
    ln2_gain,
    ln2_bias,
    fc1_bias,
    fc2_bias,
):
    count = tokens.shape[1]
    side = lax.axis_index("seq").astype(jnp.int32)
    index = side.reshape(1)
    at = jnp.stack([*place(), side])
    shared = jnp.where(side == 0, 256, 0)
    live = (
        (side * count + lax.broadcasted_iota(jnp.int32, (count, 1), 0)) < jnp.sum(lengths)
    ).astype(jnp.float32)

    parts = skip_parts.reshape(2, count, D)
    skip_far = swap_seq(take(parts, 0, 1 - side))
    tok_flat = tokens.reshape(count, D)

    q0 = core_pair(jnp.concatenate([qkv_w, proj_w], 1))
    s0 = skip_w
    s1, t0, s0c = next_z(s0), swap_y(s0), swap_core(s0)
    s1, t0 = tied(s1, t0)
    s2, t1 = next_z(s1), swap_y(s1)
    s2, t1, s1, q0, t0, s0c = tied(s2, t1, s1, q0, t0, s0c)
    s3, t2, q1 = next_z(s2), swap_y(s2), next_z(q0)
    s1c, t0c = swap_core(s1), swap_core(t0)
    s3, t2, s2, q0, t1, s1c, t0c = tied(s3, t2, s2, q0, t1, s1c, t0c)
    t3, r0 = swap_y(s3), swap_y(q0)
    s2c, s3c, t1c, t2c = swap_core(s2), swap_core(s3), swap_core(t1), swap_core(t2)
    s2c, s3c, t1c, t2c, t3, skip_far, q1, q0 = tied(s2c, s3c, t1c, t2c, t3, skip_far, q1, q0)
    q2, r1 = next_z(q1), swap_y(q1)
    w_skip = assemble(
        [s0, s1, s2, s3, t0, t1, t2, t3, s0c, s1c, s2c, s3c, t0c, t1c, t2c, swap_core(t3)], "rows"
    )
    skip_flat = b16(f32(take(parts, 0, side)) + f32(skip_far))
    h_zero = fwd_dot(tok_flat, w_skip[:D]) + fwd_dot(skip_flat, w_skip[D:]) + skip_bias
    normed_one, ln1_back = jax.vjp(layer_norm, h_zero, ln1_gain, ln1_bias)
    act_one = b16(normed_one)
    act_send = lax.dynamic_slice(act_one, (shared, 0), (REM, D))
    u0 = core_pair(fc1_w)
    q2, r1, r0, act_one, act_send, u0, q1 = tied(q2, r1, r0, act_one, act_send, u0, q1)
    act_far = swap_seq(act_send)
    q3, r2 = next_z(q2), swap_y(q2)
    q0c, q1c, r0c = swap_core(q0), swap_core(q1), swap_core(r0)
    q3, r2, u0, q2, q0c, q1c, r0c, r1 = tied(q3, r2, u0, q2, q0c, q1c, r0c, r1)
    r3, u1 = swap_y(q3), next_z(u0)
    q2c, q3c, r1c, r2c = swap_core(q2), swap_core(q3), swap_core(r1), swap_core(r2)
    r3, u1, q3, q2c, q3c, r1c, r2c = tied(r3, u1, q3, q2c, q3c, r1c, r2c)
    u2, v0 = next_z(u1), swap_y(u0)
    w_qkv, w_proj = assemble(
        [q0, q1, q2, q3, r0, r1, r2, r3, q0c, q1c, q2c, q3c, r0c, r1c, r2c, swap_core(r3)], "split"
    )
    u2, v0, w_qkv, w_proj, u1, u0, act_far = tied(u2, v0, w_qkv, w_proj, u1, u0, act_far)
    u3, v1 = next_z(u2), swap_y(u1)
    u0c, u1c, v0c = swap_core(u0), swap_core(u1), swap_core(v0)
    qkv = b16(fwd_dot(act_one, w_qkv))
    kv_far = b16(fwd_dot(act_far, w_qkv[:, D:]))
    u3, v1, u2, u0c, u1c, v0c, qkv, kv_far, fc2_w = tied(
        u3, v1, u2, u0c, u1c, v0c, qkv, kv_far, fc2_w
    )
    w_down = lax.all_gather(fc2_w, "batch", axis=0, tiled=True)
    v2, v3 = swap_y(u2), swap_y(u3)
    u2c, u3c, v1c = swap_core(u2), swap_core(u3), swap_core(v1)
    att, lse = attn_fwd(index, qkv, kv_far)
    v2, v3, u2c, u3c, v1c, att = tied(v2, v3, u2c, u3c, v1c, att)
    v2c, v3c = swap_core(v2), swap_core(v3)
    h_one = h_zero + fwd_dot(att, w_proj) + proj_bias
    normed_two, ln2_back = jax.vjp(layer_norm, h_one, ln2_gain, ln2_bias)
    act_two = b16(normed_two)
    w_up = assemble(
        [u0, u1, u2, u3, v0, v1, v2, v3, u0c, u1c, u2c, u3c, v0c, v1c, v2c, v3c], "ringhalves"
    )

    grad_two = f32(cotangent.reshape(count, D)) * live
    grad_low = b16(grad_two)
    gelu_low, slope, dn, dn_got = mlp_up(at, act_two, w_up, fc1_bias, grad_low)
    dn_got, gelu_low, slope, w_down = tied(dn_got, gelu_low, slope, w_down)
    dn_got = swap_core(dn_got)
    up, up_got, h_add, d_act_two, d_up_bias = mlp_back(
        at, act_two, grad_low, gelu_low, slope, w_up, w_down
    )
    dn, dn_got, up_got, d_act_two = tied(dn, dn_got, up_got, d_act_two)
    up_got = swap_core(up_got)
    dn_far = swap_seq(added(dn[1], dn_got[1]))
    dn = added(dn[0], dn_got[0])
    output = b16((h_one + h_add + fc2_bias) * live).reshape(1, count, D)
    d_h_one, d_ln2_gain, d_ln2_bias = ln2_back(d_act_two)
    d_h_one = d_h_one + grad_two
    proj_low = b16(d_h_one)
    up_got, proj_low, dn = tied(up_got, proj_low, dn)
    up_far = swap_y(added(up[1], up_got[1]))
    up = added(up[0], up_got[0])
    d_proj = b16(contract_rows(att, proj_low))
    d_att = b16(back_dot(proj_low, w_proj))
    d_att, d_proj, output, up = tied(d_att, d_proj, output, up)
    proj_part = sc_sum(d_proj)
    pick = (
        lax.broadcasted_iota(jnp.int32, (D, HEADS), 0) // HD
        == lax.broadcasted_iota(jnp.int32, (D, HEADS), 1)
    ).astype(jnp.float32)
    row_dot = lax.dot_general(
        pick, f32(d_att) * f32(att), (((0,), (1,)), ((), ())), precision=lax.Precision.HIGHEST
    )
    lse = lse[:, :HEADS].T
    d_qkv, d_far = attn_bwd(index, qkv, kv_far, d_att, lse, row_dot)
    far = b16(back_dot(d_far, w_qkv[:, D:]))
    far, d_qkv, d_far, dn, dn_far = tied(far, d_qkv, d_far, dn, dn_far)
    dn_send = [added(dn[1, 0:2], dn_far[1, 0:2]), added(dn[1, 2:4], dn_far[1, 2:4])]
    dn = added(dn[0], dn_far[0])
    dn, dn_send, up_far = tied(dn, dn_send, up_far)
    up = added(up, up_far)
    far, d_qkv, d_far, dn, dn_send, up = tied(far, d_qkv, d_far, dn, dn_send, up)
    up_part = z_scatter(up.reshape(4 * 72, 4 * D))
    low_far = swap_seq(far[: REM // 2])
    dn_low = swap_y(dn_send[0])
    q, q_got = qkv_grad(at, act_one, act_far, d_qkv, d_far)
    d_qkv, q, q_got, low_far, dn_low, far = tied(d_qkv, q, q_got, low_far, dn_low, far)
    q_got = swap_core(q_got)
    high_far = swap_seq(far[REM // 2 :])
    dn_high = swap_y(dn_send[1])
    d_act_one = back_dot(d_qkv, w_qkv)
    q_got, d_act_one, high_far = tied(q_got, d_act_one, high_far)
    far = f32(jnp.concatenate([low_far, high_far], 0))
    here = lax.dynamic_slice(d_act_one, (shared, 0), (REM, D))
    d_act_one = lax.dynamic_update_slice(d_act_one, here + far, (shared, 0))
    q_send = [added(q[1, i], q_got[1, i]) for i in range(4)]
    q_y = {i: swap_y(q_send[i]) for i in (3, 2)}
    q = added(q[0], q_got[0])
    dn = added(dn, jnp.concatenate([dn_low, dn_high], 0))
    dn = [take(dn, 0, (place()[0] + i) % 4) for i in range(4)]
    dn_next = next_z(dn[3])
    d_h_zero, d_ln1_gain, d_ln1_bias = ln1_back(d_act_one)
    d_h_zero = d_h_zero + d_h_one
    zero_low = b16(d_h_zero)
    k, k_got = skip_back(at, tok_flat, skip_flat, zero_low)

    def onward(mine, got, so_far):
        return next_z(b16(f32(mine) + f32(got) + f32(so_far)))

    sums = jnp.concatenate(
        [
            jnp.sum(d_h_zero, axis=0),
            d_ln1_gain,
            d_ln1_bias,
            jnp.sum(d_h_one, axis=0),
            d_ln2_gain,
            d_ln2_bias,
            d_up_bias[0],
            jnp.sum(grad_two, axis=0),
        ]
    ).reshape(-1, 128)
    q_y[3], q_y[2], q, q_send, k, k_got, zero_low, sums, proj_part, dn_next, dn = tied(
        q_y[3], q_y[2], q, q_send, k, k_got, zero_low, sums, proj_part, dn_next, dn
    )
    dn_next = next_z(added(dn[2], dn_next))
    k_got = swap_core(k_got)
    q_next = next_z(added(q[3], q_y[3]))
    q_y[1] = swap_y(q_send[1])
    proj_far = swap_seq(proj_part)
    d_tokens = back_dot(zero_low, w_skip[:D]).reshape(1, count, D)
    sums = vector_step(sums, 1)
    q_next, q_y, k, k_got, sums, zero_low, d_tokens, proj_far, up_part, dn_next = tied(
        q_next, q_y, k, k_got, sums, zero_low, d_tokens, proj_far, up_part, dn_next
    )
    dn_next = next_z(added(dn[1], dn_next))
    q_next = onward(q[2], q_y[2], q_next)
    k_send = [added(k[1, i], k_got[1, i]) for i in range(4)]
    q_y[0] = swap_y(q_send[0])
    k_y = {3: swap_y(k_send[3])}
    k = added(k[0], k_got[0])
    up_far = swap_seq(up_part)
    out_proj = f32(proj_part) + f32(proj_far)
    d_skip = back_dot(zero_low, w_skip[D:]).reshape(1, count, D)
    sums = vector_step(sums, 0, "seq")
    q_next, q_y, k_y, k, k_send, sums, d_skip, up_far, dn_next = tied(
        q_next, q_y, k_y, k, k_send, sums, d_skip, up_far, dn_next
    )
    dn_part = added(dn[0], dn_next)
    dn_got = swap_seq(dn_part)
    q_next = onward(q[1], q_y[1], q_next)
    k_next = next_z(added(k[3], k_y[3]))
    k_y[2], k_y[1] = swap_y(k_send[2]), swap_y(k_send[1])
    out_up = f32(up_part) + f32(up_far)
    sums = vector_step(sums, 2)
    q_next, k_next, k_y, sums, dn_part, dn_got = tied(
        q_next, k_next, k_y, sums, dn_part, dn_got
    )
    out_down = by_side(side, dn_part, dn_got)
    q_sum = b16(f32(q[0]) + f32(q_y[0]) + f32(q_next))
    q_got = swap_seq(q_sum)
    k_next = onward(k[2], k_y[2], k_next)
    k_y[0] = swap_y(k_send[0])
    sums = vector_step(sums, 4)
    q_got, k_next, k_y, sums = tied(q_got, k_next, k_y, sums)
    out_qkv = f32(q_sum) + f32(q_got)
    k_next = onward(k[1], k_y[1], k_next)
    sums = vector_step(sums, 8)
    k_next, k_y, sums = tied(k_next, k_y, sums)
    k_sum = b16(f32(k[0]) + f32(k_y[0]) + f32(k_next))
    out_skip = f32(k_sum) + f32(swap_seq(k_sum))
    sums = sums.reshape(-1)
    starts = [0, D, 2 * D, 3 * D, 4 * D, 5 * D, 6 * D, 10 * D, 11 * D]
    sums = [sums[a:b] for a, b in zip(starts, starts[1:])]
    grads = (out_skip, out_qkv, out_proj, out_up, out_down)
    return (output, d_tokens, d_skip, *grads, *sums)


def solution(mesh):
    in_specs = (
        P("batch", "seq", None),
        P("seq", "batch", None, None),
        P("batch", None),
        P("batch", "seq", None),
        *(P("batch", None),) * 5,
        *(P(),) * 8,
    )
    out_specs = (*(P("batch", "seq", None),) * 3, *(P("batch", None),) * 5, *(P(),) * 8)
    pair = mesh.shape["batch"] == ROWS and mesh.shape["seq"] == 2
    return jax.shard_map(
        per_device_pair if pair else per_device,
        mesh=mesh,
        in_specs=in_specs,
        out_specs=out_specs,
        check_vma=False,

    )
```
